256 devices in a mesh: tm: 64 (over y, z, core), chan: 4 (over x).
Axes of the slice: x: 4, y: 4, z: 8, core: 2. Of those that a mesh axis runs over, the one named last changes fastest.
Arguments:
- reference_signal: float32 [2, 131072], P(None, 'tm'), may hold values from -12 to 12, as said below
- surveillance: float32 [2, 64, 131072], P(None, 'chan', 'tm'), may hold values from -30 to 30, as said below
- loading: float32 [1], replicated, may hold values from 0.0005 to 0.005
Outputs:
- range_doppler: float32 [256, 2, 64, 1024], P(('tm', 'chan'))
- clutter_weights: float32 [2, 256, 64], P(None, None, 'chan')
The draws below stay inside these ranges and needn't reach their ends.
Inputs may be any that keep to these rules, and one draw needn't show every extreme that they name: `reference_signal`: complex reference samples; row 0 holds the real parts, row 1 the imaginary parts. `surveillance`: complex surveillance samples; index 0 of the first dimension holds the real parts, index 1 the imaginary parts.
All inputs are finite; a program needn't handle non-finite values.
Results may differ from the reference program's by a relative error of at most 0.0003.
Values sent between devices are 32-bit elements; how exact they have to be, the bound alone decides.
A program may use at most 64 MiB of HBM per device.

```python
import math
import jax
import jax.numpy as jnp
from jax import lax

LAGS = 256
CHAN = 64
DOPP = 1024
SEG_LEN = 512
SAMPLES = 131072
SEGMENTS = 256


def radar_scene(key):
    base = jax.random.fold_in(key, 4099)
    keys = jax.random.split(base, 5)
    total = SAMPLES
    blocks = total // SEG_LEN
    white = jax.random.normal(keys[0], (2, total + 2), jnp.float32)
    levels = jnp.exp(jax.random.uniform(keys[1], (blocks,), jnp.float32, -0.5, 0.5))
    colored = white[:, 2:] + 0.7 * white[:, 1:-1] + 0.4 * white[:, :-2]
    position = jnp.arange(total, dtype=jnp.float32)
    ramp = jnp.sqrt(1.0 + 2.0 * position / total)
    envelope = ramp * jnp.repeat(levels, SEG_LEN, total_repeat_length=total)
    signal = jnp.clip(colored * envelope, -12.0, 12.0)
    delays = jax.random.randint(keys[2], (16,), 0, LAGS)
    coefficients = jax.random.normal(keys[3], (2, CHAN, 16), jnp.float32) * 0.5
    padded = jnp.concatenate([jnp.zeros((2, LAGS), jnp.float32), signal], axis=1)
    source_index = jnp.arange(total, dtype=jnp.int32)[None, :] + LAGS - delays[:, None]
    moved = padded[:, source_index]
    real = jnp.einsum('ct,tn->cn', coefficients[0], moved[0]) - jnp.einsum('ct,tn->cn', coefficients[1], moved[1])
    imag = jnp.einsum('ct,tn->cn', coefficients[0], moved[1]) + jnp.einsum('ct,tn->cn', coefficients[1], moved[0])
    noise = jax.random.normal(keys[4], (2, CHAN, total), jnp.float32) * (0.7 * ramp)
    echoes = jnp.clip(jnp.stack([real, imag]) + noise, -30.0, 30.0)
    return (signal, echoes)


def draw_reference_signal(key, part):
    return radar_scene(key)[0]


def draw_surveillance(key, part):
    return radar_scene(key)[1]


def setup_inputs(seed: int = 0) -> dict:
    seeds = jax.random.split(jax.random.key(seed), 4)
    reference_signal = draw_reference_signal(jax.random.fold_in(seeds[3], 71), 0)
    surveillance = draw_surveillance(jax.random.fold_in(seeds[3], 71), 0)
    loading = jnp.clip(jnp.exp(jax.random.uniform(seeds[2], (1,), jnp.float32, math.log(0.0005), math.log(0.005))), 0.0005, 0.005)
    return {"reference_signal": reference_signal, "surveillance": surveillance, "loading": loading}


highest = lax.Precision.HIGHEST
epsilon = 1e-06

def band(series, rows, cols):
    period = series.shape[-1]
    tiled = jnp.tile(series, (1, rows))[:, :rows * (period - 1)]
    return tiled.reshape(series.shape[0], rows, period - 1)[:, :, :cols]

def delay_block(window, lags):
    rows = window.shape[1] - lags
    series = jnp.concatenate([window[:, lags::-1], window[:, :lags:-1]], axis=1)
    mats = band(series, rows, lags)
    return jnp.concatenate([mats[0], mats[1]], axis=1)

def self_product(block):
    return lax.dot_general(block.astype(jnp.float32), block.astype(jnp.float32), (((0,), (0,)), ((), ())), precision=highest, preferred_element_type=jnp.float32)

def hermitian_parts(full, lags):
    real = full[:lags, :lags] + full[lags:, lags:]
    imag = full[:lags, lags:] - full[lags:, :lags]
    return (real, imag)

def paired(product, width, lags):
    real = product[:width, :lags] + product[width:, lags:]
    imag = product[width:, :lags] - product[:width, lags:]
    return jnp.stack([real, imag])

def first_column_matrix(column):
    lags = column.shape[1]
    blank = jnp.zeros((1,), jnp.float32)
    real = jnp.concatenate([column[0], blank, column[0, 1:][::-1]])
    imag = jnp.concatenate([-column[1], blank, column[1, 1:][::-1]])
    mats = band(jnp.stack([real, imag]), lags, lags)
    return (mats[0], mats[1])

def edge_matrix(history):
    lags = history.shape[1]
    series = jnp.concatenate([jnp.zeros((2, 1), jnp.float32), history[:, :lags - 1], jnp.zeros((2, lags), jnp.float32)], axis=1)
    mats = band(series, lags, lags)
    block = jnp.concatenate([mats[0], mats[1]], axis=1)
    return hermitian_parts(self_product(block), lags)

def solve_weights(normal_real, normal_imag, cross, loading):
    lags = normal_real.shape[0]
    damping = loading[0] * jnp.trace(normal_real) / lags
    diagonal = jnp.eye(lags, dtype=jnp.float32) * damping
    system = jnp.concatenate([jnp.concatenate([normal_real + diagonal, -normal_imag], axis=1), jnp.concatenate([normal_imag, normal_real + diagonal], axis=1)], axis=0)
    factor = jnp.linalg.cholesky(system)
    right = jnp.concatenate([cross[0].T, cross[1].T], axis=0)
    middle = lax.linalg.triangular_solve(factor, right, left_side=True, lower=True)
    solved = lax.linalg.triangular_solve(factor, middle, left_side=True, lower=True, transpose_a=True)
    return (solved.reshape(2, lags, cross.shape[1]), damping)

def mixing_matrix(weights):
    real_t = weights[0].T
    imag_t = weights[1].T
    return jnp.concatenate([jnp.concatenate([real_t, -imag_t], axis=1), jnp.concatenate([imag_t, real_t], axis=1)], axis=0)

def reference(reference_signal, surveillance, loading):
    lags = LAGS
    total = SAMPLES
    padded = jnp.concatenate([jnp.zeros((2, lags), jnp.float32), reference_signal], axis=1)
    signal = surveillance.reshape(2 * CHAN, total)

    def lag_term(lag):
        moved = lax.dynamic_slice_in_dim(padded, lags - lag, total, 1)
        real = jnp.sum(moved[0] * reference_signal[0] + moved[1] * reference_signal[1])
        imag = jnp.sum(moved[0] * reference_signal[1] - moved[1] * reference_signal[0])
        return jnp.stack([real, imag])
    column = lax.map(lag_term, jnp.arange(lags, dtype=jnp.int32)).T
    base_real, base_imag = first_column_matrix(column)
    edge_real, edge_imag = edge_matrix(reference_signal[:, total - lags:][:, ::-1])
    normal_real = base_real - edge_real
    normal_imag = base_imag - edge_imag

    def cross_step(running, index):
        start = index * SEG_LEN
        block = delay_block(lax.dynamic_slice_in_dim(padded, start, SEG_LEN + lags, 1), lags)
        rows = lax.dynamic_slice_in_dim(signal, start, SEG_LEN, 1)
        return (running + jnp.dot(rows.astype(jnp.float32), block.astype(jnp.float32), precision=highest, preferred_element_type=jnp.float32), None)
    cross_total = lax.scan(cross_step, jnp.zeros((2 * CHAN, 2 * lags), jnp.float32), jnp.arange(SEGMENTS, dtype=jnp.int32))[0]
    cross_terms = paired(cross_total, CHAN, lags)
    weights, damping = solve_weights(normal_real, normal_imag, cross_terms, loading)
    mixing = mixing_matrix(weights)

    def corr_step(index):
        start = index * SEG_LEN
        block = delay_block(lax.dynamic_slice_in_dim(padded, start, SEG_LEN + lags, 1), lags)
        rows = lax.dynamic_slice_in_dim(signal, start, SEG_LEN, 1)
        clutter = lax.dot_general(mixing.astype(jnp.float32), block.astype(jnp.float32), (((1,), (1,)), ((), ())), precision=highest, preferred_element_type=jnp.float32)
        residual = rows - clutter
        product = jnp.dot(residual.astype(jnp.float32), block.astype(jnp.float32), precision=highest, preferred_element_type=jnp.float32)
        return (paired(product, CHAN, lags), lax.optimization_barrier(jnp.sum(residual * residual, axis=1)))
    corrs, squares = lax.map(corr_step, jnp.arange(SEGMENTS, dtype=jnp.int32))
    energy = lax.optimization_barrier(jnp.sum(squares, axis=0))
    power = energy[:CHAN] + energy[CHAN:]
    scale = lax.rsqrt(total * (power / total + epsilon))
    scaled = corrs * scale[None, None, :, None]
    folds = -(-SEGMENTS // DOPP)
    extra = folds * DOPP - SEGMENTS
    widened = jnp.concatenate([scaled, jnp.zeros((extra, 2, CHAN, lags), jnp.float32)], axis=0)
    folded = lax.optimization_barrier(jnp.sum(widened.reshape(folds, DOPP, 2, CHAN, lags), axis=0))
    spectrum = jnp.fft.fft(folded[:, 0] + 1j * folded[:, 1], axis=0)
    result = jnp.stack([jnp.real(spectrum), jnp.imag(spectrum)], axis=1)
    return (jnp.transpose(result, (3, 1, 2, 0)), weights)
```

```python
import functools

import jax
import jax.numpy as jnp
import numpy as np
from jax import lax
from jax.experimental import pallas as pl
from jax.experimental.pallas import tpu as pltpu
from jax.sharding import Mesh
from jax.sharding import PartitionSpec as P

LAGS = 256
DOPP = 1024
SEG_LEN = 512
TM = ("tm_0", "tm_1", "tm_2")
TM_CHAN = ("tm_0", "tm_1", "tm_2", "chan")
EPSILON = 1e-06
PANEL = 32
PIVOTS = 4
ROWS = 40

highest = lax.Precision.HIGHEST
NN = (((1,), (0,)), ((), ()))
NT = (((1,), (1,)), ((), ()))


def dot(a, b, dims=NN):
    return lax.dot_general(a, b, dims, precision=highest, preferred_element_type=jnp.float32)


def halves(x):
    high = x.astype(jnp.bfloat16)
    return high, (x - high.astype(jnp.float32)).astype(jnp.bfloat16)


def dot3(a, b, dims=NN):
    def one(x, y):
        return lax.dot_general(x, y, dims, preferred_element_type=jnp.float32)

    return one(a[0], b[0]) + (one(a[0], b[1]) + one(a[1], b[0]))


def toeplitz(row, rows):
    wide = jnp.broadcast_to(row, (rows, row.shape[1]))
    return pltpu.roll(wide, 0, 1, stride=1, stride_axis=0)


def delays(window):
    tiles = window.shape[1] // 128
    parts = [jnp.zeros((128, 128), jnp.float32)]
    for t in range(1, tiles):
        parts.append(toeplitz(window[:, 128 * t - 128 : 128 * t + 128], 128)[:, 128:])
    return jnp.concatenate(parts, axis=1)


def first_kernel(last_index, position, prior, reference, surveillance, sums, table):
    length = reference.shape[1]
    width = surveillance.shape[1]
    window = jnp.concatenate([prior[...], reference[...]], axis=1)
    taps = []
    for part in range(2):
        taps.append(halves(delays(window[part : part + 1])))
        for piece in range(2):
            table[part, piece] = taps[part][piece]
    s_re, s_im = surveillance[0], surveillance[1]
    r_re, r_im = reference[0:1], reference[1:2]
    blank = jnp.zeros((6, length), jnp.float32)
    with_re = halves(jnp.concatenate([s_re, s_im, r_re, r_im, blank], axis=0))
    with_im = halves(jnp.concatenate([s_im, -s_re, r_im, -r_re, blank], axis=0))
    for half in range(2):
        cut = slice(256 - 128 * half, 256 - 128 * half + length)
        product = dot3([t[:, cut] for t in taps[0]], with_re, NT)
        product = product + dot3([t[:, cut] for t in taps[1]], with_im, NT)
        wide = jnp.concatenate([product, jnp.zeros((128, 128 - ROWS), jnp.float32)], axis=1)
        sums[:, 128 * half : 128 * half + 128] = wide.T[:ROWS]
    owner = jnp.where(position[0] == last_index, 1.0, 0.0)
    sums[34:36, :] = reference[:, length - LAGS :] * owner


def first_pass(prior, reference, surveillance, position, last_index):
    vmem = pl.BlockSpec(memory_space=pltpu.VMEM)
    length = reference.shape[1]
    return pl.pallas_call(
        functools.partial(first_kernel, last_index),
        out_shape=[
            jax.ShapeDtypeStruct((ROWS, LAGS), jnp.float32),
            jax.ShapeDtypeStruct((2, 2, 128, LAGS + length), jnp.bfloat16),
        ],
        in_specs=[pl.BlockSpec(memory_space=pltpu.SMEM), vmem, vmem, vmem],
        out_specs=[vmem, vmem],
        name="first_pass",
    )(position, prior, reference, surveillance)


def times(a, b):
    if a[1] is None and b[1] is None:
        return (a[0] * b[0], None)
    if a[1] is None:
        return (a[0] * b[0], a[0] * b[1])
    if b[1] is None:
        return (a[0] * b[0], a[1] * b[0])
    return (a[0] * b[0] - a[1] * b[1], a[0] * b[1] + a[1] * b[0])


def plus(a, b):
    if a[1] is None:
        return (a[0] + b[0], b[1])
    if b[1] is None:
        return (a[0] + b[0], a[1])
    return (a[0] + b[0], a[1] + b[1])


def minus(a, b):
    return (a[0] - b[0], None if b[1] is None else a[1] - b[1])


def negative(a):
    return (-a[0], None if a[1] is None else -a[1])


def conjugate(a):
    return (a[0], None if a[1] is None else -a[1])


def product(left, right):
    out = []
    for row in left:
        line = []
        for j in range(len(right[0])):
            total = times(row[0], right[0][j])
            for k in range(1, len(row)):
                total = plus(total, times(row[k], right[k][j]))
            line.append(total)
        out.append(line)
    return out


def adjoint(block):
    return [[conjugate(block[j][i]) for j in range(len(block))] for i in range(len(block[0]))]


def hermitian_inverse(block):
    size = len(block)
    if size == 1:
        return [[(1.0 / block[0][0][0], None)]]
    if size == 2:
        a, c, d = block[0][0][0], block[0][1], block[1][1][0]
        scale = 1.0 / (a * d - (c[0] * c[0] + c[1] * c[1]))
        off = (-c[0] * scale, -c[1] * scale)
        return [[(d * scale, None), off], [conjugate(off), (a * scale, None)]]
    half = size // 2
    head = [row[:half] for row in block[:half]]
    side = [row[half:] for row in block[:half]]
    tail = [row[half:] for row in block[half:]]
    head_inverse = hermitian_inverse(head)
    lifted = product(head_inverse, side)
    drop = product(adjoint(side), lifted)
    rest = [[minus(tail[i][j], drop[i][j]) for j in range(half)] for i in range(half)]
    rest_inverse = hermitian_inverse(rest)
    corner = product(lifted, rest_inverse)
    extra = product(corner, adjoint(lifted))
    first = [[plus(head_inverse[i][j], extra[i][j]) for j in range(half)] for i in range(half)]
    right = [[negative(corner[i][j]) for j in range(half)] for i in range(half)]
    below = adjoint(right)
    return [first[i] + right[i] for i in range(half)] + [below[i] + rest_inverse[i] for i in range(half)]


def eliminate(real, imag):
    height, n = real.shape
    m = PIVOTS
    lane = lax.broadcasted_iota(jnp.int32, (1, n), 1)
    lanes = lax.broadcasted_iota(jnp.int32, (height, 128), 1)
    rows = lax.broadcasted_iota(jnp.int32, (height, 128), 0)

    def wide(value):
        return None if value is None else jnp.concatenate([value] * (n // 128), axis=1)

    for k in range(0, height, m):
        col_r = [jnp.broadcast_to(real[:, k + j : k + j + 1], (height, 128)) for j in range(m)]
        col_i = [jnp.broadcast_to(imag[:, k + j : k + j + 1], (height, 128)) for j in range(m)]
        block = [
            [(col_r[j][k + i : k + i + 1], col_i[j][k + i : k + i + 1]) for j in range(m)]
            for i in range(m)
        ]
        inverse = [[(wide(q[0]), wide(q[1])) for q in row] for row in hermitian_inverse(block)]
        hit = (lane >= k) & (lane < k + m)
        old = [
            (
                jnp.where(hit, jnp.where(lane == k + i, 1.0, 0.0), real[k + i : k + i + 1]),
                jnp.where(hit, 0.0, imag[k + i : k + i + 1]),
            )
            for i in range(m)
        ]
        new = product(inverse, [[value] for value in old])
        new = [line[0] for line in new]
        inside = (rows >= k) & (rows < k + m)
        col_r = [jnp.where(inside, jnp.where(rows == k + j, -1.0, 0.0), col_r[j]) for j in range(m)]
        col_i = [jnp.where(inside, 0.0, col_i[j]) for j in range(m)]
        gone = inside | ((lanes >= k) & (lanes < k + m))
        out_r, out_i = [], []
        for t in range(n // 128):
            cut = slice(128 * t, 128 * t + 128)
            mask = gone if t == 0 else inside
            next_r = jnp.where(mask, 0.0, real[:, cut])
            next_i = jnp.where(mask, 0.0, imag[:, cut])
            for j in range(m):
                row_r, row_i = new[j][0][:, cut], new[j][1][:, cut]
                next_r = next_r - (col_r[j] * row_r - col_i[j] * row_i)
                next_i = next_i - (col_r[j] * row_i + col_i[j] * row_r)
            out_r.append(next_r)
            out_i.append(next_i)
        real = jnp.concatenate(out_r, axis=1)
        imag = jnp.concatenate(out_i, axis=1)
    return real, imag


def invert(real, imag):
    b = PANEL

    def panel(index, carry):
        start = pl.multiple_of(index * b, b)
        held = pl.ds(start, b)
        top_r, top_i = eliminate(real[held, :], imag[held, :])
        all_r, all_i = real[...], imag[...]
        lane = lax.broadcasted_iota(jnp.int32, (LAGS, 128), 1)
        row = lax.broadcasted_iota(jnp.int32, (LAGS, 128), 0)
        factor = jnp.where(lane < b, all_r[:, :128], pltpu.roll(all_i[:, :128], b, 1))
        inside = (row >= start) & (row < start + b)
        factor = jnp.where(inside | (lane >= 2 * b), 0.0, factor)
        right = jnp.concatenate(
            [
                jnp.concatenate([top_r, top_i], axis=1),
                jnp.concatenate([-top_i, top_r], axis=1),
                jnp.zeros((128 - 2 * b, 2 * LAGS), jnp.float32),
            ],
            axis=0,
        )
        update = dot(factor, right)
        column = lax.broadcasted_iota(jnp.int32, (LAGS, LAGS), 1)
        all_r = jnp.where(column < b, 0.0, all_r) - update[:, :LAGS]
        all_i = jnp.where(column < b, 0.0, all_i) - update[:, LAGS:]
        real[...] = pltpu.roll(all_r, LAGS - b, 1)
        imag[...] = pltpu.roll(all_i, LAGS - b, 1)
        real[held, :] = pltpu.roll(top_r, LAGS - b, 1)
        imag[held, :] = pltpu.roll(top_i, LAGS - b, 1)
        return carry

    lax.fori_loop(0, LAGS // b, panel, 0)


def normal_matrix(column, loading):
    i0 = lax.broadcasted_iota(jnp.int32, (LAGS, LAGS), 0)
    i1 = lax.broadcasted_iota(jnp.int32, (LAGS, LAGS), 1)
    flip = jnp.where(i0 + i1 == LAGS - 1, 1.0, 0.0)
    behind = pltpu.roll(dot(column, flip), 1, 1)
    lane = lax.broadcasted_iota(jnp.int32, behind.shape, 1)
    behind = jnp.where(lane == 0, 0.0, behind)
    base_r = toeplitz(jnp.concatenate([column[0:1], behind[0:1]], axis=1), LAGS)[:, :LAGS]
    base_i = toeplitz(jnp.concatenate([-column[1:2], behind[1:2]], axis=1), LAGS)[:, :LAGS]
    blank = jnp.zeros((1, LAGS), jnp.float32)
    edge_r = toeplitz(jnp.concatenate([blank, column[2:3]], axis=1), LAGS)[:, :LAGS]
    edge_i = toeplitz(jnp.concatenate([blank, column[3:4]], axis=1), LAGS)[:, :LAGS]
    one = jnp.concatenate([edge_r, edge_i], axis=1)
    two = jnp.concatenate([edge_i, -edge_r], axis=1)
    real = base_r - dot(one, one, NT)
    imag = base_i - dot(one, two, NT)
    diagonal = i0 == i1
    lam = loading * (jnp.sum(jnp.where(diagonal, real, 0.0)) / LAGS)
    return jnp.where(diagonal, real + lam, real), imag


def solve_kernel(loading, sums, weights, real, imag):
    start_r, start_i = normal_matrix(sums[32:40, :], loading[0])
    real[...] = start_r
    imag[...] = start_i
    invert(real, imag)
    half = (ROWS - 8) // 2
    c_re, c_im = sums[:half, :], sums[half : 2 * half, :]
    weights[...] = dot(sums[: 2 * half, :], real[...], NT) + dot(
        jnp.concatenate([-c_im, c_re], axis=0), imag[...], NT
    )


def solve(sums, loading):
    vmem = pl.BlockSpec(memory_space=pltpu.VMEM)
    return pl.pallas_call(
        solve_kernel,
        out_shape=jax.ShapeDtypeStruct((ROWS - 8, LAGS), jnp.float32),
        in_specs=[pl.BlockSpec(memory_space=pltpu.SMEM), vmem],
        out_specs=vmem,
        scratch_shapes=[pltpu.VMEM((LAGS, LAGS), jnp.float32)] * 2,
        name="solve",
    )(loading, sums)


def second_kernel(weights, table, surveillance, corr, energy):
    length = surveillance.shape[2]
    width = surveillance.shape[1]
    w = weights[...]
    w_re, w_im = w[:width], w[width:]
    on_re = halves(w)
    on_im = halves(jnp.concatenate([-w_im, w_re], axis=0))
    clutter = jnp.zeros((2 * width, length), jnp.float32)
    taps = []
    for half in range(2):
        cut = slice(256 - 128 * half, 256 - 128 * half + length)
        lags = slice(128 * half, 128 * half + 128)
        taps.append([[table[part, piece, :, cut] for piece in range(2)] for part in range(2)])
        clutter = clutter + dot3([x[:, lags] for x in on_re], taps[half][0])
        clutter = clutter + dot3([x[:, lags] for x in on_im], taps[half][1])
    residual = jnp.concatenate([surveillance[0], surveillance[1]], axis=0) - clutter
    energy[...] = jnp.broadcast_to(
        jnp.sum(residual * residual, axis=1, keepdims=True), (2 * width, 128)
    )
    turned = jnp.concatenate([residual[width:], -residual[:width]], axis=0)
    segments = length // SEG_LEN
    row = lax.broadcasted_iota(jnp.int32, (2 * width * segments, length), 0)
    col = lax.broadcasted_iota(jnp.int32, (2 * width * segments, length), 1)
    own = row // (2 * width) == col // SEG_LEN
    with_re = halves(jnp.where(own, jnp.concatenate([residual] * segments, axis=0), 0.0))
    with_im = halves(jnp.where(own, jnp.concatenate([turned] * segments, axis=0), 0.0))
    for half in range(2):
        lags = slice(128 * half, 128 * half + 128)
        corr[lags, :] = dot3(taps[half][0], with_re, NT) + dot3(taps[half][1], with_im, NT)


def second_pass(weights, table, surveillance):
    vmem = pl.BlockSpec(memory_space=pltpu.VMEM)
    width, length = surveillance.shape[1:]
    return pl.pallas_call(
        second_kernel,
        out_shape=[
            jax.ShapeDtypeStruct((LAGS, 2 * width * (length // SEG_LEN)), jnp.float32),
            jax.ShapeDtypeStruct((2 * width, 128), jnp.float32),
        ],
        in_specs=[vmem] * 3,
        out_specs=[vmem] * 2,
        name="second_pass",
    )(weights, table, surveillance)


def doppler_tables(shards, segments):
    short = DOPP // segments
    angle = 2.0 * np.pi / short * (np.outer(np.arange(shards), np.arange(short)) % short)
    table = np.concatenate([np.cos(angle), np.sin(angle)], axis=1)
    turn = 2.0 * np.pi / DOPP * np.outer(np.arange(segments), np.arange(DOPP))
    turns = np.stack([np.cos(turn), np.sin(turn)])
    return table.astype(np.float32), turns.astype(np.float32)


def doppler_kernel(cells, scale, table, turns, out):
    shards, groups, lanes = cells.shape
    segments = turns.shape[1]
    width = lanes // segments // 2
    basis = halves(table[...])
    short = DOPP // segments
    for g in range(groups):
        block = halves(cells[:, g, :].T)
        wave = dot3(block, basis)
        total_r = total_i = None
        for s in range(segments):
            base = 2 * width * s
            a_r, a_i = wave[base : base + width, :short], wave[base : base + width, short:]
            b_r, b_i = (
                wave[base + width : base + 2 * width, :short],
                wave[base + width : base + 2 * width, short:],
            )
            y_r = a_r + b_i
            y_i = b_r - a_i
            y_r = jnp.concatenate([y_r] * segments, axis=1)
            y_i = jnp.concatenate([y_i] * segments, axis=1)
            if s == 0:
                total_r, total_i = y_r, y_i
                continue
            c, d = turns[0, s : s + 1, :], turns[1, s : s + 1, :]
            total_r = total_r + (y_r * c + y_i * d)
            total_i = total_i + (y_i * c - y_r * d)
        at = slice(width * g, width * g + width)
        by = scale[at, 0:1]
        out[0, 0, at, :] = total_r * by
        out[0, 1, at, :] = total_i * by


def doppler(cells, scale, segments):
    vmem = pl.BlockSpec(memory_space=pltpu.VMEM)
    table, turns = doppler_tables(cells.shape[0], segments)
    width = cells.shape[2] // segments // 2
    return pl.pallas_call(
        doppler_kernel,
        out_shape=jax.ShapeDtypeStruct((1, 2, width * cells.shape[1], DOPP), jnp.float32),
        in_specs=[vmem] * 4,
        out_specs=vmem,
        name="doppler",
    )(cells, scale, jnp.asarray(table), jnp.asarray(turns))


def per_device(reference_signal, surveillance, loading):
    shards = lax.axis_size(TM)
    length = reference_signal.shape[1]
    width = surveillance.shape[1]
    total = length * shards
    segments = length // SEG_LEN
    here = lax.axis_index(TM)
    pairs = [(i, i + 1) for i in range(shards - 1)]
    prior = lax.ppermute(reference_signal[:, length - LAGS :], TM, pairs)
    local, table = first_pass(prior, reference_signal, surveillance, here[None], shards - 1)
    sums = lax.psum(local, TM)
    weights = solve(sums, loading)
    corr, energy = second_pass(weights, table, surveillance)
    power = lax.psum(energy[:width, 0] + energy[width:, 0], TM)
    scale = lax.rsqrt(total * (power / total + EPSILON))
    scale = lax.all_gather(scale, "chan", tiled=True)
    cells = lax.all_to_all(corr[:, None, :], TM_CHAN, split_axis=0, concat_axis=0, tiled=True)
    cells = cells.reshape(shards, LAGS // shards, corr.shape[1])
    full = doppler(cells, jnp.broadcast_to(scale[:, None], (scale.shape[0], 128)), segments)
    return full, jnp.swapaxes(weights.reshape(2, width, LAGS), 1, 2)


def solution(mesh):
    split = Mesh(
        mesh.devices.reshape(4, 8, 2, mesh.shape["chan"]), ("tm_0", "tm_1", "tm_2", "chan")
    )
    in_specs = (P(None, TM), P(None, "chan", TM), P())
    out_specs = (P(TM_CHAN, None, None, None), P(None, None, "chan"))
    return jax.shard_map(
        per_device, mesh=split, in_specs=in_specs, out_specs=out_specs, check_vma=False
    )
```

```python
import functools

import jax
import jax.numpy as jnp
import numpy as np
from jax import lax
from jax.experimental import pallas as pl
from jax.experimental.pallas import tpu as pltpu
from jax.sharding import Mesh
from jax.sharding import PartitionSpec as P

LAGS = 256
DOPP = 1024
SEG_LEN = 512
TM = ("tm_0", "tm_1", "tm_2")
TM_CHAN = ("tm_0", "tm_1", "tm_2", "chan")
EPSILON = 1e-06
PANEL = 32
PIVOTS = 4
ROWS = 40
MESH = pl.DeviceIdType.MESH

highest = lax.Precision.HIGHEST
NN = (((1,), (0,)), ((), ()))
NT = (((1,), (1,)), ((), ()))


def dot(a, b, dims=NN):
    return lax.dot_general(a, b, dims, precision=highest, preferred_element_type=jnp.float32)


def halves(x):
    high = x.astype(jnp.bfloat16)
    return high, (x - high.astype(jnp.float32)).astype(jnp.bfloat16)


def dot3(a, b, dims=NN):
    def one(x, y):
        return lax.dot_general(x, y, dims, preferred_element_type=jnp.float32)

    return one(a[0], b[0]) + (one(a[0], b[1]) + one(a[1], b[0]))


def toeplitz(row, rows):
    wide = jnp.broadcast_to(row, (rows, row.shape[1]))
    return pltpu.roll(wide, 0, 1, stride=1, stride_axis=0)


def exchange(axes, src, dst, send, recv):
    sizes = [lax.axis_size(a) for a in axes]
    count = int(np.prod(sizes))
    here = place(axes)
    copies = []
    for d in range(1, count):
        there = lax.rem(here + d, count)
        copies.append(
            pltpu.make_async_remote_copy(
                src_ref=src(there),
                dst_ref=dst(here),
                send_sem=send.at[d - 1],
                recv_sem=recv.at[d - 1],
                device_id=device(axes, there),
                device_id_type=MESH,
            )
        )
        copies[-1].start()
    return copies


def place(axes):
    index = lax.axis_index(axes[0])
    for a in axes[1:]:
        index = index * lax.axis_size(a) + lax.axis_index(a)
    return index


def device(axes, index):
    coordinates = {}
    for a in reversed(axes):
        coordinates[a] = lax.rem(index, lax.axis_size(a))
        index = lax.div(index, lax.axis_size(a))
    return coordinates


def greet(groups):
    barrier = pltpu.get_barrier_semaphore()
    total = 0
    for axes, offsets in groups:
        count = int(np.prod([lax.axis_size(a) for a in axes]))
        here = place(axes)
        for d in offsets:
            pl.semaphore_signal(
                barrier, inc=1, device_id=device(axes, lax.rem(here + d, count)), device_id_type=MESH
            )
            total += 1
    return barrier, total


def finish(copies):
    for copy in copies:
        copy.wait()


def first_kernel(
    reference, surveillance, sums, table,
    halo, mine, pair, ring_y, ring_z, edge_sem, core_send, core_recv, y_send, y_recv, z_send, z_recv, out_send, out_recv,
):
    length = reference.shape[1]
    count = lax.axis_size(TM)
    here = place(TM)
    core, y, z = lax.axis_index(TM[2]), lax.axis_index(TM[0]), lax.axis_index(TM[1])
    barrier, total = greet(
        [(TM, (1, count - 1)), (TM[2:], (1,)), (TM[:1], (1, 2, 3)), (TM[1:2], tuple(range(1, 8)))]
    )
    pl.semaphore_wait(barrier, total)
    forward = pltpu.make_async_remote_copy(
        src_ref=reference.at[:, pl.ds(length - LAGS, LAGS)],
        dst_ref=halo,
        send_sem=edge_sem.at[0],
        recv_sem=edge_sem.at[1],
        device_id=device(TM, lax.rem(here + 1, count)),
        device_id_type=MESH,
    )
    forward.start()

    def fill(tile, part, window):
        high, low = halves(toeplitz(window, 128)[:, 128:])
        cut = slice(128 * tile, 128 * tile + 128)
        table[part, 0, :, cut] = high
        table[part, 1, :, cut] = low

    for part in range(2):
        for tile in range(3, (LAGS + length) // 128):
            fill(tile, part, reference[part : part + 1, 128 * tile - 384 : 128 * tile - 128])
    s_re, s_im = surveillance[0], surveillance[1]
    r_re, r_im = reference[0:1], reference[1:2]
    blank = jnp.zeros((6, length), jnp.float32)
    with_re = halves(jnp.concatenate([s_re, s_im, r_re, r_im, blank], axis=0))
    with_im = halves(jnp.concatenate([s_im, -s_re, r_im, -r_re, blank], axis=0))
    forward.wait()
    before = jnp.where(here > 0, halo[...], 0.0)
    for part in range(2):
        fill(1, part, before[part : part + 1])
        fill(2, part, jnp.concatenate([before[part : part + 1, 128:], reference[part : part + 1, :128]], axis=1))
    owner = jnp.where(here == count - 1, 1.0, 0.0)
    for half in range(2):
        cut = slice(256 - 128 * half, 256 - 128 * half + length)
        taps = [[table[part, piece, :, cut] for piece in range(2)] for part in range(2)]
        product = dot3(taps[0], with_re, NT) + dot3(taps[1], with_im, NT)
        wide = jnp.concatenate([product, jnp.zeros((128, 128 - ROWS), jnp.float32)], axis=1)
        mine[half] = wide.T[:ROWS]
        at = length - LAGS + 128 * half
        mine[half, 34:36, :] = reference[:, at : at + 128] * owner

    finish(exchange(TM[2:], lambda p: mine.at[p], lambda p: pair, core_send, core_recv))
    ring_y[y] = mine[core] + pair[...]
    finish(exchange(TM[:1], lambda p: ring_y.at[y], lambda p: ring_y.at[p], y_send, y_recv))
    ring_z[z] = (ring_y[0] + ring_y[1]) + (ring_y[2] + ring_y[3])
    finish(exchange(TM[1:2], lambda p: ring_z.at[z], lambda p: ring_z.at[p], z_send, z_recv))
    sums[core] = ((ring_z[0] + ring_z[1]) + (ring_z[2] + ring_z[3])) + (
        (ring_z[4] + ring_z[5]) + (ring_z[6] + ring_z[7])
    )
    finish(exchange(TM[2:], lambda p: sums.at[core], lambda p: sums.at[p], out_send, out_recv))


def first_pass(reference, surveillance):
    vmem = pl.BlockSpec(memory_space=pltpu.VMEM)
    length = reference.shape[1]
    part = (ROWS, 128)
    dma = pltpu.SemaphoreType.DMA
    return pl.pallas_call(
        first_kernel,
        out_shape=[
            jax.ShapeDtypeStruct((2,) + part, jnp.float32),
            jax.ShapeDtypeStruct((2, 2, 128, LAGS + length), jnp.bfloat16),
        ],
        in_specs=[vmem, vmem],
        out_specs=[vmem, vmem],
        scratch_shapes=[
            pltpu.VMEM((2, LAGS), jnp.float32),
            pltpu.VMEM((2,) + part, jnp.float32),
            pltpu.VMEM(part, jnp.float32),
            pltpu.VMEM((4,) + part, jnp.float32),
            pltpu.VMEM((8,) + part, jnp.float32),
            dma((2,)),
            dma((1,)), dma((1,)), dma((3,)), dma((3,)), dma((7,)), dma((7,)), dma((1,)), dma((1,)),
        ],
        compiler_params=pltpu.CompilerParams(collective_id=0, has_side_effects=True),
        name="first_pass",
    )(reference, surveillance)


def times(a, b):
    if a[1] is None and b[1] is None:
        return (a[0] * b[0], None)
    if a[1] is None:
        return (a[0] * b[0], a[0] * b[1])
    if b[1] is None:
        return (a[0] * b[0], a[1] * b[0])
    return (a[0] * b[0] - a[1] * b[1], a[0] * b[1] + a[1] * b[0])


def plus(a, b):
    if a[1] is None:
        return (a[0] + b[0], b[1])
    if b[1] is None:
        return (a[0] + b[0], a[1])
    return (a[0] + b[0], a[1] + b[1])


def minus(a, b):
    return (a[0] - b[0], None if b[1] is None else a[1] - b[1])


def negative(a):
    return (-a[0], None if a[1] is None else -a[1])


def conjugate(a):
    return (a[0], None if a[1] is None else -a[1])


def product(left, right):
    out = []
    for row in left:
        line = []
        for j in range(len(right[0])):
            total = times(row[0], right[0][j])
            for k in range(1, len(row)):
                total = plus(total, times(row[k], right[k][j]))
            line.append(total)
        out.append(line)
    return out


def adjoint(block):
    return [[conjugate(block[j][i]) for j in range(len(block))] for i in range(len(block[0]))]


def hermitian_inverse(block):
    size = len(block)
    if size == 1:
        return [[(1.0 / block[0][0][0], None)]]
    if size == 2:
        a, c, d = block[0][0][0], block[0][1], block[1][1][0]
        scale = 1.0 / (a * d - (c[0] * c[0] + c[1] * c[1]))
        off = (-c[0] * scale, -c[1] * scale)
        return [[(d * scale, None), off], [conjugate(off), (a * scale, None)]]
    half = size // 2
    head = [row[:half] for row in block[:half]]
    side = [row[half:] for row in block[:half]]
    tail = [row[half:] for row in block[half:]]
    head_inverse = hermitian_inverse(head)
    lifted = product(head_inverse, side)
    drop = product(adjoint(side), lifted)
    rest = [[minus(tail[i][j], drop[i][j]) for j in range(half)] for i in range(half)]
    rest_inverse = hermitian_inverse(rest)
    corner = product(lifted, rest_inverse)
    extra = product(corner, adjoint(lifted))
    first = [[plus(head_inverse[i][j], extra[i][j]) for j in range(half)] for i in range(half)]
    right = [[negative(corner[i][j]) for j in range(half)] for i in range(half)]
    below = adjoint(right)
    return [first[i] + right[i] for i in range(half)] + [below[i] + rest_inverse[i] for i in range(half)]


def eliminate(real, imag):
    height, n = real.shape
    m = PIVOTS
    lane = lax.broadcasted_iota(jnp.int32, (1, n), 1)
    lanes = lax.broadcasted_iota(jnp.int32, (height, 128), 1)
    rows = lax.broadcasted_iota(jnp.int32, (height, 128), 0)

    def wide(value):
        return None if value is None else jnp.concatenate([value] * (n // 128), axis=1)

    for k in range(0, height, m):
        col_r = [jnp.broadcast_to(real[:, k + j : k + j + 1], (height, 128)) for j in range(m)]
        col_i = [jnp.broadcast_to(imag[:, k + j : k + j + 1], (height, 128)) for j in range(m)]
        block = [
            [(col_r[j][k + i : k + i + 1], col_i[j][k + i : k + i + 1]) for j in range(m)]
            for i in range(m)
        ]
        inverse = [[(wide(q[0]), wide(q[1])) for q in row] for row in hermitian_inverse(block)]
        hit = (lane >= k) & (lane < k + m)
        old = [
            (
                jnp.where(hit, jnp.where(lane == k + i, 1.0, 0.0), real[k + i : k + i + 1]),
                jnp.where(hit, 0.0, imag[k + i : k + i + 1]),
            )
            for i in range(m)
        ]
        new = product(inverse, [[value] for value in old])
        new = [line[0] for line in new]
        inside = (rows >= k) & (rows < k + m)
        col_r = [jnp.where(inside, jnp.where(rows == k + j, -1.0, 0.0), col_r[j]) for j in range(m)]
        col_i = [jnp.where(inside, 0.0, col_i[j]) for j in range(m)]
        gone = inside | ((lanes >= k) & (lanes < k + m))
        out_r, out_i = [], []
        for t in range(n // 128):
            cut = slice(128 * t, 128 * t + 128)
            mask = gone if t == 0 else inside
            next_r = jnp.where(mask, 0.0, real[:, cut])
            next_i = jnp.where(mask, 0.0, imag[:, cut])
            for j in range(m):
                row_r, row_i = new[j][0][:, cut], new[j][1][:, cut]
                next_r = next_r - (col_r[j] * row_r - col_i[j] * row_i)
                next_i = next_i - (col_r[j] * row_i + col_i[j] * row_r)
            out_r.append(next_r)
            out_i.append(next_i)
        real = jnp.concatenate(out_r, axis=1)
        imag = jnp.concatenate(out_i, axis=1)
    return real, imag


def invert(real, imag):
    b = PANEL

    def panel(index, carry):
        start = pl.multiple_of(index * b, b)
        held = pl.ds(start, b)
        top_r, top_i = eliminate(real[held, :], imag[held, :])
        all_r, all_i = real[...], imag[...]
        lane = lax.broadcasted_iota(jnp.int32, (LAGS, 128), 1)
        row = lax.broadcasted_iota(jnp.int32, (LAGS, 128), 0)
        factor = jnp.where(lane < b, all_r[:, :128], pltpu.roll(all_i[:, :128], b, 1))
        inside = (row >= start) & (row < start + b)
        factor = jnp.where(inside | (lane >= 2 * b), 0.0, factor)
        right = jnp.concatenate(
            [
                jnp.concatenate([top_r, top_i], axis=1),
                jnp.concatenate([-top_i, top_r], axis=1),
                jnp.zeros((128 - 2 * b, 2 * LAGS), jnp.float32),
            ],
            axis=0,
        )
        update = dot(factor, right)
        column = lax.broadcasted_iota(jnp.int32, (LAGS, LAGS), 1)
        all_r = jnp.where(column < b, 0.0, all_r) - update[:, :LAGS]
        all_i = jnp.where(column < b, 0.0, all_i) - update[:, LAGS:]
        real[...] = pltpu.roll(all_r, LAGS - b, 1)
        imag[...] = pltpu.roll(all_i, LAGS - b, 1)
        real[held, :] = pltpu.roll(top_r, LAGS - b, 1)
        imag[held, :] = pltpu.roll(top_i, LAGS - b, 1)
        return carry

    lax.fori_loop(0, LAGS // b, panel, 0)


def normal_matrix(column, loading):
    i0 = lax.broadcasted_iota(jnp.int32, (LAGS, LAGS), 0)
    i1 = lax.broadcasted_iota(jnp.int32, (LAGS, LAGS), 1)
    flip = jnp.where(i0 + i1 == LAGS - 1, 1.0, 0.0)
    behind = pltpu.roll(dot(column, flip), 1, 1)
    lane = lax.broadcasted_iota(jnp.int32, behind.shape, 1)
    behind = jnp.where(lane == 0, 0.0, behind)
    base_r = toeplitz(jnp.concatenate([column[0:1], behind[0:1]], axis=1), LAGS)[:, :LAGS]
    base_i = toeplitz(jnp.concatenate([-column[1:2], behind[1:2]], axis=1), LAGS)[:, :LAGS]
    blank = jnp.zeros((1, LAGS), jnp.float32)
    edge_r = toeplitz(jnp.concatenate([blank, column[2:3]], axis=1), LAGS)[:, :LAGS]
    edge_i = toeplitz(jnp.concatenate([blank, column[3:4]], axis=1), LAGS)[:, :LAGS]
    one = jnp.concatenate([edge_r, edge_i], axis=1)
    two = jnp.concatenate([edge_i, -edge_r], axis=1)
    real = base_r - dot(one, one, NT)
    imag = base_i - dot(one, two, NT)
    diagonal = i0 == i1
    lam = loading * (jnp.sum(jnp.where(diagonal, real, 0.0)) / LAGS)
    return jnp.where(diagonal, real + lam, real), imag


def solve_kernel(loading, sums, weights, real, imag):
    joined = jnp.concatenate([sums[0], sums[1]], axis=1)
    start_r, start_i = normal_matrix(joined[32:40, :], loading[0])
    real[...] = start_r
    imag[...] = start_i
    invert(real, imag)
    half = (ROWS - 8) // 2
    c_re, c_im = joined[:half, :], joined[half : 2 * half, :]
    weights[...] = dot(joined[: 2 * half, :], real[...], NT) + dot(
        jnp.concatenate([-c_im, c_re], axis=0), imag[...], NT
    )


def solve(sums, loading):
    vmem = pl.BlockSpec(memory_space=pltpu.VMEM)
    return pl.pallas_call(
        solve_kernel,
        out_shape=jax.ShapeDtypeStruct((ROWS - 8, LAGS), jnp.float32),
        in_specs=[pl.BlockSpec(memory_space=pltpu.SMEM), vmem],
        out_specs=vmem,
        scratch_shapes=[pltpu.VMEM((LAGS, LAGS), jnp.float32)] * 2,
        name="solve",
    )(loading, sums)


def second_kernel(
    weights, table, surveillance, cells, energies,
    corr, landed, turned, power, ring_z, ring_y,
    far_send, far_recv, near_send, near_recv, z_send, z_recv, y_send, y_recv, e_send, e_recv,
):
    length = surveillance.shape[2]
    width = surveillance.shape[1]
    far, near = TM[:2], (TM[2], "chan")
    z, y, me_far, me_near = place(TM[1:2]), place(TM[:1]), place(far), place(near)
    barrier, total = greet([(far, tuple(range(1, 32))), (near, tuple(range(1, 8))), (TM[1:2], tuple(range(1, 8))), (TM[:1], (1, 2, 3))])
    pl.semaphore_wait(barrier, total)
    w = weights[...]
    w_re, w_im = w[:width], w[width:]
    on_re = halves(w)
    on_im = halves(jnp.concatenate([-w_im, w_re], axis=0))
    clutter = jnp.zeros((2 * width, length), jnp.float32)
    taps = []
    for half in range(2):
        cut = slice(256 - 128 * half, 256 - 128 * half + length)
        lags = slice(128 * half, 128 * half + 128)
        taps.append([[table[part, piece, :, cut] for piece in range(2)] for part in range(2)])
        clutter = clutter + dot3([x[:, lags] for x in on_re], taps[half][0])
        clutter = clutter + dot3([x[:, lags] for x in on_im], taps[half][1])
    residual = jnp.concatenate([surveillance[0], surveillance[1]], axis=0) - clutter
    energy = jnp.sum(residual * residual, axis=1, keepdims=True)
    energy = jnp.broadcast_to(energy[:width] + energy[width:], (width, 128))
    energy = jnp.concatenate([energy, jnp.zeros((128 - width, 128), jnp.float32)], axis=0)
    ring_z[z] = energy.T[:8]
    along_z = exchange(TM[1:2], lambda p: ring_z.at[z], lambda p: ring_z.at[p], z_send, z_recv)
    swapped = jnp.concatenate([residual[width:], -residual[:width]], axis=0)
    segments = length // SEG_LEN
    row = lax.broadcasted_iota(jnp.int32, (2 * width * segments, length), 0)
    col = lax.broadcasted_iota(jnp.int32, (2 * width * segments, length), 1)
    own = row // (2 * width) == col // SEG_LEN
    with_re = halves(jnp.where(own, jnp.concatenate([residual] * segments, axis=0), 0.0))
    with_im = halves(jnp.where(own, jnp.concatenate([swapped] * segments, axis=0), 0.0))
    for half in range(2):
        block = dot3(taps[half][0], with_re, NT) + dot3(taps[half][1], with_im, NT)
        corr[16 * half : 16 * half + 16] = block.reshape(16, 8, 128)
    to_far = exchange(far, lambda p: corr.at[p], lambda p: landed.at[p], far_send, far_recv)
    landed[me_far] = corr[me_far]
    finish(along_z)
    parts = [ring_z[i] for i in range(8)]
    ring_y[y] = ((parts[0] + parts[1]) + (parts[2] + parts[3])) + ((parts[4] + parts[5]) + (parts[6] + parts[7]))
    along_y = exchange(TM[:1], lambda p: ring_y.at[y], lambda p: ring_y.at[p], y_send, y_recv)
    finish(along_y)
    power[...] = (ring_y[0] + ring_y[1]) + (ring_y[2] + ring_y[3])
    energies[me_near] = power[...]
    to_all = exchange(near, lambda p: power, lambda p: energies.at[p], e_send, e_recv)
    finish(to_far)
    everything = landed[...]
    for lag in range(8):
        turned[lag] = everything[:, lag, :]
    to_near = exchange(near, lambda p: turned.at[p], lambda p: cells.at[p], near_send, near_recv)
    cells[me_near] = turned[me_near]
    finish(to_all)
    finish(to_near)


def second_pass(weights, table, surveillance):
    vmem = pl.BlockSpec(memory_space=pltpu.VMEM)
    dma = pltpu.SemaphoreType.DMA
    f32 = jnp.float32
    return pl.pallas_call(
        second_kernel,
        out_shape=[
            jax.ShapeDtypeStruct((8, 32, 128), f32),
            jax.ShapeDtypeStruct((8, 8, 128), f32),
        ],
        in_specs=[vmem] * 3,
        out_specs=[vmem] * 2,
        scratch_shapes=[
            pltpu.VMEM((32, 8, 128), f32),
            pltpu.VMEM((32, 8, 128), f32),
            pltpu.VMEM((8, 32, 128), f32),
            pltpu.VMEM((8, 128), f32),
            pltpu.VMEM((8, 8, 128), f32),
            pltpu.VMEM((4, 8, 128), f32),
            dma((31,)), dma((31,)), dma((7,)), dma((7,)), dma((7,)), dma((7,)), dma((3,)), dma((3,)), dma((7,)), dma((7,)),
        ],
        compiler_params=pltpu.CompilerParams(collective_id=1, has_side_effects=True),
        name="second_pass",
    )(weights, table, surveillance)


def doppler_tables(shards, segments):
    short = DOPP // segments
    order = np.arange(shards).reshape(-1, 2).T.reshape(-1)
    angle = 2.0 * np.pi / short * (np.outer(order, np.arange(short)) % short)
    table = np.concatenate([np.cos(angle), np.sin(angle)], axis=1)
    turn = 2.0 * np.pi / DOPP * np.outer(np.arange(segments), np.arange(DOPP))
    turns = np.stack([np.cos(turn), np.sin(turn)])
    return table.astype(np.float32), turns.astype(np.float32)


def doppler_kernel(samples, cells, energies, table, turns, out):
    near, _, lanes = cells.shape
    groups = near // 2
    segments = turns.shape[1]
    width = lanes // segments // 2
    basis = halves(table[...])
    short = DOPP // segments
    for g in range(groups):
        power = (energies[g] + energies[groups + g]) / samples
        scale = lax.rsqrt(samples * (power + EPSILON))
        by = jnp.broadcast_to(scale[0:1], (128, 128)).T[:width, 0:1]
        rows = jnp.concatenate([cells[g], cells[groups + g]], axis=0)
        wave = dot3(halves(rows.T), basis)
        total_r = total_i = None
        for s in range(segments):
            base = 2 * width * s
            a_r, a_i = wave[base : base + width, :short], wave[base : base + width, short:]
            b_r, b_i = (
                wave[base + width : base + 2 * width, :short],
                wave[base + width : base + 2 * width, short:],
            )
            y_r = (a_r + b_i) * by
            y_i = (b_r - a_i) * by
            y_r = jnp.concatenate([y_r] * segments, axis=1)
            y_i = jnp.concatenate([y_i] * segments, axis=1)
            if s == 0:
                total_r, total_i = y_r, y_i
                continue
            c, d = turns[0, s : s + 1, :], turns[1, s : s + 1, :]
            total_r = total_r + (y_r * c + y_i * d)
            total_i = total_i + (y_i * c - y_r * d)
        at = slice(width * g, width * g + width)
        out[0, 0, at, :] = total_r
        out[0, 1, at, :] = total_i


def doppler(cells, energies, segments, samples):
    vmem = pl.BlockSpec(memory_space=pltpu.VMEM)
    shards = 2 * cells.shape[1]
    table, turns = doppler_tables(shards, segments)
    width = cells.shape[2] // segments // 2
    return pl.pallas_call(
        functools.partial(doppler_kernel, samples),
        out_shape=jax.ShapeDtypeStruct((1, 2, width * cells.shape[0] // 2, DOPP), jnp.float32),
        in_specs=[vmem] * 4,
        out_specs=vmem,
        name="doppler",
    )(cells, energies, jnp.asarray(table), jnp.asarray(turns))


def per_device(reference_signal, surveillance, loading):
    shards = lax.axis_size(TM)
    length = reference_signal.shape[1]
    width = surveillance.shape[1]
    sums, table = first_pass(reference_signal, surveillance)
    weights = solve(sums, loading)
    cells, energies = second_pass(weights, table, surveillance)
    full = doppler(cells, energies, length // SEG_LEN, float(length * shards))
    return full, jnp.swapaxes(weights.reshape(2, width, LAGS), 1, 2)


def solution(mesh):
    split = Mesh(
        mesh.devices.reshape(4, 8, 2, mesh.shape["chan"]), ("tm_0", "tm_1", "tm_2", "chan")
    )
    in_specs = (P(None, TM), P(None, "chan", TM), P())
    out_specs = (P(TM_CHAN, None, None, None), P(None, None, "chan"))
    return jax.shard_map(
        per_device, mesh=split, in_specs=in_specs, out_specs=out_specs, check_vma=False
    )
```

```python
import functools

import jax
import jax.numpy as jnp
import numpy as np
from jax import lax
from jax.experimental import pallas as pl
from jax.experimental.pallas import tpu as pltpu
from jax.sharding import Mesh
from jax.sharding import PartitionSpec as P

LAGS = 256
DOPP = 1024
SEG_LEN = 512
TM = ("tm_0", "tm_1", "tm_2")
TM_CHAN = ("tm_0", "tm_1", "tm_2", "chan")
EPSILON = 1e-06
PANEL = 32
PIVOTS = 4
ROWS = 40
MESH = pl.DeviceIdType.MESH

highest = lax.Precision.HIGHEST
NN = (((1,), (0,)), ((), ()))
NT = (((1,), (1,)), ((), ()))


def dot(a, b, dims=NN):
    return lax.dot_general(a, b, dims, precision=highest, preferred_element_type=jnp.float32)


def halves(x):
    high = x.astype(jnp.bfloat16)
    return high, (x - high.astype(jnp.float32)).astype(jnp.bfloat16)


def dot3(a, b, dims=NN):
    def one(x, y):
        return lax.dot_general(x, y, dims, preferred_element_type=jnp.float32)

    return one(a[0], b[0]) + (one(a[0], b[1]) + one(a[1], b[0]))


def toeplitz(row, rows):
    wide = jnp.broadcast_to(row, (rows, row.shape[1]))
    return pltpu.roll(wide, 0, 1, stride=1, stride_axis=0)


def exchange(axes, src, dst, send, recv, start=True):
    sizes = [lax.axis_size(a) for a in axes]
    count = int(np.prod(sizes))
    here = place(axes)
    copies = []
    for d in range(1, count):
        there = lax.rem(here + d, count)
        copies.append(
            pltpu.make_async_remote_copy(
                src_ref=src(there),
                dst_ref=dst(here),
                send_sem=send.at[d - 1],
                recv_sem=recv.at[d - 1],
                device_id=device(axes, there),
                device_id_type=MESH,
            )
        )
        if start:
            copies[-1].start()
    return copies


def place(axes):
    index = lax.axis_index(axes[0])
    for a in axes[1:]:
        index = index * lax.axis_size(a) + lax.axis_index(a)
    return index


def device(axes, index):
    coordinates = {}
    for a in reversed(axes):
        coordinates[a] = lax.rem(index, lax.axis_size(a))
        index = lax.div(index, lax.axis_size(a))
    return coordinates


def greet(barrier, axes, offsets):
    count = int(np.prod([lax.axis_size(a) for a in axes]))
    here = place(axes)

    def one(d):
        pl.semaphore_signal(
            barrier, inc=1, device_id=device(axes, lax.rem(here + d, count)), device_id_type=MESH
        )

    for d in offsets:
        one(d)
    return len(offsets)


def finish(copies):
    for copy in copies:
        copy.wait()


def times(a, b):
    if a[1] is None and b[1] is None:
        return (a[0] * b[0], None)
    if a[1] is None:
        return (a[0] * b[0], a[0] * b[1])
    if b[1] is None:
        return (a[0] * b[0], a[1] * b[0])
    return (a[0] * b[0] - a[1] * b[1], a[0] * b[1] + a[1] * b[0])


def plus(a, b):
    if a[1] is None:
        return (a[0] + b[0], b[1])
    if b[1] is None:
        return (a[0] + b[0], a[1])
    return (a[0] + b[0], a[1] + b[1])


def minus(a, b):
    return (a[0] - b[0], None if b[1] is None else a[1] - b[1])


def negative(a):
    return (-a[0], None if a[1] is None else -a[1])


def conjugate(a):
    return (a[0], None if a[1] is None else -a[1])


def product(left, right):
    out = []
    for row in left:
        line = []
        for j in range(len(right[0])):
            total = times(row[0], right[0][j])
            for k in range(1, len(row)):
                total = plus(total, times(row[k], right[k][j]))
            line.append(total)
        out.append(line)
    return out


def adjoint(block):
    return [[conjugate(block[j][i]) for j in range(len(block))] for i in range(len(block[0]))]


def hermitian_inverse(block):
    size = len(block)
    if size == 1:
        return [[(1.0 / block[0][0][0], None)]]
    if size == 2:
        a, c, d = block[0][0][0], block[0][1], block[1][1][0]
        scale = 1.0 / (a * d - (c[0] * c[0] + c[1] * c[1]))
        off = (-c[0] * scale, -c[1] * scale)
        return [[(d * scale, None), off], [conjugate(off), (a * scale, None)]]
    half = size // 2
    head = [row[:half] for row in block[:half]]
    side = [row[half:] for row in block[:half]]
    tail = [row[half:] for row in block[half:]]
    head_inverse = hermitian_inverse(head)
    lifted = product(head_inverse, side)
    drop = product(adjoint(side), lifted)
    rest = [[minus(tail[i][j], drop[i][j]) for j in range(half)] for i in range(half)]
    rest_inverse = hermitian_inverse(rest)
    corner = product(lifted, rest_inverse)
    extra = product(corner, adjoint(lifted))
    first = [[plus(head_inverse[i][j], extra[i][j]) for j in range(half)] for i in range(half)]
    right = [[negative(corner[i][j]) for j in range(half)] for i in range(half)]
    below = adjoint(right)
    return [first[i] + right[i] for i in range(half)] + [below[i] + rest_inverse[i] for i in range(half)]


def eliminate(real, imag):
    height, n = real.shape
    m = PIVOTS
    lane = lax.broadcasted_iota(jnp.int32, (1, n), 1)
    lanes = lax.broadcasted_iota(jnp.int32, (height, 128), 1)
    rows = lax.broadcasted_iota(jnp.int32, (height, 128), 0)

    def wide(value):
        return None if value is None else jnp.concatenate([value] * (n // 128), axis=1)

    for k in range(0, height, m):
        col_r = [jnp.broadcast_to(real[:, k + j : k + j + 1], (height, 128)) for j in range(m)]
        col_i = [jnp.broadcast_to(imag[:, k + j : k + j + 1], (height, 128)) for j in range(m)]
        block = [
            [(col_r[j][k + i : k + i + 1], col_i[j][k + i : k + i + 1]) for j in range(m)]
            for i in range(m)
        ]
        inverse = [[(wide(q[0]), wide(q[1])) for q in row] for row in hermitian_inverse(block)]
        hit = (lane >= k) & (lane < k + m)
        old = [
            (
                jnp.where(hit, jnp.where(lane == k + i, 1.0, 0.0), real[k + i : k + i + 1]),
                jnp.where(hit, 0.0, imag[k + i : k + i + 1]),
            )
            for i in range(m)
        ]
        new = product(inverse, [[value] for value in old])
        new = [line[0] for line in new]
        inside = (rows >= k) & (rows < k + m)
        col_r = [jnp.where(inside, jnp.where(rows == k + j, -1.0, 0.0), col_r[j]) for j in range(m)]
        col_i = [jnp.where(inside, 0.0, col_i[j]) for j in range(m)]
        gone = inside | ((lanes >= k) & (lanes < k + m))
        out_r, out_i = [], []
        for t in range(n // 128):
            cut = slice(128 * t, 128 * t + 128)
            mask = gone if t == 0 else inside
            next_r = jnp.where(mask, 0.0, real[:, cut])
            next_i = jnp.where(mask, 0.0, imag[:, cut])
            for j in range(m):
                row_r, row_i = new[j][0][:, cut], new[j][1][:, cut]
                next_r = next_r - (col_r[j] * row_r - col_i[j] * row_i)
                next_i = next_i - (col_r[j] * row_i + col_i[j] * row_r)
            out_r.append(next_r)
            out_i.append(next_i)
        real = jnp.concatenate(out_r, axis=1)
        imag = jnp.concatenate(out_i, axis=1)
    return real, imag


def invert(real, imag, between):
    b = PANEL

    def panel(index, carry):
        between(index)
        start = pl.multiple_of(index * b, b)
        held = pl.ds(start, b)
        top_r, top_i = eliminate(real[held, :], imag[held, :])
        all_r, all_i = real[...], imag[...]
        lane = lax.broadcasted_iota(jnp.int32, (LAGS, 128), 1)
        row = lax.broadcasted_iota(jnp.int32, (LAGS, 128), 0)
        factor = jnp.where(lane < b, all_r[:, :128], pltpu.roll(all_i[:, :128], b, 1))
        inside = (row >= start) & (row < start + b)
        factor = jnp.where(inside | (lane >= 2 * b), 0.0, factor)
        right = jnp.concatenate(
            [
                jnp.concatenate([top_r, top_i], axis=1),
                jnp.concatenate([-top_i, top_r], axis=1),
                jnp.zeros((128 - 2 * b, 2 * LAGS), jnp.float32),
            ],
            axis=0,
        )
        update = dot(factor, right)
        column = lax.broadcasted_iota(jnp.int32, (LAGS, LAGS), 1)
        all_r = jnp.where(column < b, 0.0, all_r) - update[:, :LAGS]
        all_i = jnp.where(column < b, 0.0, all_i) - update[:, LAGS:]
        real[...] = pltpu.roll(all_r, LAGS - b, 1)
        imag[...] = pltpu.roll(all_i, LAGS - b, 1)
        real[held, :] = pltpu.roll(top_r, LAGS - b, 1)
        imag[held, :] = pltpu.roll(top_i, LAGS - b, 1)
        return carry

    lax.fori_loop(0, LAGS // b, panel, 0)


def normal_matrix(column, tail, loading):
    i0 = lax.broadcasted_iota(jnp.int32, (LAGS, LAGS), 0)
    i1 = lax.broadcasted_iota(jnp.int32, (LAGS, LAGS), 1)
    flip = jnp.where(i0 + i1 == LAGS - 1, 1.0, 0.0)
    behind = pltpu.roll(dot(column, flip), 1, 1)
    lane = lax.broadcasted_iota(jnp.int32, behind.shape, 1)
    behind = jnp.where(lane == 0, 0.0, behind)
    base_r = toeplitz(jnp.concatenate([column[0:1], behind[0:1]], axis=1), LAGS)[:, :LAGS]
    base_i = toeplitz(jnp.concatenate([-column[1:2], behind[1:2]], axis=1), LAGS)[:, :LAGS]
    blank = jnp.zeros((1, LAGS), jnp.float32)
    edge_r = toeplitz(jnp.concatenate([blank, tail[0:1]], axis=1), LAGS)[:, :LAGS]
    edge_i = toeplitz(jnp.concatenate([blank, tail[1:2]], axis=1), LAGS)[:, :LAGS]
    one = jnp.concatenate([edge_r, edge_i], axis=1)
    two = jnp.concatenate([edge_i, -edge_r], axis=1)
    real = base_r - dot(one, one, NT)
    imag = base_i - dot(one, two, NT)
    diagonal = i0 == i1
    lam = loading * (jnp.sum(jnp.where(diagonal, real, 0.0)) / LAGS)
    return jnp.where(diagonal, real + lam, real), imag


PAIR, FAR, NEAR = TM[2:], TM[:2], (TM[2], "chan")
ALONG_Y, ALONG_Z = TM[:1], TM[1:2]


def cancel_kernel(
    loading, reference, surveillance, weights, cells, energies,
    table, halo, tail, mine, gram_pair, gram_all, real, imag,
    pair, ring_y, ring_z, cross, corr, landed, turned, power, power_z, power_y,
    edge_sem, tail_send, tail_recv, gram_sem, gram_send, gram_recv,
    pair_sem, y_send, y_recv, z_send, z_recv, out_sem,
    far_send, far_recv, near_send, near_recv, pz_send, pz_recv, py_send, py_recv, pa_send, pa_recv,
):
    length = reference.shape[1]
    width = surveillance.shape[1]
    count = lax.axis_size(TM)
    here = place(TM)
    core, y, z, far, near = place(PAIR), place(ALONG_Y), place(ALONG_Z), place(FAR), place(NEAR)
    barrier = pltpu.get_barrier_semaphore()
    total = greet(barrier, TM, range(1, count))
    total += greet(barrier, NEAR, [d for d in range(1, 8) if d != 4])

    def fill(tile, part, window):
        high, low = halves(toeplitz(window, 128)[:, 128:])
        cut = slice(128 * tile, 128 * tile + 128)
        table[part, 0, :, cut] = high
        table[part, 1, :, cut] = low

    for part in range(2):
        for tile in range(3, (LAGS + length) // 128):
            fill(tile, part, reference[part : part + 1, 128 * tile - 384 : 128 * tile - 128])

    pl.semaphore_wait(barrier, total)
    forward = pltpu.make_async_remote_copy(
        src_ref=reference.at[:, pl.ds(length - LAGS, LAGS)],
        dst_ref=halo,
        send_sem=edge_sem.at[0],
        recv_sem=edge_sem.at[1],
        device_id=device(TM, lax.rem(here + 1, count)),
        device_id_type=MESH,
    )
    forward.start()
    source = reference.at[:, pl.ds(length - LAGS, LAGS)]

    def tail_copy(d, semaphore):
        return pltpu.make_async_remote_copy(
            src_ref=source,
            dst_ref=tail,
            send_sem=tail_send.at[semaphore],
            recv_sem=tail_recv.at[0],
            device_id=device(TM, lax.rem(here + d, count)),
            device_id_type=MESH,
        )

    @pl.when(here == count - 1)
    def _():
        tail[...] = reference[:, length - LAGS :]
        for d in range(1, count):
            tail_copy(d, d - 1).start()

    s_re, s_im = surveillance[0], surveillance[1]
    r_re, r_im = reference[0:1], reference[1:2]
    blank = jnp.zeros((6, length), jnp.float32)
    with_re = halves(jnp.concatenate([s_re, s_im, r_re, r_im, blank], axis=0))
    with_im = halves(jnp.concatenate([s_im, -s_re, r_im, -r_re, blank], axis=0))
    forward.wait()
    before = jnp.where(here > 0, halo[...], 0.0)
    for part in range(2):
        fill(1, part, before[part : part + 1])
        fill(2, part, jnp.concatenate([before[part : part + 1, 128:], reference[part : part + 1, :128]], axis=1))

    for half in range(2):
        cut = slice(256 - 128 * half, 256 - 128 * half + length)
        taps = [[table[part, piece, :, cut] for piece in range(2)] for part in range(2)]
        sums = dot3(taps[0], with_re, NT) + dot3(taps[1], with_im, NT)
        sums = jnp.concatenate([sums, jnp.zeros((128, 128 - ROWS), jnp.float32)], axis=1).T
        mine[half] = sums[: 2 * width]
        gram_pair[0, half : half + 1, :] = sums[2 * width : 2 * width + 1]
        gram_pair[0, 2 + half : 3 + half, :] = sums[2 * width + 1 : 2 * width + 2]
    finish(exchange(PAIR, lambda p: gram_pair.at[0], lambda p: gram_pair.at[1], gram_sem.at[0:1], gram_sem.at[1:2]))
    gram_all[far] = gram_pair[0] + gram_pair[1]
    to_gram = exchange(FAR, lambda p: gram_all.at[far], lambda p: gram_all.at[p], gram_send, gram_recv)
    exchange(PAIR, lambda p: mine.at[p], lambda p: pair, pair_sem.at[0:1], pair_sem.at[1:2])

    @pl.when(here == count - 1)
    def _():
        for d in range(1, count):
            tail_copy(d, d - 1).wait_send()

    @pl.when(here != count - 1)
    def _():
        tail_copy(1, 0).wait_recv()

    finish(to_gram)
    gram = jnp.sum(gram_all[...], axis=0)
    column = jnp.concatenate([gram[0:1], gram[1:2]], axis=1)
    column = jnp.concatenate([column, jnp.concatenate([gram[2:3], gram[3:4]], axis=1)], axis=0)
    column = jnp.concatenate([column, jnp.zeros((6, LAGS), jnp.float32)], axis=0)
    start_r, start_i = normal_matrix(column, tail[...], loading[0])
    real[...] = start_r
    imag[...] = start_i

    def pair_copy(start):
        return exchange(PAIR, lambda p: mine.at[p], lambda p: pair, pair_sem.at[0:1], pair_sem.at[1:2], start)

    def y_copy(start):
        return exchange(ALONG_Y, lambda p: ring_y.at[y], lambda p: ring_y.at[p], y_send, y_recv, start)

    def z_copy(start):
        return exchange(ALONG_Z, lambda p: ring_z.at[z], lambda p: ring_z.at[p], z_send, z_recv, start)

    def out_copy(start):
        return exchange(PAIR, lambda p: cross.at[core], lambda p: cross.at[p], out_sem.at[0:1], out_sem.at[1:2], start)

    def between(index):
        @pl.when(index == 1)
        def _():
            finish(pair_copy(False))
            ring_y[y] = mine[core] + pair[...]
            y_copy(True)

        @pl.when(index == 3)
        def _():
            finish(y_copy(False))
            ring_z[z] = (ring_y[0] + ring_y[1]) + (ring_y[2] + ring_y[3])
            z_copy(True)

        @pl.when(index == 6)
        def _():
            finish(z_copy(False))
            cross[core] = ((ring_z[0] + ring_z[1]) + (ring_z[2] + ring_z[3])) + (
                (ring_z[4] + ring_z[5]) + (ring_z[6] + ring_z[7])
            )
            out_copy(True)

    invert(real, imag, between)
    finish(out_copy(False))
    right = jnp.concatenate([cross[0], cross[1]], axis=1)
    spun = jnp.concatenate([-right[width:], right[:width]], axis=0)
    w = dot(right, real[...], NT) + dot(spun, imag[...], NT)
    weights[...] = w

    w_re, w_im = w[:width], w[width:]
    on_re = halves(w)
    on_im = halves(jnp.concatenate([-w_im, w_re], axis=0))
    clutter = jnp.zeros((2 * width, length), jnp.float32)
    taps = []
    for half in range(2):
        cut = slice(256 - 128 * half, 256 - 128 * half + length)
        lags = slice(128 * half, 128 * half + 128)
        taps.append([[table[part, piece, :, cut] for piece in range(2)] for part in range(2)])
        clutter = clutter + dot3([x[:, lags] for x in on_re], taps[half][0])
        clutter = clutter + dot3([x[:, lags] for x in on_im], taps[half][1])
    residual = jnp.concatenate([surveillance[0], surveillance[1]], axis=0) - clutter
    energy = jnp.sum(residual * residual, axis=1, keepdims=True)
    energy = jnp.broadcast_to(energy[:width] + energy[width:], (width, 128))
    energy = jnp.concatenate([energy, jnp.zeros((128 - width, 128), jnp.float32)], axis=0)
    power_z[z] = energy.T[:8]
    along_z = exchange(ALONG_Z, lambda p: power_z.at[z], lambda p: power_z.at[p], pz_send, pz_recv)
    swapped = jnp.concatenate([residual[width:], -residual[:width]], axis=0)
    segments = length // SEG_LEN
    row = lax.broadcasted_iota(jnp.int32, (2 * width * segments, length), 0)
    col = lax.broadcasted_iota(jnp.int32, (2 * width * segments, length), 1)
    own = row // (2 * width) == col // SEG_LEN
    with_re = halves(jnp.where(own, jnp.concatenate([residual] * segments, axis=0), 0.0))
    with_im = halves(jnp.where(own, jnp.concatenate([swapped] * segments, axis=0), 0.0))
    for half in range(2):
        block = dot3(taps[half][0], with_re, NT) + dot3(taps[half][1], with_im, NT)
        corr[16 * half : 16 * half + 16] = block.reshape(16, 8, 128)

    to_far = exchange(FAR, lambda p: corr.at[p], lambda p: landed.at[p], far_send, far_recv)
    landed[far] = corr[far]
    finish(along_z)
    parts = [power_z[i] for i in range(8)]
    power_y[y] = ((parts[0] + parts[1]) + (parts[2] + parts[3])) + ((parts[4] + parts[5]) + (parts[6] + parts[7]))
    finish(exchange(ALONG_Y, lambda p: power_y.at[y], lambda p: power_y.at[p], py_send, py_recv))
    power[...] = (power_y[0] + power_y[1]) + (power_y[2] + power_y[3])
    energies[near] = power[...]
    to_all = exchange(NEAR, lambda p: power, lambda p: energies.at[p], pa_send, pa_recv)
    finish(to_far)
    everything = landed[...]
    for lag in range(8):
        turned[lag] = everything[:, lag, :]
    to_near = exchange(NEAR, lambda p: turned.at[p], lambda p: cells.at[p], near_send, near_recv)
    cells[near] = turned[near]
    finish(to_all)
    finish(to_near)


def cancel(loading, reference, surveillance):
    vmem = pl.BlockSpec(memory_space=pltpu.VMEM)
    length = reference.shape[1]
    width = surveillance.shape[1]
    dma = pltpu.SemaphoreType.DMA

    def block(*shape):
        return pltpu.VMEM(shape, jnp.float32)

    half = (2 * width, 128)
    return pl.pallas_call(
        cancel_kernel,
        out_shape=[
            jax.ShapeDtypeStruct((2 * width, LAGS), jnp.float32),
            jax.ShapeDtypeStruct((8, 32, 128), jnp.float32),
            jax.ShapeDtypeStruct((8, 8, 128), jnp.float32),
        ],
        in_specs=[pl.BlockSpec(memory_space=pltpu.SMEM), vmem, vmem],
        out_specs=[vmem] * 3,
        scratch_shapes=[
            pltpu.VMEM((2, 2, 128, LAGS + length), jnp.bfloat16),
            block(2, LAGS), block(2, LAGS), block(2, *half), block(2, 4, 128), block(32, 4, 128),
            block(LAGS, LAGS), block(LAGS, LAGS),
            block(*half), block(4, *half), block(8, *half), block(2, *half),
            block(32, 8, 128), block(32, 8, 128), block(8, 32, 128), block(8, 128), block(8, 8, 128), block(4, 8, 128),
            dma((2,)), dma((63,)), dma((1,)), dma((2,)), dma((31,)), dma((31,)),
            dma((2,)), dma((3,)), dma((3,)), dma((7,)), dma((7,)), dma((2,)),
            dma((31,)), dma((31,)), dma((7,)), dma((7,)), dma((7,)), dma((7,)), dma((3,)), dma((3,)), dma((7,)), dma((7,)),
        ],
        compiler_params=pltpu.CompilerParams(collective_id=0, has_side_effects=True),
        name="cancel",
    )(loading, reference, surveillance)


def doppler_tables(shards, segments):
    short = DOPP // segments
    order = np.arange(shards).reshape(-1, 2).T.reshape(-1)
    angle = 2.0 * np.pi / short * (np.outer(order, np.arange(short)) % short)
    table = np.concatenate([np.cos(angle), np.sin(angle)], axis=1)
    turn = 2.0 * np.pi / DOPP * np.outer(np.arange(segments), np.arange(DOPP))
    turns = np.stack([np.cos(turn), np.sin(turn)])
    return table.astype(np.float32), turns.astype(np.float32)


def doppler_kernel(samples, cells, energies, table, turns, out):
    near, _, lanes = cells.shape
    groups = near // 2
    segments = turns.shape[1]
    width = lanes // segments // 2
    basis = halves(table[...])
    short = DOPP // segments
    for g in range(groups):
        power = (energies[g] + energies[groups + g]) / samples
        scale = lax.rsqrt(samples * (power + EPSILON))
        by = jnp.broadcast_to(scale[0:1], (128, 128)).T[:width, 0:1]
        rows = jnp.concatenate([cells[g], cells[groups + g]], axis=0)
        wave = dot3(halves(rows.T), basis)
        total_r = total_i = None
        for s in range(segments):
            base = 2 * width * s
            a_r, a_i = wave[base : base + width, :short], wave[base : base + width, short:]
            b_r, b_i = (
                wave[base + width : base + 2 * width, :short],
                wave[base + width : base + 2 * width, short:],
            )
            y_r = (a_r + b_i) * by
            y_i = (b_r - a_i) * by
            y_r = jnp.concatenate([y_r] * segments, axis=1)
            y_i = jnp.concatenate([y_i] * segments, axis=1)
            if s == 0:
                total_r, total_i = y_r, y_i
                continue
            c, d = turns[0, s : s + 1, :], turns[1, s : s + 1, :]
            total_r = total_r + (y_r * c + y_i * d)
            total_i = total_i + (y_i * c - y_r * d)
        at = slice(width * g, width * g + width)
        out[0, 0, at, :] = total_r
        out[0, 1, at, :] = total_i


def doppler(cells, energies, segments, samples):
    vmem = pl.BlockSpec(memory_space=pltpu.VMEM)
    shards = 2 * cells.shape[1]
    table, turns = doppler_tables(shards, segments)
    width = cells.shape[2] // segments // 2
    return pl.pallas_call(
        functools.partial(doppler_kernel, samples),
        out_shape=jax.ShapeDtypeStruct((1, 2, width * cells.shape[0] // 2, DOPP), jnp.float32),
        in_specs=[vmem] * 4,
        out_specs=vmem,
        name="doppler",
    )(cells, energies, jnp.asarray(table), jnp.asarray(turns))


def per_device(reference_signal, surveillance, loading):
    length = reference_signal.shape[1]
    width = surveillance.shape[1]
    samples = float(length * lax.axis_size(TM))
    weights, cells, energies = cancel(loading, reference_signal, surveillance)
    full = doppler(cells, energies, length // SEG_LEN, samples)
    return full, jnp.swapaxes(weights.reshape(2, width, LAGS), 1, 2)


def solution(mesh):
    split = Mesh(
        mesh.devices.reshape(4, 8, 2, mesh.shape["chan"]), ("tm_0", "tm_1", "tm_2", "chan")
    )
    in_specs = (P(None, TM), P(None, "chan", TM), P())
    out_specs = (P(TM_CHAN, None, None, None), P(None, None, "chan"))
    return jax.shard_map(
        per_device, mesh=split, in_specs=in_specs, out_specs=out_specs, check_vma=False
    )
```

```python
import functools

import jax
import jax.numpy as jnp
import numpy as np
from jax import lax
from jax.experimental import pallas as pl
from jax.experimental.pallas import tpu as pltpu
from jax.sharding import Mesh
from jax.sharding import PartitionSpec as P

LAGS = 256
DOPP = 1024
SEG_LEN = 512
TM = ("tm_0", "tm_1", "tm_2")
TM_CHAN = ("tm_0", "tm_1", "tm_2", "chan")
EPSILON = 1e-06
PANEL = 32
PIVOTS = 4
ROWS = 40
MESH = pl.DeviceIdType.MESH

highest = lax.Precision.HIGHEST
NN = (((1,), (0,)), ((), ()))
NT = (((1,), (1,)), ((), ()))


def dot(a, b, dims=NN):
    return lax.dot_general(a, b, dims, precision=highest, preferred_element_type=jnp.float32)


def halves(x):
    high = x.astype(jnp.bfloat16)
    return high, (x - high.astype(jnp.float32)).astype(jnp.bfloat16)


def dot3(a, b, dims=NN):
    def one(x, y):
        return lax.dot_general(x, y, dims, preferred_element_type=jnp.float32)

    return one(a[0], b[0]) + (one(a[0], b[1]) + one(a[1], b[0]))


def dot_beside(a, b):
    both = lax.dot_general(a[0], jnp.concatenate(b, axis=0), NT, preferred_element_type=jnp.float32)
    rest = lax.dot_general(a[1], b[0], NT, preferred_element_type=jnp.float32)
    return both[:, :128] + (both[:, 128:] + rest)


def dot_stacked(a, b):
    rows = a[0].shape[0]
    both = lax.dot_general(jnp.concatenate(a, axis=0), b[0], NN, preferred_element_type=jnp.float32)
    rest = lax.dot_general(a[0], b[1], NN, preferred_element_type=jnp.float32)
    return both[:rows] + (both[rows:] + rest)


def toeplitz(row, rows):
    wide = jnp.broadcast_to(row, (rows, row.shape[1]))
    return pltpu.roll(wide, 0, 1, stride=1, stride_axis=0)


def exchange(axes, src, dst, send, recv, start=True):
    sizes = [lax.axis_size(a) for a in axes]
    count = int(np.prod(sizes))
    here = place(axes)
    copies = []
    for d in range(1, count):
        there = lax.rem(here + d, count)
        copies.append(
            pltpu.make_async_remote_copy(
                src_ref=src(there),
                dst_ref=dst(here),
                send_sem=send.at[d - 1],
                recv_sem=recv.at[d - 1],
                device_id=device(axes, there),
                device_id_type=MESH,
            )
        )
        if start:
            copies[-1].start()
    return copies


def place(axes):
    index = lax.axis_index(axes[0])
    for a in axes[1:]:
        index = index * lax.axis_size(a) + lax.axis_index(a)
    return index


def device(axes, index):
    coordinates = {}
    for a in reversed(axes):
        coordinates[a] = lax.rem(index, lax.axis_size(a))
        index = lax.div(index, lax.axis_size(a))
    return coordinates


def greet(barrier, axes, offsets):
    count = int(np.prod([lax.axis_size(a) for a in axes]))
    here = place(axes)

    def one(d):
        pl.semaphore_signal(
            barrier, inc=1, device_id=device(axes, lax.rem(here + d, count)), device_id_type=MESH
        )

    for d in offsets:
        one(d)
    return len(offsets)


def finish(copies):
    for copy in copies:
        copy.wait()


def times(a, b):
    if a[1] is None and b[1] is None:
        return (a[0] * b[0], None)
    if a[1] is None:
        return (a[0] * b[0], a[0] * b[1])
    if b[1] is None:
        return (a[0] * b[0], a[1] * b[0])
    return (a[0] * b[0] - a[1] * b[1], a[0] * b[1] + a[1] * b[0])


def plus(a, b):
    if a[1] is None:
        return (a[0] + b[0], b[1])
    if b[1] is None:
        return (a[0] + b[0], a[1])
    return (a[0] + b[0], a[1] + b[1])


def minus(a, b):
    return (a[0] - b[0], None if b[1] is None else a[1] - b[1])


def negative(a):
    return (-a[0], None if a[1] is None else -a[1])


def conjugate(a):
    return (a[0], None if a[1] is None else -a[1])


def product(left, right):
    out = []
    for row in left:
        line = []
        for j in range(len(right[0])):
            total = times(row[0], right[0][j])
            for k in range(1, len(row)):
                total = plus(total, times(row[k], right[k][j]))
            line.append(total)
        out.append(line)
    return out


def adjoint(block):
    return [[conjugate(block[j][i]) for j in range(len(block))] for i in range(len(block[0]))]


def hermitian_inverse(block):
    size = len(block)
    if size == 1:
        return [[(1.0 / block[0][0][0], None)]]
    if size == 2:
        a, c, d = block[0][0][0], block[0][1], block[1][1][0]
        scale = 1.0 / (a * d - (c[0] * c[0] + c[1] * c[1]))
        off = (-c[0] * scale, -c[1] * scale)
        return [[(d * scale, None), off], [conjugate(off), (a * scale, None)]]
    half = size // 2
    head = [row[:half] for row in block[:half]]
    side = [row[half:] for row in block[:half]]
    tail = [row[half:] for row in block[half:]]
    head_inverse = hermitian_inverse(head)
    lifted = product(head_inverse, side)
    drop = product(adjoint(side), lifted)
    rest = [[minus(tail[i][j], drop[i][j]) for j in range(half)] for i in range(half)]
    rest_inverse = hermitian_inverse(rest)
    corner = product(lifted, rest_inverse)
    extra = product(corner, adjoint(lifted))
    first = [[plus(head_inverse[i][j], extra[i][j]) for j in range(half)] for i in range(half)]
    right = [[negative(corner[i][j]) for j in range(half)] for i in range(half)]
    below = adjoint(right)
    return [first[i] + right[i] for i in range(half)] + [below[i] + rest_inverse[i] for i in range(half)]


def added(terms):
    while len(terms) > 1:
        terms = [sum(terms[i : i + 2][1:], terms[i]) for i in range(0, len(terms), 2)]
    return terms[0]


def eliminate(real, imag, first):
    height, n = real.shape
    m = PIVOTS
    lane = lax.broadcasted_iota(jnp.int32, (1, n), 1)
    lanes = lax.broadcasted_iota(jnp.int32, (height, 128), 1)
    rows = lax.broadcasted_iota(jnp.int32, (height, 128), 0)

    def wide(value):
        return None if value is None else jnp.concatenate([value] * (n // 128), axis=1)

    for k in range(0, height, m):
        at = first + k
        col_r = [jnp.broadcast_to(real[:, at + j : at + j + 1], (height, 128)) for j in range(m)]
        col_i = [jnp.broadcast_to(imag[:, at + j : at + j + 1], (height, 128)) for j in range(m)]
        block = [
            [(col_r[j][k + i : k + i + 1], col_i[j][k + i : k + i + 1]) for j in range(m)]
            for i in range(m)
        ]
        inverse = [[(wide(q[0]), wide(q[1])) for q in row] for row in hermitian_inverse(block)]
        hit = (lane >= at) & (lane < at + m)
        old = [
            (
                jnp.where(hit, jnp.where(lane == at + i, 1.0, 0.0), real[k + i : k + i + 1]),
                jnp.where(hit, 0.0, imag[k + i : k + i + 1]),
            )
            for i in range(m)
        ]
        new = product(inverse, [[value] for value in old])
        new = [line[0] for line in new]
        inside = (rows >= k) & (rows < k + m)
        col_r = [jnp.where(inside, jnp.where(rows == k + j, -1.0, 0.0), col_r[j]) for j in range(m)]
        col_i = [jnp.where(inside, 0.0, col_i[j]) for j in range(m)]
        gone = inside | ((lanes >= at % 128) & (lanes < at % 128 + m))
        out_r, out_i = [], []
        for t in range(n // 128):
            cut = slice(128 * t, 128 * t + 128)
            mask = gone if t == at // 128 else inside
            next_r = jnp.where(mask, 0.0, real[:, cut])
            next_i = jnp.where(mask, 0.0, imag[:, cut])
            terms_r, terms_i = [], []
            for j in range(m):
                row_r, row_i = new[j][0][:, cut], new[j][1][:, cut]
                terms_r.append(col_r[j] * row_r - col_i[j] * row_i)
                terms_i.append(col_r[j] * row_i + col_i[j] * row_r)
            out_r.append(next_r - added(terms_r))
            out_i.append(next_i - added(terms_i))
        real = jnp.concatenate(out_r, axis=1)
        imag = jnp.concatenate(out_i, axis=1)
    return real, imag


def thirds(x):
    high = x.astype(jnp.bfloat16)
    rest = x - high.astype(jnp.float32)
    middle = rest.astype(jnp.bfloat16)
    return high, middle, (rest - middle.astype(jnp.float32)).astype(jnp.bfloat16)


def packed(factor, top_r, top_i, first):
    turned = first // PANEL
    high, middle, low = [
        [x[:PANEL], x[PANEL:]]
        for x in thirds(
            jnp.concatenate(
                [jnp.concatenate([top_r, top_i], axis=1), jnp.concatenate([-top_i, top_r], axis=1)], axis=0
            )
        )
    ]
    blocks = []
    for pieces in (high + middle, low + high, middle + high):
        blocks += pieces[4 - turned :] + pieces[: 4 - turned]
    right = jnp.concatenate(blocks, axis=0)
    high = factor.astype(jnp.bfloat16).astype(jnp.float32)
    rest = factor - high
    middle = rest.astype(jnp.bfloat16).astype(jnp.float32)
    low = rest - middle
    left = [high + pltpu.roll(high, 64, 1), high + pltpu.roll(middle, 64, 1), middle + pltpu.roll(low, 64, 1)]
    left = jnp.concatenate(left, axis=1).astype(jnp.bfloat16)
    return lax.dot_general(left, right, NN, preferred_element_type=jnp.float32)


def factors(real, imag, first):
    lane = lax.broadcasted_iota(jnp.int32, real.shape, 1)
    behind = (first + PANEL) % 128
    in_r = (lane >= first) & (lane < first + PANEL)
    in_i = (lane >= behind) & (lane < behind + PANEL)
    return jnp.where(in_r, real, jnp.where(in_i, pltpu.roll(imag, PANEL, 1), 0.0))


def without(x, first):
    tile = first // 128
    cut = x[:, 128 * tile : 128 * tile + 128]
    lane = lax.broadcasted_iota(jnp.int32, cut.shape, 1) + 128 * tile
    cut = jnp.where((lane >= first) & (lane < first + PANEL), 0.0, cut)
    return jnp.concatenate([cut, x[:, 128:]] if tile == 0 else [x[:, :128], cut], axis=1)


def invert(real, imag, between):
    b = PANEL
    panels = LAGS // b

    def update(rows, last, done):
        first = last * b
        tile = slice(first // 128 * 128, first // 128 * 128 + 128)
        old_r, old_i = real[rows, :], imag[rows, :]
        change = packed(factors(old_r[:, tile], old_i[:, tile], first % 128), *done, first % 128)
        return without(old_r, first) - change[:, :LAGS], without(old_i, first) - change[:, LAGS:]

    def apply(last, done):
        held = slice(last * b, last * b + b)
        new_r, new_i = update(slice(0, LAGS), last, done)
        for rows in (slice(0, last * b), slice(last * b + b, LAGS)):
            if rows.start < rows.stop:
                real[rows, :] = new_r[rows]
                imag[rows, :] = new_i[rows]
        real[held, :] = done[0]
        imag[held, :] = done[1]

    top = (real[:b, :], imag[:b, :])
    done = None
    for p in range(panels):
        between(p)
        if done is not None:
            apply(p - 1, done)
        done = eliminate(*top, p * b)
        if p + 1 < panels:
            top = update(slice(p * b + b, p * b + 2 * b), p, done)
    apply(panels - 1, done)


def edge_matrix(tail):
    blank = jnp.zeros((1, LAGS), jnp.float32)
    edge_r = toeplitz(jnp.concatenate([blank, tail[0:1]], axis=1), LAGS)[:, :LAGS]
    edge_i = toeplitz(jnp.concatenate([blank, tail[1:2]], axis=1), LAGS)[:, :LAGS]
    one = jnp.concatenate([edge_r, edge_i], axis=1)
    two = jnp.concatenate([edge_i, -edge_r], axis=1)
    return dot(one, one, NT), dot(one, two, NT)


def normal_matrix(column, edge_r, edge_i, loading):
    i0 = lax.broadcasted_iota(jnp.int32, (LAGS, LAGS), 0)
    i1 = lax.broadcasted_iota(jnp.int32, (LAGS, LAGS), 1)
    flip = jnp.where(i0 + i1 == LAGS - 1, 1.0, 0.0)
    behind = pltpu.roll(dot(column, flip), 1, 1)
    lane = lax.broadcasted_iota(jnp.int32, behind.shape, 1)
    behind = jnp.where(lane == 0, 0.0, behind)
    base_r = toeplitz(jnp.concatenate([column[0:1], behind[0:1]], axis=1), LAGS)[:, :LAGS]
    base_i = toeplitz(jnp.concatenate([-column[1:2], behind[1:2]], axis=1), LAGS)[:, :LAGS]
    diagonal = i0 == i1
    off = jnp.sum(jnp.sum(jnp.where(diagonal, edge_r, 0.0), axis=0, keepdims=True), axis=1, keepdims=True)
    lam = loading * (column[0:1, 0:1] - off / LAGS)
    real = base_r - edge_r
    return jnp.where(diagonal, real + lam, real), base_i - edge_i


PAIR, FAR, NEAR = TM[2:], TM[:2], (TM[2], "chan")
ALONG_Y, ALONG_Z = TM[:1], TM[1:2]


def cancel_kernel(
    loading, reference, surveillance, weights, cells, energies,
    table, halo, tail, mine, gram_pair, gram_all, real, imag,
    pair, ring_y, ring_z, cross, corr, landed, turned, power, power_z, power_y,
    edge_sem, tail_send, tail_recv, gram_sem, gram_send, gram_recv,
    pair_sem, y_send, y_recv, z_send, z_recv, out_sem,
    far_send, far_recv, near_send, near_recv, pz_send, pz_recv, py_send, py_recv, pa_send, pa_recv,
):
    length = reference.shape[1]
    width = surveillance.shape[1]
    count = lax.axis_size(TM)
    here = place(TM)
    core, y, z, far, near = place(PAIR), place(ALONG_Y), place(ALONG_Z), place(FAR), place(NEAR)
    barrier = pltpu.get_barrier_semaphore()
    total = greet(barrier, TM, range(1, count))
    total += greet(barrier, NEAR, [d for d in range(1, 8) if d != 4])

    sums = [[jnp.zeros((128, 128), jnp.float32)] * 2 for _ in range(2)]

    def fill(tile, windows):
        delayed = [toeplitz(x, 128)[:, 128:] for x in windows]
        at = slice(128 * tile, 128 * tile + 128)
        for part in range(2):
            high, low = halves(delayed[part])
            table[part, 0, :, at] = high
            table[part, 1, :, at] = low
        for half in range(2):
            start = 128 * (tile - 2 + half)
            if 0 <= start < length:
                now_r, now_i = reference[0:1, start : start + 128], reference[1:2, start : start + 128]
                sums[half][0] = sums[half][0] + (delayed[0] * now_r + delayed[1] * now_i)
                sums[half][1] = sums[half][1] + (delayed[0] * now_i - delayed[1] * now_r)

    for tile in range(3, (LAGS + length) // 128):
        fill(tile, [reference[part : part + 1, 128 * tile - 384 : 128 * tile - 128] for part in range(2)])

    pl.semaphore_wait(barrier, total)
    forward = pltpu.make_async_remote_copy(
        src_ref=reference.at[:, pl.ds(length - LAGS, LAGS)],
        dst_ref=halo,
        send_sem=edge_sem.at[0],
        recv_sem=edge_sem.at[1],
        device_id=device(TM, lax.rem(here + 1, count)),
        device_id_type=MESH,
    )
    forward.start()
    source = reference.at[:, pl.ds(length - LAGS, LAGS)]

    def tail_copy(d, semaphore):
        return pltpu.make_async_remote_copy(
            src_ref=source,
            dst_ref=tail,
            send_sem=tail_send.at[semaphore],
            recv_sem=tail_recv.at[0],
            device_id=device(TM, lax.rem(here + d, count)),
            device_id_type=MESH,
        )

    @pl.when(here == count - 1)
    def _():
        tail[...] = reference[:, length - LAGS :]
        for d in range(1, count):
            tail_copy(d, d - 1).start()

    forward.wait()
    before = jnp.where(here > 0, halo[...], 0.0)
    fill(1, [before[part : part + 1] for part in range(2)])
    fill(2, [jnp.concatenate([before[part : part + 1, 128:], reference[part : part + 1, :128]], axis=1) for part in range(2)])
    for half in range(2):
        for part in range(2):
            line = jnp.sum(sums[half][part].T, axis=0, keepdims=True)
            gram_pair[0, 2 * part + half : 2 * part + half + 1, :] = line
    finish(exchange(PAIR, lambda p: gram_pair.at[0], lambda p: gram_pair.at[1], gram_sem.at[0:1], gram_sem.at[1:2]))
    gram_all[far] = gram_pair[0] + gram_pair[1]
    to_gram = exchange(FAR, lambda p: gram_all.at[far], lambda p: gram_all.at[p], gram_send, gram_recv)

    s_re, s_im = surveillance[0], surveillance[1]
    blank = jnp.zeros((128 - 2 * width, length), jnp.float32)
    with_re = halves(jnp.concatenate([s_re, s_im, blank], axis=0))
    with_im = halves(jnp.concatenate([s_im, -s_re, blank], axis=0))
    for half in range(2):
        cut = slice(256 - 128 * half, 256 - 128 * half + length)
        taps = [[table[part, piece, :, cut] for piece in range(2)] for part in range(2)]
        mine[half] = (dot_beside(taps[0], with_re) + dot_beside(taps[1], with_im)).T[: 2 * width]
    exchange(PAIR, lambda p: mine.at[p], lambda p: pair, pair_sem.at[0:1], pair_sem.at[1:2])

    @pl.when(here == count - 1)
    def _():
        for d in range(1, count):
            tail_copy(d, d - 1).wait_send()

    @pl.when(here != count - 1)
    def _():
        tail_copy(1, 0).wait_recv()

    edge_r, edge_i = edge_matrix(tail[...])
    real[...] = edge_r
    imag[...] = edge_i
    finish(to_gram)
    gram = jnp.sum(gram_all[...], axis=0)
    column = jnp.concatenate([gram[0:1], gram[1:2]], axis=1)
    column = jnp.concatenate([column, jnp.concatenate([gram[2:3], gram[3:4]], axis=1)], axis=0)
    column = jnp.concatenate([column, jnp.zeros((6, LAGS), jnp.float32)], axis=0)
    start_r, start_i = normal_matrix(column, real[...], imag[...], loading[0])
    real[...] = start_r
    imag[...] = start_i

    def pair_copy(start):
        return exchange(PAIR, lambda p: mine.at[p], lambda p: pair, pair_sem.at[0:1], pair_sem.at[1:2], start)

    def y_copy(start):
        return exchange(ALONG_Y, lambda p: ring_y.at[y], lambda p: ring_y.at[p], y_send, y_recv, start)

    def z_copy(start):
        return exchange(ALONG_Z, lambda p: ring_z.at[z], lambda p: ring_z.at[p], z_send, z_recv, start)

    def out_copy(start):
        return exchange(PAIR, lambda p: cross.at[core], lambda p: cross.at[p], out_sem.at[0:1], out_sem.at[1:2], start)

    def between(index):
        if index == 1:
            finish(pair_copy(False))
            ring_y[y] = mine[core] + pair[...]
            y_copy(True)
        if index == 3:
            finish(y_copy(False))
            ring_z[z] = (ring_y[0] + ring_y[1]) + (ring_y[2] + ring_y[3])
            z_copy(True)
        if index == 6:
            finish(z_copy(False))
            cross[core] = ((ring_z[0] + ring_z[1]) + (ring_z[2] + ring_z[3])) + (
                (ring_z[4] + ring_z[5]) + (ring_z[6] + ring_z[7])
            )
            out_copy(True)

    invert(real, imag, between)
    finish(out_copy(False))
    right = jnp.concatenate([cross[0], cross[1]], axis=1)
    spun = jnp.concatenate([-right[width:], right[:width]], axis=0)
    w = dot(right, real[...], NT) + dot(spun, imag[...], NT)
    weights[...] = w

    w_re, w_im = w[:width], w[width:]
    on_re = halves(w)
    on_im = halves(jnp.concatenate([-w_im, w_re], axis=0))
    taps = []
    for half in range(2):
        cut = slice(256 - 128 * half, 256 - 128 * half + length)
        taps.append([[table[part, piece, :, cut] for piece in range(2)] for part in range(2)])
    joined = [[jnp.concatenate([taps[0][part][piece], taps[1][part][piece]], axis=0) for piece in range(2)] for part in range(2)]
    clutter = dot_stacked(on_re, joined[0]) + dot_stacked(on_im, joined[1])
    residual = jnp.concatenate([surveillance[0], surveillance[1]], axis=0) - clutter
    energy = jnp.sum(residual * residual, axis=1, keepdims=True)
    energy = jnp.broadcast_to(energy[:width] + energy[width:], (width, 128))
    energy = jnp.concatenate([energy, jnp.zeros((128 - width, 128), jnp.float32)], axis=0)
    power_z[z] = energy.T[:8]
    along_z = exchange(ALONG_Z, lambda p: power_z.at[z], lambda p: power_z.at[p], pz_send, pz_recv)
    swapped = jnp.concatenate([residual[width:], -residual[:width]], axis=0)
    segments = length // SEG_LEN
    row = lax.broadcasted_iota(jnp.int32, (2 * width * segments, length), 0)
    col = lax.broadcasted_iota(jnp.int32, (2 * width * segments, length), 1)
    own = row // (2 * width) == col // SEG_LEN
    with_re = halves(jnp.where(own, jnp.concatenate([residual] * segments, axis=0), 0.0))
    with_im = halves(jnp.where(own, jnp.concatenate([swapped] * segments, axis=0), 0.0))
    for half in range(2):
        block = dot_beside(taps[half][0], with_re) + dot_beside(taps[half][1], with_im)
        corr[16 * half : 16 * half + 16] = block.reshape(16, 8, 128)

    to_far = exchange(FAR, lambda p: corr.at[p], lambda p: landed.at[p], far_send, far_recv)
    landed[far] = corr[far]
    finish(along_z)
    parts = [power_z[i] for i in range(8)]
    power_y[y] = ((parts[0] + parts[1]) + (parts[2] + parts[3])) + ((parts[4] + parts[5]) + (parts[6] + parts[7]))
    finish(exchange(ALONG_Y, lambda p: power_y.at[y], lambda p: power_y.at[p], py_send, py_recv))
    power[...] = (power_y[0] + power_y[1]) + (power_y[2] + power_y[3])
    energies[near] = power[...]
    to_all = exchange(NEAR, lambda p: power, lambda p: energies.at[p], pa_send, pa_recv)
    finish(to_far)
    everything = landed[...]
    for lag in range(8):
        turned[lag] = everything[:, lag, :]
    to_near = exchange(NEAR, lambda p: turned.at[p], lambda p: cells.at[p], near_send, near_recv)
    cells[near] = turned[near]
    finish(to_all)
    finish(to_near)


def cancel(loading, reference, surveillance):
    vmem = pl.BlockSpec(memory_space=pltpu.VMEM)
    length = reference.shape[1]
    width = surveillance.shape[1]
    dma = pltpu.SemaphoreType.DMA

    def block(*shape):
        return pltpu.VMEM(shape, jnp.float32)

    half = (2 * width, 128)
    return pl.pallas_call(
        cancel_kernel,
        out_shape=[
            jax.ShapeDtypeStruct((2 * width, LAGS), jnp.float32),
            jax.ShapeDtypeStruct((8, 32, 128), jnp.float32),
            jax.ShapeDtypeStruct((8, 8, 128), jnp.float32),
        ],
        in_specs=[pl.BlockSpec(memory_space=pltpu.SMEM), vmem, vmem],
        out_specs=[vmem] * 3,
        scratch_shapes=[
            pltpu.VMEM((2, 2, 128, LAGS + length), jnp.bfloat16),
            block(2, LAGS), block(2, LAGS), block(2, *half), block(2, 4, 128), block(32, 4, 128),
            block(LAGS, LAGS), block(LAGS, LAGS),
            block(*half), block(4, *half), block(8, *half), block(2, *half),
            block(32, 8, 128), block(32, 8, 128), block(8, 32, 128), block(8, 128), block(8, 8, 128), block(4, 8, 128),
            dma((2,)), dma((63,)), dma((1,)), dma((2,)), dma((31,)), dma((31,)),
            dma((2,)), dma((3,)), dma((3,)), dma((7,)), dma((7,)), dma((2,)),
            dma((31,)), dma((31,)), dma((7,)), dma((7,)), dma((7,)), dma((7,)), dma((3,)), dma((3,)), dma((7,)), dma((7,)),
        ],
        compiler_params=pltpu.CompilerParams(collective_id=0, has_side_effects=True),
        name="cancel",
    )(loading, reference, surveillance)


def doppler_tables(shards, segments):
    short = DOPP // segments
    order = np.arange(shards).reshape(-1, 2).T.reshape(-1)
    angle = 2.0 * np.pi / short * (np.outer(order, np.arange(short)) % short)
    table = np.concatenate([np.cos(angle), np.sin(angle)], axis=1)
    turn = 2.0 * np.pi / DOPP * np.outer(np.arange(segments), np.arange(DOPP))
    turns = np.stack([np.cos(turn), np.sin(turn)])
    return table.astype(np.float32), turns.astype(np.float32)


def doppler_kernel(samples, weights, cells, energies, table, turns, out, kept, held, sems):
    near, _, lanes = cells.shape
    groups = near // 2
    segments = turns.shape[1]
    width = lanes // segments // 2
    basis = halves(table[...])
    short = DOPP // segments
    copies = []
    for g in range(groups):
        power = (energies[g] + energies[groups + g]) / samples
        scale = lax.rsqrt(samples * (power + EPSILON))
        by = jnp.broadcast_to(scale[0:1], (128, 128)).T[:width, 0:1]
        rows = jnp.concatenate([cells[g], cells[groups + g]], axis=0)
        wave = dot3(halves(rows.T), basis)
        total_r = total_i = None
        for s in range(segments):
            base = 2 * width * s
            a_r, a_i = wave[base : base + width, :short], wave[base : base + width, short:]
            b_r, b_i = (
                wave[base + width : base + 2 * width, :short],
                wave[base + width : base + 2 * width, short:],
            )
            y_r = (a_r + b_i) * by
            y_i = (b_r - a_i) * by
            y_r = jnp.concatenate([y_r] * segments, axis=1)
            y_i = jnp.concatenate([y_i] * segments, axis=1)
            if s == 0:
                total_r, total_i = y_r, y_i
                continue
            c, d = turns[0, s : s + 1, :], turns[1, s : s + 1, :]
            total_r = total_r + (y_r * c + y_i * d)
            total_i = total_i + (y_i * c - y_r * d)
        held[g, 0] = total_r
        held[g, 1] = total_i
        copy = pltpu.make_async_copy(held.at[g], out.at[0, :, pl.ds(width * g, width), :], sems.at[g])
        copy.start()
        copies.append(copy)
    kept[...] = weights[...]
    for copy in copies:
        copy.wait()


def doppler(weights, cells, energies, segments, samples):
    vmem = pl.BlockSpec(memory_space=pltpu.VMEM)
    shards = 2 * cells.shape[1]
    table, turns = doppler_tables(shards, segments)
    width = cells.shape[2] // segments // 2
    groups = cells.shape[0] // 2
    return pl.pallas_call(
        functools.partial(doppler_kernel, samples),
        out_shape=[
            jax.ShapeDtypeStruct((1, 2, width * groups, DOPP), jnp.float32),
            jax.ShapeDtypeStruct(weights.shape, jnp.float32),
        ],
        in_specs=[vmem] * 5,
        out_specs=[pl.BlockSpec(memory_space=pl.ANY), vmem],
        scratch_shapes=[
            pltpu.VMEM((groups, 2, width, DOPP), jnp.float32),
            pltpu.SemaphoreType.DMA((groups,)),
        ],
        name="doppler",
    )(weights, cells, energies, jnp.asarray(table), jnp.asarray(turns))


def per_device(reference_signal, surveillance, loading):
    length = reference_signal.shape[1]
    samples = float(length * lax.axis_size(TM))
    weights, cells, energies = cancel(loading, reference_signal, surveillance)
    full, weights = doppler(weights, cells, energies, length // SEG_LEN, samples)
    return full, jnp.swapaxes(weights.reshape(2, -1, LAGS), 1, 2)


def solution(mesh):
    split = Mesh(
        mesh.devices.reshape(4, 8, 2, mesh.shape["chan"]), ("tm_0", "tm_1", "tm_2", "chan")
    )
    in_specs = (P(None, TM), P(None, "chan", TM), P())
    out_specs = (P(TM_CHAN, None, None, None), P(None, None, "chan"))
    return jax.shard_map(
        per_device, mesh=split, in_specs=in_specs, out_specs=out_specs, check_vma=False
    )
```

```python
import functools

import jax
import jax.numpy as jnp
import numpy as np
from jax import lax
from jax.experimental import pallas as pl
from jax.experimental.pallas import tpu as pltpu
from jax.sharding import Mesh
from jax.sharding import PartitionSpec as P

LAGS = 256
DOPP = 1024
SEG_LEN = 512
TM = ("tm_0", "tm_1", "tm_2")
TM_CHAN = ("tm_0", "tm_1", "tm_2", "chan")
EPSILON = 1e-06
PANEL = 32
UNROLL = 2
PIVOTS = 4
ROWS = 40
MESH = pl.DeviceIdType.MESH

highest = lax.Precision.HIGHEST
NN = (((1,), (0,)), ((), ()))
NT = (((1,), (1,)), ((), ()))


def dot(a, b, dims=NN):
    return lax.dot_general(a, b, dims, precision=highest, preferred_element_type=jnp.float32)


def halves(x):
    high = x.astype(jnp.bfloat16)
    return high, (x - high.astype(jnp.float32)).astype(jnp.bfloat16)


def dot3(a, b, dims=NN):
    def one(x, y):
        return lax.dot_general(x, y, dims, preferred_element_type=jnp.float32)

    return one(a[0], b[0]) + (one(a[0], b[1]) + one(a[1], b[0]))


def dot_beside(a, b):
    both = lax.dot_general(a[0], jnp.concatenate(b, axis=0), NT, preferred_element_type=jnp.float32)
    rest = lax.dot_general(a[1], b[0], NT, preferred_element_type=jnp.float32)
    return both[:, :128] + (both[:, 128:] + rest)


def dot_stacked(a, b):
    rows = a[0].shape[0]
    both = lax.dot_general(jnp.concatenate(a, axis=0), b[0], NN, preferred_element_type=jnp.float32)
    rest = lax.dot_general(a[0], b[1], NN, preferred_element_type=jnp.float32)
    return both[:rows] + (both[rows:] + rest)


def toeplitz(row, rows):
    wide = jnp.broadcast_to(row, (rows, row.shape[1]))
    return pltpu.roll(wide, 0, 1, stride=1, stride_axis=0)


def each(count, act):
    if count == 2:
        act(1)
    else:
        lax.fori_loop(1, count, lambda d, carry: (act(d), carry)[1], 0)


class Exchange:
    def __init__(self, axes, src, dst, send, recv):
        self.axes, self.src, self.dst, self.send, self.recv = axes, src, dst, send, recv
        self.count = int(np.prod([lax.axis_size(a) for a in axes]))

    def copy(self, d):
        here = place(self.axes)
        there = lax.rem(here + d, self.count)
        return pltpu.make_async_remote_copy(
            src_ref=self.src(there),
            dst_ref=self.dst(here),
            send_sem=self.send.at[d - 1],
            recv_sem=self.recv.at[d - 1],
            device_id=device(self.axes, there),
            device_id_type=MESH,
        )

    def start(self):
        each(self.count, lambda d: self.copy(d).start())
        return self

    def wait(self):
        each(self.count, lambda d: self.copy(d).wait())


def place(axes):
    index = lax.axis_index(axes[0])
    for a in axes[1:]:
        index = index * lax.axis_size(a) + lax.axis_index(a)
    return index


def device(axes, index):
    coordinates = {}
    for a in reversed(axes):
        coordinates[a] = lax.rem(index, lax.axis_size(a))
        index = lax.div(index, lax.axis_size(a))
    return coordinates


def greet(barrier, axes, skip=0):
    count = int(np.prod([lax.axis_size(a) for a in axes]))
    here = place(axes)

    def one(d):
        pl.semaphore_signal(
            barrier, inc=1, device_id=device(axes, lax.rem(here + d, count)), device_id_type=MESH
        )

    if skip:
        for d in range(1, count):
            if d != skip:
                one(d)
        return count - 2
    each(count, one)
    return count - 1


def times(a, b):
    if a[1] is None and b[1] is None:
        return (a[0] * b[0], None)
    if a[1] is None:
        return (a[0] * b[0], a[0] * b[1])
    if b[1] is None:
        return (a[0] * b[0], a[1] * b[0])
    return (a[0] * b[0] - a[1] * b[1], a[0] * b[1] + a[1] * b[0])


def plus(a, b):
    if a[1] is None:
        return (a[0] + b[0], b[1])
    if b[1] is None:
        return (a[0] + b[0], a[1])
    return (a[0] + b[0], a[1] + b[1])


def minus(a, b):
    return (a[0] - b[0], None if b[1] is None else a[1] - b[1])


def negative(a):
    return (-a[0], None if a[1] is None else -a[1])


def conjugate(a):
    return (a[0], None if a[1] is None else -a[1])


def product(left, right):
    out = []
    for row in left:
        line = []
        for j in range(len(right[0])):
            total = times(row[0], right[0][j])
            for k in range(1, len(row)):
                total = plus(total, times(row[k], right[k][j]))
            line.append(total)
        out.append(line)
    return out


def adjoint(block):
    return [[conjugate(block[j][i]) for j in range(len(block))] for i in range(len(block[0]))]


def hermitian_inverse(block):
    size = len(block)
    if size == 1:
        return [[(1.0 / block[0][0][0], None)]]
    if size == 2:
        a, c, d = block[0][0][0], block[0][1], block[1][1][0]
        scale = 1.0 / (a * d - (c[0] * c[0] + c[1] * c[1]))
        off = (-c[0] * scale, -c[1] * scale)
        return [[(d * scale, None), off], [conjugate(off), (a * scale, None)]]
    half = size // 2
    head = [row[:half] for row in block[:half]]
    side = [row[half:] for row in block[:half]]
    tail = [row[half:] for row in block[half:]]
    head_inverse = hermitian_inverse(head)
    lifted = product(head_inverse, side)
    drop = product(adjoint(side), lifted)
    rest = [[minus(tail[i][j], drop[i][j]) for j in range(half)] for i in range(half)]
    rest_inverse = hermitian_inverse(rest)
    corner = product(lifted, rest_inverse)
    extra = product(corner, adjoint(lifted))
    first = [[plus(head_inverse[i][j], extra[i][j]) for j in range(half)] for i in range(half)]
    right = [[negative(corner[i][j]) for j in range(half)] for i in range(half)]
    below = adjoint(right)
    return [first[i] + right[i] for i in range(half)] + [below[i] + rest_inverse[i] for i in range(half)]


def added(terms):
    while len(terms) > 1:
        terms = [sum(terms[i : i + 2][1:], terms[i]) for i in range(0, len(terms), 2)]
    return terms[0]


def eliminate(real, imag):
    height, n = real.shape
    m = PIVOTS
    lane = lax.broadcasted_iota(jnp.int32, (1, n), 1)
    lanes = lax.broadcasted_iota(jnp.int32, (height, 128), 1)
    rows = lax.broadcasted_iota(jnp.int32, (height, 128), 0)

    def wide(value):
        return None if value is None else jnp.concatenate([value] * (n // 128), axis=1)

    for k in range(0, height, m):
        col_r = [jnp.broadcast_to(real[:, k + j : k + j + 1], (height, 128)) for j in range(m)]
        col_i = [jnp.broadcast_to(imag[:, k + j : k + j + 1], (height, 128)) for j in range(m)]
        block = [
            [(col_r[j][k + i : k + i + 1], col_i[j][k + i : k + i + 1]) for j in range(m)]
            for i in range(m)
        ]
        inverse = [[(wide(q[0]), wide(q[1])) for q in row] for row in hermitian_inverse(block)]
        hit = (lane >= k) & (lane < k + m)
        old = [
            (
                jnp.where(hit, jnp.where(lane == k + i, 1.0, 0.0), real[k + i : k + i + 1]),
                jnp.where(hit, 0.0, imag[k + i : k + i + 1]),
            )
            for i in range(m)
        ]
        new = product(inverse, [[value] for value in old])
        new = [line[0] for line in new]
        inside = (rows >= k) & (rows < k + m)
        col_r = [jnp.where(inside, jnp.where(rows == k + j, -1.0, 0.0), col_r[j]) for j in range(m)]
        col_i = [jnp.where(inside, 0.0, col_i[j]) for j in range(m)]
        gone = inside | ((lanes >= k) & (lanes < k + m))
        out_r, out_i = [], []
        for t in range(n // 128):
            cut = slice(128 * t, 128 * t + 128)
            mask = gone if t == 0 else inside
            next_r = jnp.where(mask, 0.0, real[:, cut])
            next_i = jnp.where(mask, 0.0, imag[:, cut])
            terms_r, terms_i = [], []
            for j in range(m):
                row_r, row_i = new[j][0][:, cut], new[j][1][:, cut]
                terms_r.append(col_r[j] * row_r - col_i[j] * row_i)
                terms_i.append(col_r[j] * row_i + col_i[j] * row_r)
            out_r.append(next_r - added(terms_r))
            out_i.append(next_i - added(terms_i))
        real = jnp.concatenate(out_r, axis=1)
        imag = jnp.concatenate(out_i, axis=1)
    return real, imag


def thirds(x):
    high = x.astype(jnp.bfloat16)
    rest = x - high.astype(jnp.float32)
    middle = rest.astype(jnp.bfloat16)
    return high, middle, (rest - middle.astype(jnp.float32)).astype(jnp.bfloat16)


def packed(factor, top_r, top_i):
    width = 2 * PANEL
    right = jnp.concatenate(
        [jnp.concatenate([top_r, top_i], axis=1), jnp.concatenate([-top_i, top_r], axis=1)], axis=0
    )
    high, middle, low = thirds(right)
    right = jnp.concatenate([high, middle, low, high, middle, high], axis=0)
    high = factor.astype(jnp.bfloat16).astype(jnp.float32)
    rest = factor - high
    middle = rest.astype(jnp.bfloat16).astype(jnp.float32)
    low = rest - middle
    if width < 128:
        parts = [high + pltpu.roll(high, width, 1), high + pltpu.roll(middle, width, 1), middle + pltpu.roll(low, width, 1)]
    else:
        parts = [high, high, high, middle, middle, low]
    left = jnp.concatenate(parts, axis=1).astype(jnp.bfloat16)
    return lax.dot_general(left, right, NN, preferred_element_type=jnp.float32)


def beside(first, second):
    lane = lax.broadcasted_iota(jnp.int32, first.shape, 1)
    both = jnp.where(lane < PANEL, first, pltpu.roll(second, PANEL, 1))
    return jnp.where(lane < 2 * PANEL, both, 0.0)


def invert(real, imag, top, done, between):
    b = PANEL
    panels = LAGS // b

    def turn(x):
        return pltpu.roll(x, LAGS - b, 1)

    def apply(last, live):
        all_r, all_i = real[...], imag[...]
        row = lax.broadcasted_iota(jnp.int32, (LAGS, 128), 0)
        outside = (row < last * b) | (row >= last * b + b)
        if live is not None:
            outside = outside & live
        factor = jnp.where(outside, beside(all_r[:, :128], all_i[:, :128]), 0.0)
        update = packed(factor, done[0], done[1])
        column = lax.broadcasted_iota(jnp.int32, (LAGS, LAGS), 1)
        drop = column < b
        if live is not None:
            drop = drop & live
        real[...] = turn(jnp.where(drop, 0.0, all_r) - update[:, :LAGS])
        imag[...] = turn(jnp.where(drop, 0.0, all_i) - update[:, LAGS:])
        held = pl.ds(pl.multiple_of(last * b, b), b)
        real[held, :] = turn(done[0])
        imag[held, :] = turn(done[1])

    top[0] = real[:b, :]
    top[1] = imag[:b, :]
    real[...] = pltpu.roll(real[...], b, 1)
    imag[...] = pltpu.roll(imag[...], b, 1)
    done[0] = real[LAGS - b :, :]
    done[1] = imag[LAGS - b :, :]

    def panel(index, carry):
        between(index)
        apply(lax.rem(index + panels - 1, panels), index > 0)
        new_r, new_i = eliminate(top[0], top[1])
        held = pl.ds(pl.multiple_of(lax.rem(index + 1, panels) * b, b), b)
        row_r, row_i = real[held, :], imag[held, :]
        update = packed(beside(row_r[:, :128], row_i[:, :128]), new_r, new_i)
        drop = lax.broadcasted_iota(jnp.int32, (b, LAGS), 1) < b
        top[0] = turn(jnp.where(drop, 0.0, row_r) - update[:, :LAGS])
        top[1] = turn(jnp.where(drop, 0.0, row_i) - update[:, LAGS:])
        done[0] = new_r
        done[1] = new_i
        return carry

    lax.fori_loop(0, panels, panel, 0)
    apply(panels - 1, None)


def edge_matrix(tail):
    blank = jnp.zeros((1, LAGS), jnp.float32)
    edge_r = toeplitz(jnp.concatenate([blank, tail[0:1]], axis=1), LAGS)[:, :LAGS]
    edge_i = toeplitz(jnp.concatenate([blank, tail[1:2]], axis=1), LAGS)[:, :LAGS]
    one = jnp.concatenate([edge_r, edge_i], axis=1)
    two = jnp.concatenate([edge_i, -edge_r], axis=1)
    return dot(one, one, NT), dot(one, two, NT)


def normal_matrix(column, edge_r, edge_i, loading):
    i0 = lax.broadcasted_iota(jnp.int32, (LAGS, LAGS), 0)
    i1 = lax.broadcasted_iota(jnp.int32, (LAGS, LAGS), 1)
    flip = jnp.where(i0 + i1 == LAGS - 1, 1.0, 0.0)
    behind = pltpu.roll(dot(column, flip), 1, 1)
    lane = lax.broadcasted_iota(jnp.int32, behind.shape, 1)
    behind = jnp.where(lane == 0, 0.0, behind)
    base_r = toeplitz(jnp.concatenate([column[0:1], behind[0:1]], axis=1), LAGS)[:, :LAGS]
    base_i = toeplitz(jnp.concatenate([-column[1:2], behind[1:2]], axis=1), LAGS)[:, :LAGS]
    diagonal = i0 == i1
    off = jnp.sum(jnp.sum(jnp.where(diagonal, edge_r, 0.0), axis=0, keepdims=True), axis=1, keepdims=True)
    lam = loading * (column[0:1, 0:1] - off / LAGS)
    real = base_r - edge_r
    return jnp.where(diagonal, real + lam, real), base_i - edge_i


PAIR, FAR, NEAR = TM[2:], TM[:2], (TM[2], "chan")
ALONG_Y, ALONG_Z = TM[:1], TM[1:2]


def cancel_kernel(
    loading, reference, surveillance, weights, cells, energies,
    table, halo, tail, mine, gram_pair, gram_all, real, imag, top, done,
    pair, ring_y, ring_z, cross, residual, corr, landed, turned, power, power_z, power_y,
    edge_sem, tail_send, tail_recv, gram_sem, gram_send, gram_recv,
    pair_sem, y_send, y_recv, z_send, z_recv, out_sem,
    far_send, far_recv, near_send, near_recv, pz_send, pz_recv, py_send, py_recv, pa_send, pa_recv,
):
    length = reference.shape[1]
    width = surveillance.shape[1]
    count = lax.axis_size(TM)
    here = place(TM)
    core, y, z, far, near = place(PAIR), place(ALONG_Y), place(ALONG_Z), place(FAR), place(NEAR)
    barrier = pltpu.get_barrier_semaphore()
    total = greet(barrier, TM)
    total += greet(barrier, NEAR, 4)

    def fill(tile, windows):
        delayed = [toeplitz(x, 128)[:, 128:] for x in windows]
        at = pl.ds(pl.multiple_of(128 * tile, 128), 128)
        for part in range(2):
            high, low = halves(delayed[part])
            table[part, 0, :, at] = high
            table[part, 1, :, at] = low
        return delayed

    def lagged(delayed, start):
        now = reference[:, pl.ds(pl.multiple_of(start, 128), 128)]
        now_r, now_i = now[0:1], now[1:2]
        return (delayed[0] * now_r + delayed[1] * now_i, delayed[0] * now_i - delayed[1] * now_r)

    def plus_all(sums, terms):
        return tuple(x + y for x, y in zip(sums, terms))

    tiles = (LAGS + length) // 128

    def fill_inner(tile, sums):
        start = pl.multiple_of(128 * tile - 384, 128)
        window = reference[:, pl.ds(start, LAGS)]
        delayed = fill(tile, [window[0:1], window[1:2]])
        return (
            plus_all(sums[0], lagged(delayed, 128 * tile - 256)),
            plus_all(sums[1], lagged(delayed, 128 * tile - 128)),
        )

    blank = (jnp.zeros((128, 128), jnp.float32),) * 2
    sums = lax.fori_loop(3, tiles - 1, fill_inner, (blank, blank))
    window = reference[:, length - LAGS :]
    delayed = fill(tiles - 1, [window[0:1], window[1:2]])
    sums = [plus_all(sums[0], lagged(delayed, length - 128)), sums[1]]

    pl.semaphore_wait(barrier, total)
    forward = pltpu.make_async_remote_copy(
        src_ref=reference.at[:, pl.ds(length - LAGS, LAGS)],
        dst_ref=halo,
        send_sem=edge_sem.at[0],
        recv_sem=edge_sem.at[1],
        device_id=device(TM, lax.rem(here + 1, count)),
        device_id_type=MESH,
    )
    forward.start()

    def tail_copy(d):
        return pltpu.make_async_remote_copy(
            src_ref=reference.at[:, pl.ds(length - LAGS, LAGS)],
            dst_ref=tail,
            send_sem=tail_send.at[d - 1],
            recv_sem=tail_recv.at[0],
            device_id=device(TM, lax.rem(here + d, count)),
            device_id_type=MESH,
        )

    @pl.when(here == count - 1)
    def _():
        tail[...] = reference[:, length - LAGS :]
        each(count, lambda d: tail_copy(d).start())

    forward.wait()
    before = jnp.where(here > 0, halo[...], 0.0)
    delayed = fill(1, [before[0:1], before[1:2]])
    sums[1] = plus_all(sums[1], lagged(delayed, 0))
    joint = jnp.concatenate([before[:, 128:], reference[:, :128]], axis=1)
    delayed = fill(2, [joint[0:1], joint[1:2]])
    sums[0] = plus_all(sums[0], lagged(delayed, 0))
    sums[1] = plus_all(sums[1], lagged(delayed, 128))
    for half in range(2):
        for part in range(2):
            line = jnp.sum(sums[half][part].T, axis=0, keepdims=True)
            gram_pair[0, 2 * part + half : 2 * part + half + 1, :] = line
    Exchange(PAIR, lambda p: gram_pair.at[0], lambda p: gram_pair.at[1], gram_sem.at[0:1], gram_sem.at[1:2]).start().wait()
    gram_all[far] = gram_pair[0] + gram_pair[1]
    to_gram = Exchange(FAR, lambda p: gram_all.at[far], lambda p: gram_all.at[p], gram_send, gram_recv).start()

    segments = length // SEG_LEN

    def taps_of(segment):
        taps = []
        for half in range(2):
            at = pl.ds(pl.multiple_of(segment * SEG_LEN + 256 - 128 * half, 128), SEG_LEN)
            taps.append([[table[part, piece, :, at] for piece in range(2)] for part in range(2)])
        return taps

    def signal_of(segment):
        at = pl.ds(pl.multiple_of(segment * SEG_LEN, 128), SEG_LEN)
        return surveillance[0, :, at], surveillance[1, :, at]

    def cross_terms(segment, total):
        s_re, s_im = signal_of(segment)
        zero = jnp.zeros((128 - 2 * width, SEG_LEN), jnp.float32)
        with_re = halves(jnp.concatenate([s_re, s_im, zero], axis=0))
        with_im = halves(jnp.concatenate([s_im, -s_re, zero], axis=0))
        return tuple(
            x + (dot_beside(taps[0], with_re) + dot_beside(taps[1], with_im))
            for x, taps in zip(total, taps_of(segment))
        )

    product = lax.fori_loop(0, segments, cross_terms, blank, unroll=UNROLL)
    for half in range(2):
        mine[half] = product[half].T[: 2 * width]
    to_pair = Exchange(PAIR, lambda p: mine.at[p], lambda p: pair, pair_sem.at[0:1], pair_sem.at[1:2]).start()

    @pl.when(here == count - 1)
    def _():
        each(count, lambda d: tail_copy(d).wait_send())

    @pl.when(here != count - 1)
    def _():
        tail_copy(1).wait_recv()

    edge_r, edge_i = edge_matrix(tail[...])
    real[...] = edge_r
    imag[...] = edge_i
    to_gram.wait()
    gram = jnp.sum(gram_all[...], axis=0)
    column = jnp.concatenate([gram[0:1], gram[1:2]], axis=1)
    column = jnp.concatenate([column, jnp.concatenate([gram[2:3], gram[3:4]], axis=1)], axis=0)
    column = jnp.concatenate([column, jnp.zeros((6, LAGS), jnp.float32)], axis=0)
    start_r, start_i = normal_matrix(column, real[...], imag[...], loading[0])
    real[...] = start_r
    imag[...] = start_i

    along_y = Exchange(ALONG_Y, lambda p: ring_y.at[y], lambda p: ring_y.at[p], y_send, y_recv)
    along_z = Exchange(ALONG_Z, lambda p: ring_z.at[z], lambda p: ring_z.at[p], z_send, z_recv)
    out = Exchange(PAIR, lambda p: cross.at[core], lambda p: cross.at[p], out_sem.at[0:1], out_sem.at[1:2])

    def between(index):
        @pl.when(index == 1)
        def _():
            to_pair.wait()
            ring_y[y] = mine[core] + pair[...]
            along_y.start()

        @pl.when(index == 3)
        def _():
            along_y.wait()
            ring_z[z] = (ring_y[0] + ring_y[1]) + (ring_y[2] + ring_y[3])
            along_z.start()

        @pl.when(index == 6)
        def _():
            along_z.wait()
            cross[core] = ((ring_z[0] + ring_z[1]) + (ring_z[2] + ring_z[3])) + (
                (ring_z[4] + ring_z[5]) + (ring_z[6] + ring_z[7])
            )
            out.start()

    invert(real, imag, top, done, between)
    out.wait()
    right = jnp.concatenate([cross[0], cross[1]], axis=1)
    spun = jnp.concatenate([-right[width:], right[:width]], axis=0)
    w = dot(right, real[...], NT) + dot(spun, imag[...], NT)
    weights[...] = w

    w_re, w_im = w[:width], w[width:]
    on_re = halves(w)
    on_im = halves(jnp.concatenate([-w_im, w_re], axis=0))
    own_row = lax.broadcasted_iota(jnp.int32, (128, SEG_LEN), 0) // (2 * width)

    def cancelled(segment, energy):
        taps = taps_of(segment)
        joined = [
            [jnp.concatenate([taps[0][part][piece], taps[1][part][piece]], axis=0) for piece in range(2)]
            for part in range(2)
        ]
        clutter = dot_stacked(on_re, joined[0]) + dot_stacked(on_im, joined[1])
        rest = jnp.concatenate(signal_of(segment), axis=0) - clutter
        residual[segment] = rest
        square = rest * rest
        for tile in range(SEG_LEN // 128):
            energy = energy + square[:, 128 * tile : 128 * tile + 128]
        return energy

    energy = lax.fori_loop(0, segments, cancelled, jnp.zeros((2 * width, 128), jnp.float32), unroll=UNROLL)
    energy = jnp.sum(energy, axis=1, keepdims=True)
    energy = jnp.broadcast_to(energy[:width] + energy[width:], (width, 128))
    energy = jnp.concatenate([energy, jnp.zeros((128 - width, 128), jnp.float32)], axis=0)
    power_z[z] = energy.T[:8]
    to_z = Exchange(ALONG_Z, lambda p: power_z.at[z], lambda p: power_z.at[p], pz_send, pz_recv).start()

    to_far = Exchange(FAR, lambda p: corr.at[p], lambda p: landed.at[p], far_send, far_recv)
    for half in range(2):

        def correlate(segment, total):
            at = pl.ds(pl.multiple_of(segment * SEG_LEN + 256 - 128 * half, 128), SEG_LEN)
            rest = residual[segment]
            swapped = jnp.concatenate([rest[width:], -rest[:width]], axis=0)
            own = own_row == segment
            with_re = halves(jnp.where(own, jnp.concatenate([rest] * segments, axis=0), 0.0))
            with_im = halves(jnp.where(own, jnp.concatenate([swapped] * segments, axis=0), 0.0))
            real_taps = [table[0, piece, :, at] for piece in range(2)]
            imag_taps = [table[1, piece, :, at] for piece in range(2)]
            return total + (dot_beside(real_taps, with_re) + dot_beside(imag_taps, with_im))

        total = lax.fori_loop(0, segments, correlate, blank[0], unroll=UNROLL)
        corr[16 * half : 16 * half + 16] = total.reshape(16, 8, 128)

        def send(p, carry):
            @pl.when(p != far)
            def _():
                to_far.copy(lax.rem(p - far + 32, 32)).start()

            return carry

        lax.fori_loop(16 * half, 16 * half + 16, send, 0)
    landed[far] = corr[far]
    to_z.wait()
    parts = [power_z[i] for i in range(8)]
    power_y[y] = ((parts[0] + parts[1]) + (parts[2] + parts[3])) + ((parts[4] + parts[5]) + (parts[6] + parts[7]))
    to_y = Exchange(ALONG_Y, lambda p: power_y.at[y], lambda p: power_y.at[p], py_send, py_recv).start()
    to_far.wait()
    everything = landed[...]
    for lag in range(8):
        turned[lag] = everything[:, lag, :]
    to_near = Exchange(NEAR, lambda p: turned.at[p], lambda p: cells.at[p], near_send, near_recv).start()
    cells[near] = turned[near]
    to_y.wait()
    power[...] = (power_y[0] + power_y[1]) + (power_y[2] + power_y[3])
    energies[near] = power[...]
    Exchange(NEAR, lambda p: power, lambda p: energies.at[p], pa_send, pa_recv).start().wait()
    to_near.wait()


def cancel(loading, reference, surveillance):
    vmem = pl.BlockSpec(memory_space=pltpu.VMEM)
    length = reference.shape[1]
    width = surveillance.shape[1]
    dma = pltpu.SemaphoreType.DMA

    def block(*shape):
        return pltpu.VMEM(shape, jnp.float32)

    half = (2 * width, 128)
    return pl.pallas_call(
        cancel_kernel,
        out_shape=[
            jax.ShapeDtypeStruct((2 * width, LAGS), jnp.float32),
            jax.ShapeDtypeStruct((8, 32, 128), jnp.float32),
            jax.ShapeDtypeStruct((8, 8, 128), jnp.float32),
        ],
        in_specs=[pl.BlockSpec(memory_space=pltpu.SMEM), vmem, vmem],
        out_specs=[vmem] * 3,
        scratch_shapes=[
            pltpu.VMEM((2, 2, 128, LAGS + length), jnp.bfloat16),
            block(2, LAGS), block(2, LAGS), block(2, *half), block(2, 4, 128), block(32, 4, 128),
            block(LAGS, LAGS), block(LAGS, LAGS), block(2, PANEL, LAGS), block(2, PANEL, LAGS),
            block(*half), block(4, *half), block(8, *half), block(2, *half), block(4, 2 * width, SEG_LEN),
            block(32, 8, 128), block(32, 8, 128), block(8, 32, 128), block(8, 128), block(8, 8, 128), block(4, 8, 128),
            dma((2,)), dma((63,)), dma((1,)), dma((2,)), dma((31,)), dma((31,)),
            dma((2,)), dma((3,)), dma((3,)), dma((7,)), dma((7,)), dma((2,)),
            dma((31,)), dma((31,)), dma((7,)), dma((7,)), dma((7,)), dma((7,)), dma((3,)), dma((3,)), dma((7,)), dma((7,)),
        ],
        compiler_params=pltpu.CompilerParams(collective_id=0, has_side_effects=True, vmem_limit_bytes=24 * 2**20),
        name="cancel",
    )(loading, reference, surveillance)


def doppler_tables(shards, segments):
    short = DOPP // segments
    order = np.arange(shards).reshape(-1, 2).T.reshape(-1)
    angle = 2.0 * np.pi / short * (np.outer(order, np.arange(short)) % short)
    table = np.concatenate([np.cos(angle), np.sin(angle)], axis=1)
    turn = 2.0 * np.pi / DOPP * np.outer(np.arange(segments), np.arange(DOPP))
    turns = np.stack([np.cos(turn), np.sin(turn)])
    return table.astype(np.float32), turns.astype(np.float32)


def doppler_kernel(samples, weights, cells, energies, table, turns, out, kept):
    near, _, lanes = cells.shape
    groups = near // 2
    segments = turns.shape[1]
    width = lanes // segments // 2
    basis = halves(table[...])
    short = DOPP // segments
    def group(g, carry):
        power = (energies[g] + energies[groups + g]) / samples
        scale = lax.rsqrt(samples * (power + EPSILON))
        by = jnp.broadcast_to(scale[0:1], (128, 128)).T[:width, 0:1]
        rows = jnp.concatenate([cells[g], cells[groups + g]], axis=0)
        wave = dot3(halves(rows.T), basis)
        total_r = total_i = None
        for s in range(segments):
            base = 2 * width * s
            a_r, a_i = wave[base : base + width, :short], wave[base : base + width, short:]
            b_r, b_i = (
                wave[base + width : base + 2 * width, :short],
                wave[base + width : base + 2 * width, short:],
            )
            y_r = (a_r + b_i) * by
            y_i = (b_r - a_i) * by
            y_r = jnp.concatenate([y_r] * segments, axis=1)
            y_i = jnp.concatenate([y_i] * segments, axis=1)
            if s == 0:
                total_r, total_i = y_r, y_i
                continue
            c, d = turns[0, s : s + 1, :], turns[1, s : s + 1, :]
            total_r = total_r + (y_r * c + y_i * d)
            total_i = total_i + (y_i * c - y_r * d)
        at = pl.ds(width * g, width)
        out[0, 0, at, :] = total_r
        out[0, 1, at, :] = total_i
        return carry

    for g in range(groups):
        group(g, 0)
    kept[...] = weights[...]


def doppler(weights, cells, energies, segments, samples):
    vmem = pl.BlockSpec(memory_space=pltpu.VMEM)
    shards = 2 * cells.shape[1]
    table, turns = doppler_tables(shards, segments)
    width = cells.shape[2] // segments // 2
    groups = cells.shape[0] // 2
    return pl.pallas_call(
        functools.partial(doppler_kernel, samples),
        out_shape=[
            jax.ShapeDtypeStruct((1, 2, width * groups, DOPP), jnp.float32),
            jax.ShapeDtypeStruct(weights.shape, jnp.float32),
        ],
        in_specs=[vmem] * 5,
        out_specs=[vmem, vmem],
        compiler_params=pltpu.CompilerParams(vmem_limit_bytes=24 * 2**20),
        name="doppler",
    )(weights, cells, energies, jnp.asarray(table), jnp.asarray(turns))


def per_device(reference_signal, surveillance, loading):
    length = reference_signal.shape[1]
    samples = float(length * lax.axis_size(TM))
    weights, cells, energies = cancel(loading, reference_signal, surveillance)
    full, weights = doppler(weights, cells, energies, length // SEG_LEN, samples)
    return full, jnp.swapaxes(weights.reshape(2, -1, LAGS), 1, 2)


def solution(mesh):
    split = Mesh(
        mesh.devices.reshape(4, 8, 2, mesh.shape["chan"]), ("tm_0", "tm_1", "tm_2", "chan")
    )
    in_specs = (P(None, TM), P(None, "chan", TM), P())
    out_specs = (P(TM_CHAN, None, None, None), P(None, None, "chan"))
    return jax.shard_map(
        per_device, mesh=split, in_specs=in_specs, out_specs=out_specs, check_vma=False
    )
```

```python
import functools

import jax
import jax.numpy as jnp
import numpy as np
from jax import lax
from jax.experimental import pallas as pl
from jax.experimental.pallas import tpu as pltpu
from jax.sharding import Mesh
from jax.sharding import PartitionSpec as P

LAGS = 256
DOPP = 1024
SEG_LEN = 512
TM = ("tm_0", "tm_1", "tm_2")
TM_CHAN = ("tm_0", "tm_1", "tm_2", "chan")
EPSILON = 1e-06
PANEL = 32
UNROLL = 2
PIVOTS = 4
ROWS = 40
MESH = pl.DeviceIdType.MESH

highest = lax.Precision.HIGHEST
NN = (((1,), (0,)), ((), ()))
NT = (((1,), (1,)), ((), ()))


def dot(a, b, dims=NN):
    return lax.dot_general(a, b, dims, precision=highest, preferred_element_type=jnp.float32)


def halves(x):
    high = x.astype(jnp.bfloat16)
    return high, (x - high.astype(jnp.float32)).astype(jnp.bfloat16)


def dot3(a, b, dims=NN):
    def one(x, y):
        return lax.dot_general(x, y, dims, preferred_element_type=jnp.float32)

    return one(a[0], b[0]) + (one(a[0], b[1]) + one(a[1], b[0]))


def dot_beside(a, b):
    both = lax.dot_general(a[0], jnp.concatenate(b, axis=0), NT, preferred_element_type=jnp.float32)
    rest = lax.dot_general(a[1], b[0], NT, preferred_element_type=jnp.float32)
    return both[:, :128] + (both[:, 128:] + rest)


def dot_stacked(a, b):
    rows = a[0].shape[0]
    both = lax.dot_general(jnp.concatenate(a, axis=0), b[0], NN, preferred_element_type=jnp.float32)
    rest = lax.dot_general(a[0], b[1], NN, preferred_element_type=jnp.float32)
    return both[:rows] + (both[rows:] + rest)


def toeplitz(row, rows):
    wide = jnp.broadcast_to(row, (rows, row.shape[1]))
    return pltpu.roll(wide, 0, 1, stride=1, stride_axis=0)


def each(count, act):
    if count == 2:
        act(1)
    else:
        lax.fori_loop(1, count, lambda d, carry: (act(d), carry)[1], 0)


class Exchange:
    def __init__(self, axes, src, dst, send, recv):
        self.axes, self.src, self.dst, self.send, self.recv = axes, src, dst, send, recv
        self.count = int(np.prod([lax.axis_size(a) for a in axes]))

    def copy(self, d):
        here = place(self.axes)
        there = lax.rem(here + d, self.count)
        return pltpu.make_async_remote_copy(
            src_ref=self.src(there),
            dst_ref=self.dst(here),
            send_sem=self.send.at[d - 1],
            recv_sem=self.recv.at[d - 1],
            device_id=device(self.axes, there),
            device_id_type=MESH,
        )

    def start(self):
        each(self.count, lambda d: self.copy(d).start())
        return self

    def wait(self):
        each(self.count, lambda d: self.copy(d).wait())


def place(axes):
    index = lax.axis_index(axes[0])
    for a in axes[1:]:
        index = index * lax.axis_size(a) + lax.axis_index(a)
    return index


def device(axes, index):
    coordinates = {}
    for a in reversed(axes):
        coordinates[a] = lax.rem(index, lax.axis_size(a))
        index = lax.div(index, lax.axis_size(a))
    return coordinates


def greet(barrier, axes, skip=0):
    count = int(np.prod([lax.axis_size(a) for a in axes]))
    here = place(axes)

    def one(d):
        pl.semaphore_signal(
            barrier, inc=1, device_id=device(axes, lax.rem(here + d, count)), device_id_type=MESH
        )

    if skip:
        for d in range(1, count):
            if d != skip:
                one(d)
        return count - 2
    each(count, one)
    return count - 1


def times(a, b):
    if a[1] is None and b[1] is None:
        return (a[0] * b[0], None)
    if a[1] is None:
        return (a[0] * b[0], a[0] * b[1])
    if b[1] is None:
        return (a[0] * b[0], a[1] * b[0])
    return (a[0] * b[0] - a[1] * b[1], a[0] * b[1] + a[1] * b[0])


def plus(a, b):
    if a[1] is None:
        return (a[0] + b[0], b[1])
    if b[1] is None:
        return (a[0] + b[0], a[1])
    return (a[0] + b[0], a[1] + b[1])


def minus(a, b):
    return (a[0] - b[0], None if b[1] is None else a[1] - b[1])


def negative(a):
    return (-a[0], None if a[1] is None else -a[1])


def conjugate(a):
    return (a[0], None if a[1] is None else -a[1])


def product(left, right):
    out = []
    for row in left:
        line = []
        for j in range(len(right[0])):
            total = times(row[0], right[0][j])
            for k in range(1, len(row)):
                total = plus(total, times(row[k], right[k][j]))
            line.append(total)
        out.append(line)
    return out


def adjoint(block):
    return [[conjugate(block[j][i]) for j in range(len(block))] for i in range(len(block[0]))]


def hermitian_inverse(block):
    size = len(block)
    if size == 1:
        return [[(1.0 / block[0][0][0], None)]]
    if size == 2:
        a, c, d = block[0][0][0], block[0][1], block[1][1][0]
        scale = 1.0 / (a * d - (c[0] * c[0] + c[1] * c[1]))
        off = (-c[0] * scale, -c[1] * scale)
        return [[(d * scale, None), off], [conjugate(off), (a * scale, None)]]
    half = size // 2
    head = [row[:half] for row in block[:half]]
    side = [row[half:] for row in block[:half]]
    tail = [row[half:] for row in block[half:]]
    head_inverse = hermitian_inverse(head)
    lifted = product(head_inverse, side)
    drop = product(adjoint(side), lifted)
    rest = [[minus(tail[i][j], drop[i][j]) for j in range(half)] for i in range(half)]
    rest_inverse = hermitian_inverse(rest)
    corner = product(lifted, rest_inverse)
    extra = product(corner, adjoint(lifted))
    first = [[plus(head_inverse[i][j], extra[i][j]) for j in range(half)] for i in range(half)]
    right = [[negative(corner[i][j]) for j in range(half)] for i in range(half)]
    below = adjoint(right)
    return [first[i] + right[i] for i in range(half)] + [below[i] + rest_inverse[i] for i in range(half)]


def added(terms):
    while len(terms) > 1:
        terms = [sum(terms[i : i + 2][1:], terms[i]) for i in range(0, len(terms), 2)]
    return terms[0]


def eliminate(real, imag):
    height, n = real.shape
    m = PIVOTS
    lane = lax.broadcasted_iota(jnp.int32, (1, n), 1)
    lanes = lax.broadcasted_iota(jnp.int32, (height, 128), 1)
    rows = lax.broadcasted_iota(jnp.int32, (height, 128), 0)

    def wide(value):
        return None if value is None else jnp.concatenate([value] * (n // 128), axis=1)

    for k in range(0, height, m):
        col_r = [jnp.broadcast_to(real[:, k + j : k + j + 1], (height, 128)) for j in range(m)]
        col_i = [jnp.broadcast_to(imag[:, k + j : k + j + 1], (height, 128)) for j in range(m)]
        block = [
            [(col_r[j][k + i : k + i + 1], col_i[j][k + i : k + i + 1]) for j in range(m)]
            for i in range(m)
        ]
        inverse = [[(wide(q[0]), wide(q[1])) for q in row] for row in hermitian_inverse(block)]
        hit = (lane >= k) & (lane < k + m)
        old = [
            (
                jnp.where(hit, jnp.where(lane == k + i, 1.0, 0.0), real[k + i : k + i + 1]),
                jnp.where(hit, 0.0, imag[k + i : k + i + 1]),
            )
            for i in range(m)
        ]
        new = product(inverse, [[value] for value in old])
        new = [line[0] for line in new]
        inside = (rows >= k) & (rows < k + m)
        col_r = [jnp.where(inside, jnp.where(rows == k + j, -1.0, 0.0), col_r[j]) for j in range(m)]
        col_i = [jnp.where(inside, 0.0, col_i[j]) for j in range(m)]
        gone = inside | ((lanes >= k) & (lanes < k + m))
        out_r, out_i = [], []
        for t in range(n // 128):
            cut = slice(128 * t, 128 * t + 128)
            mask = gone if t == 0 else inside
            next_r = jnp.where(mask, 0.0, real[:, cut])
            next_i = jnp.where(mask, 0.0, imag[:, cut])
            terms_r, terms_i = [], []
            for j in range(m):
                row_r, row_i = new[j][0][:, cut], new[j][1][:, cut]
                terms_r.append(col_r[j] * row_r - col_i[j] * row_i)
                terms_i.append(col_r[j] * row_i + col_i[j] * row_r)
            out_r.append(next_r - added(terms_r))
            out_i.append(next_i - added(terms_i))
        real = jnp.concatenate(out_r, axis=1)
        imag = jnp.concatenate(out_i, axis=1)
    return real, imag


def thirds(x):
    high = x.astype(jnp.bfloat16)
    rest = x - high.astype(jnp.float32)
    middle = rest.astype(jnp.bfloat16)
    return high, middle, (rest - middle.astype(jnp.float32)).astype(jnp.bfloat16)


def packed(factor, top_r, top_i):
    width = 2 * PANEL
    right = jnp.concatenate(
        [jnp.concatenate([top_r, top_i], axis=1), jnp.concatenate([-top_i, top_r], axis=1)], axis=0
    )
    high, middle, low = thirds(right)
    right = jnp.concatenate([high, middle, low, high, middle, high], axis=0)
    high = factor.astype(jnp.bfloat16).astype(jnp.float32)
    rest = factor - high
    middle = rest.astype(jnp.bfloat16).astype(jnp.float32)
    low = rest - middle
    if width < 128:
        parts = [high + pltpu.roll(high, width, 1), high + pltpu.roll(middle, width, 1), middle + pltpu.roll(low, width, 1)]
    else:
        parts = [high, high, high, middle, middle, low]
    left = jnp.concatenate(parts, axis=1).astype(jnp.bfloat16)
    return lax.dot_general(left, right, NN, preferred_element_type=jnp.float32)


def beside(first, second):
    lane = lax.broadcasted_iota(jnp.int32, first.shape, 1)
    both = jnp.where(lane < PANEL, first, pltpu.roll(second, PANEL, 1))
    return jnp.where(lane < 2 * PANEL, both, 0.0)


def invert(real, imag, top, done, between):
    b = PANEL
    panels = LAGS // b

    def turn(x):
        return pltpu.roll(x, LAGS - b, 1)

    def apply(last, live):
        all_r, all_i = real[...], imag[...]
        row = lax.broadcasted_iota(jnp.int32, (LAGS, 128), 0)
        outside = (row < last * b) | (row >= last * b + b)
        if live is not None:
            outside = outside & live
        factor = jnp.where(outside, beside(all_r[:, :128], all_i[:, :128]), 0.0)
        update = packed(factor, done[0], done[1])
        column = lax.broadcasted_iota(jnp.int32, (LAGS, LAGS), 1)
        drop = column < b
        if live is not None:
            drop = drop & live
        real[...] = turn(jnp.where(drop, 0.0, all_r) - update[:, :LAGS])
        imag[...] = turn(jnp.where(drop, 0.0, all_i) - update[:, LAGS:])
        held = pl.ds(pl.multiple_of(last * b, b), b)
        real[held, :] = turn(done[0])
        imag[held, :] = turn(done[1])

    top[0] = real[:b, :]
    top[1] = imag[:b, :]
    real[...] = pltpu.roll(real[...], b, 1)
    imag[...] = pltpu.roll(imag[...], b, 1)
    done[0] = real[LAGS - b :, :]
    done[1] = imag[LAGS - b :, :]

    def panel(index, carry):
        between(index)
        apply(lax.rem(index + panels - 1, panels), index > 0)
        new_r, new_i = eliminate(top[0], top[1])
        held = pl.ds(pl.multiple_of(lax.rem(index + 1, panels) * b, b), b)
        row_r, row_i = real[held, :], imag[held, :]
        update = packed(beside(row_r[:, :128], row_i[:, :128]), new_r, new_i)
        drop = lax.broadcasted_iota(jnp.int32, (b, LAGS), 1) < b
        top[0] = turn(jnp.where(drop, 0.0, row_r) - update[:, :LAGS])
        top[1] = turn(jnp.where(drop, 0.0, row_i) - update[:, LAGS:])
        done[0] = new_r
        done[1] = new_i
        return carry

    lax.fori_loop(0, panels, panel, 0)
    apply(panels - 1, None)


def edge_matrix(tail):
    blank = jnp.zeros((1, LAGS), jnp.float32)
    edge_r = toeplitz(jnp.concatenate([blank, tail[0:1]], axis=1), LAGS)[:, :LAGS]
    edge_i = toeplitz(jnp.concatenate([blank, tail[1:2]], axis=1), LAGS)[:, :LAGS]
    one = jnp.concatenate([edge_r, edge_i], axis=1)
    two = jnp.concatenate([edge_i, -edge_r], axis=1)
    return dot(one, one, NT), dot(one, two, NT)


def normal_matrix(column, edge_r, edge_i, loading):
    i0 = lax.broadcasted_iota(jnp.int32, (LAGS, LAGS), 0)
    i1 = lax.broadcasted_iota(jnp.int32, (LAGS, LAGS), 1)
    flip = jnp.where(i0 + i1 == LAGS - 1, 1.0, 0.0)
    behind = pltpu.roll(dot(column, flip), 1, 1)
    lane = lax.broadcasted_iota(jnp.int32, behind.shape, 1)
    behind = jnp.where(lane == 0, 0.0, behind)
    base_r = toeplitz(jnp.concatenate([column[0:1], behind[0:1]], axis=1), LAGS)[:, :LAGS]
    base_i = toeplitz(jnp.concatenate([-column[1:2], behind[1:2]], axis=1), LAGS)[:, :LAGS]
    diagonal = i0 == i1
    off = jnp.sum(jnp.sum(jnp.where(diagonal, edge_r, 0.0), axis=0, keepdims=True), axis=1, keepdims=True)
    lam = loading * (column[0:1, 0:1] - off / LAGS)
    real = base_r - edge_r
    return jnp.where(diagonal, real + lam, real), base_i - edge_i


PAIR, FAR, NEAR = TM[2:], TM[:2], (TM[2], "chan")
ALONG_Y, ALONG_Z = TM[:1], TM[1:2]


def cancel_kernel(
    loading, reference_hbm, surveillance_hbm, weights, cells, energies,
    reference, surveillance, fetch_sem, table, halo, tail, mine, gram_pair, gram_all, real, imag, top, done,
    pair, ring_y, ring_z, cross, residual, corr, landed, turned, power, power_z, power_y,
    edge_sem, tail_send, tail_recv, gram_sem, gram_send, gram_recv,
    pair_sem, y_send, y_recv, z_send, z_recv, out_sem,
    far_send, far_recv, near_send, near_recv, pz_send, pz_recv, py_send, py_recv, pa_send, pa_recv,
):
    length = reference.shape[1]
    width = surveillance.shape[1]
    count = lax.axis_size(TM)
    here = place(TM)
    core, y, z, far, near = place(PAIR), place(ALONG_Y), place(ALONG_Z), place(FAR), place(NEAR)
    fetch_r = pltpu.make_async_copy(reference_hbm, reference, fetch_sem.at[0])
    fetch_r.start()
    fetch_s = pltpu.make_async_copy(surveillance_hbm, surveillance, fetch_sem.at[1])
    fetch_s.start()
    barrier = pltpu.get_barrier_semaphore()
    total = greet(barrier, TM)
    total += greet(barrier, NEAR, 4)
    fetch_r.wait()

    def fill(tile, windows):
        delayed = [toeplitz(x, 128)[:, 128:] for x in windows]
        at = pl.ds(pl.multiple_of(128 * tile, 128), 128)
        for part in range(2):
            high, low = halves(delayed[part])
            table[part, 0, :, at] = high
            table[part, 1, :, at] = low
        return delayed

    def lagged(delayed, start):
        now = reference[:, pl.ds(pl.multiple_of(start, 128), 128)]
        now_r, now_i = now[0:1], now[1:2]
        return (delayed[0] * now_r + delayed[1] * now_i, delayed[0] * now_i - delayed[1] * now_r)

    def plus_all(sums, terms):
        return tuple(x + y for x, y in zip(sums, terms))

    tiles = (LAGS + length) // 128

    def fill_inner(tile, sums):
        start = pl.multiple_of(128 * tile - 384, 128)
        window = reference[:, pl.ds(start, LAGS)]
        delayed = fill(tile, [window[0:1], window[1:2]])
        return (
            plus_all(sums[0], lagged(delayed, 128 * tile - 256)),
            plus_all(sums[1], lagged(delayed, 128 * tile - 128)),
        )

    blank = (jnp.zeros((128, 128), jnp.float32),) * 2
    sums = lax.fori_loop(3, tiles - 1, fill_inner, (blank, blank))
    window = reference[:, length - LAGS :]
    delayed = fill(tiles - 1, [window[0:1], window[1:2]])
    sums = [plus_all(sums[0], lagged(delayed, length - 128)), sums[1]]

    pl.semaphore_wait(barrier, total)
    forward = pltpu.make_async_remote_copy(
        src_ref=reference.at[:, pl.ds(length - LAGS, LAGS)],
        dst_ref=halo,
        send_sem=edge_sem.at[0],
        recv_sem=edge_sem.at[1],
        device_id=device(TM, lax.rem(here + 1, count)),
        device_id_type=MESH,
    )
    forward.start()

    def tail_copy(d):
        return pltpu.make_async_remote_copy(
            src_ref=reference.at[:, pl.ds(length - LAGS, LAGS)],
            dst_ref=tail,
            send_sem=tail_send.at[d - 1],
            recv_sem=tail_recv.at[0],
            device_id=device(TM, lax.rem(here + d, count)),
            device_id_type=MESH,
        )

    @pl.when(here == count - 1)
    def _():
        tail[...] = reference[:, length - LAGS :]
        each(count, lambda d: tail_copy(d).start())

    forward.wait()
    before = jnp.where(here > 0, halo[...], 0.0)
    delayed = fill(1, [before[0:1], before[1:2]])
    sums[1] = plus_all(sums[1], lagged(delayed, 0))
    joint = jnp.concatenate([before[:, 128:], reference[:, :128]], axis=1)
    delayed = fill(2, [joint[0:1], joint[1:2]])
    sums[0] = plus_all(sums[0], lagged(delayed, 0))
    sums[1] = plus_all(sums[1], lagged(delayed, 128))
    for half in range(2):
        for part in range(2):
            line = jnp.sum(sums[half][part].T, axis=0, keepdims=True)
            gram_pair[0, 2 * part + half : 2 * part + half + 1, :] = line
    Exchange(PAIR, lambda p: gram_pair.at[0], lambda p: gram_pair.at[1], gram_sem.at[0:1], gram_sem.at[1:2]).start().wait()
    gram_all[far] = gram_pair[0] + gram_pair[1]
    to_gram = Exchange(FAR, lambda p: gram_all.at[far], lambda p: gram_all.at[p], gram_send, gram_recv).start()

    fetch_s.wait()
    segments = length // SEG_LEN

    def taps_of(segment):
        taps = []
        for half in range(2):
            at = pl.ds(pl.multiple_of(segment * SEG_LEN + 256 - 128 * half, 128), SEG_LEN)
            taps.append([[table[part, piece, :, at] for piece in range(2)] for part in range(2)])
        return taps

    def signal_of(segment):
        at = pl.ds(pl.multiple_of(segment * SEG_LEN, 128), SEG_LEN)
        return surveillance[0, :, at], surveillance[1, :, at]

    def cross_terms(segment, total):
        s_re, s_im = signal_of(segment)
        zero = jnp.zeros((128 - 2 * width, SEG_LEN), jnp.float32)
        with_re = halves(jnp.concatenate([s_re, s_im, zero], axis=0))
        with_im = halves(jnp.concatenate([s_im, -s_re, zero], axis=0))
        return tuple(
            x + (dot_beside(taps[0], with_re) + dot_beside(taps[1], with_im))
            for x, taps in zip(total, taps_of(segment))
        )

    product = lax.fori_loop(0, segments, cross_terms, blank, unroll=UNROLL)
    for half in range(2):
        mine[half] = product[half].T[: 2 * width]
    to_pair = Exchange(PAIR, lambda p: mine.at[p], lambda p: pair, pair_sem.at[0:1], pair_sem.at[1:2]).start()

    @pl.when(here == count - 1)
    def _():
        each(count, lambda d: tail_copy(d).wait_send())

    @pl.when(here != count - 1)
    def _():
        tail_copy(1).wait_recv()

    edge_r, edge_i = edge_matrix(tail[...])
    real[...] = edge_r
    imag[...] = edge_i
    along_y = Exchange(ALONG_Y, lambda p: ring_y.at[y], lambda p: ring_y.at[p], y_send, y_recv)
    to_pair.wait()
    ring_y[y] = mine[core] + pair[...]
    along_y.start()
    to_gram.wait()
    gram = jnp.sum(gram_all[...], axis=0)
    column = jnp.concatenate([gram[0:1], gram[1:2]], axis=1)
    column = jnp.concatenate([column, jnp.concatenate([gram[2:3], gram[3:4]], axis=1)], axis=0)
    column = jnp.concatenate([column, jnp.zeros((6, LAGS), jnp.float32)], axis=0)
    start_r, start_i = normal_matrix(column, real[...], imag[...], loading[0])
    real[...] = start_r
    imag[...] = start_i

    along_z = Exchange(ALONG_Z, lambda p: ring_z.at[z], lambda p: ring_z.at[p], z_send, z_recv)
    out = Exchange(PAIR, lambda p: cross.at[core], lambda p: cross.at[p], out_sem.at[0:1], out_sem.at[1:2])

    def between(index):
        @pl.when(index == 2)
        def _():
            along_y.wait()
            ring_z[z] = (ring_y[0] + ring_y[1]) + (ring_y[2] + ring_y[3])
            along_z.start()

        @pl.when(index == 6)
        def _():
            along_z.wait()
            cross[core] = ((ring_z[0] + ring_z[1]) + (ring_z[2] + ring_z[3])) + (
                (ring_z[4] + ring_z[5]) + (ring_z[6] + ring_z[7])
            )
            out.start()

    invert(real, imag, top, done, between)
    out.wait()
    right = jnp.concatenate([cross[0], cross[1]], axis=1)
    spun = jnp.concatenate([-right[width:], right[:width]], axis=0)
    w = dot(right, real[...], NT) + dot(spun, imag[...], NT)
    weights[...] = w

    w_re, w_im = w[:width], w[width:]
    on_re = halves(w)
    on_im = halves(jnp.concatenate([-w_im, w_re], axis=0))
    own_row = lax.broadcasted_iota(jnp.int32, (128, SEG_LEN), 0) // (2 * width)

    def cancelled(segment, energy):
        taps = taps_of(segment)
        joined = [
            [jnp.concatenate([taps[0][part][piece], taps[1][part][piece]], axis=0) for piece in range(2)]
            for part in range(2)
        ]
        clutter = dot_stacked(on_re, joined[0]) + dot_stacked(on_im, joined[1])
        rest = jnp.concatenate(signal_of(segment), axis=0) - clutter
        residual[segment] = rest
        square = rest * rest
        for tile in range(SEG_LEN // 128):
            energy = energy + square[:, 128 * tile : 128 * tile + 128]
        return energy

    energy = lax.fori_loop(0, segments, cancelled, jnp.zeros((2 * width, 128), jnp.float32), unroll=UNROLL)
    energy = jnp.sum(energy, axis=1, keepdims=True)
    energy = jnp.broadcast_to(energy[:width] + energy[width:], (width, 128))
    energy = jnp.concatenate([energy, jnp.zeros((128 - width, 128), jnp.float32)], axis=0)
    power_z[z] = energy.T[:8]
    to_z = Exchange(ALONG_Z, lambda p: power_z.at[z], lambda p: power_z.at[p], pz_send, pz_recv).start()

    to_far = Exchange(FAR, lambda p: corr.at[p], lambda p: landed.at[p], far_send, far_recv)
    for half in range(2):

        def correlate(segment, total):
            at = pl.ds(pl.multiple_of(segment * SEG_LEN + 256 - 128 * half, 128), SEG_LEN)
            rest = residual[segment]
            swapped = jnp.concatenate([rest[width:], -rest[:width]], axis=0)
            own = own_row == segment
            with_re = halves(jnp.where(own, jnp.concatenate([rest] * segments, axis=0), 0.0))
            with_im = halves(jnp.where(own, jnp.concatenate([swapped] * segments, axis=0), 0.0))
            real_taps = [table[0, piece, :, at] for piece in range(2)]
            imag_taps = [table[1, piece, :, at] for piece in range(2)]
            return total + (dot_beside(real_taps, with_re) + dot_beside(imag_taps, with_im))

        total = lax.fori_loop(0, segments, correlate, blank[0], unroll=UNROLL)
        corr[16 * half : 16 * half + 16] = total.reshape(16, 8, 128)

        def send(p, carry):
            @pl.when(p != far)
            def _():
                to_far.copy(lax.rem(p - far + 32, 32)).start()

            return carry

        lax.fori_loop(16 * half, 16 * half + 16, send, 0)
    landed[far] = corr[far]
    to_z.wait()
    parts = [power_z[i] for i in range(8)]
    power_y[y] = ((parts[0] + parts[1]) + (parts[2] + parts[3])) + ((parts[4] + parts[5]) + (parts[6] + parts[7]))
    to_y = Exchange(ALONG_Y, lambda p: power_y.at[y], lambda p: power_y.at[p], py_send, py_recv).start()
    to_far.wait()
    everything = landed[...]
    for lag in range(8):
        turned[lag] = everything[:, lag, :]
    to_near = Exchange(NEAR, lambda p: turned.at[p], lambda p: cells.at[p], near_send, near_recv).start()
    cells[near] = turned[near]
    to_y.wait()
    power[...] = (power_y[0] + power_y[1]) + (power_y[2] + power_y[3])
    energies[near] = power[...]
    Exchange(NEAR, lambda p: power, lambda p: energies.at[p], pa_send, pa_recv).start().wait()
    to_near.wait()


def cancel(loading, reference, surveillance):
    vmem = pl.BlockSpec(memory_space=pltpu.VMEM)
    length = reference.shape[1]
    width = surveillance.shape[1]
    dma = pltpu.SemaphoreType.DMA

    def block(*shape):
        return pltpu.VMEM(shape, jnp.float32)

    half = (2 * width, 128)
    return pl.pallas_call(
        cancel_kernel,
        out_shape=[
            jax.ShapeDtypeStruct((2 * width, LAGS), jnp.float32),
            jax.ShapeDtypeStruct((8, 32, 128), jnp.float32),
            jax.ShapeDtypeStruct((8, 8, 128), jnp.float32),
        ],
        in_specs=[pl.BlockSpec(memory_space=pltpu.SMEM)] + [pl.BlockSpec(memory_space=pltpu.HBM)] * 2,
        out_specs=[vmem] * 3,
        scratch_shapes=[
            block(*reference.shape), block(*surveillance.shape), dma((2,)),
            pltpu.VMEM((2, 2, 128, LAGS + length), jnp.bfloat16),
            block(2, LAGS), block(2, LAGS), block(2, *half), block(2, 4, 128), block(32, 4, 128),
            block(LAGS, LAGS), block(LAGS, LAGS), block(2, PANEL, LAGS), block(2, PANEL, LAGS),
            block(*half), block(4, *half), block(8, *half), block(2, *half), block(4, 2 * width, SEG_LEN),
            block(32, 8, 128), block(32, 8, 128), block(8, 32, 128), block(8, 128), block(8, 8, 128), block(4, 8, 128),
            dma((2,)), dma((63,)), dma((1,)), dma((2,)), dma((31,)), dma((31,)),
            dma((2,)), dma((3,)), dma((3,)), dma((7,)), dma((7,)), dma((2,)),
            dma((31,)), dma((31,)), dma((7,)), dma((7,)), dma((7,)), dma((7,)), dma((3,)), dma((3,)), dma((7,)), dma((7,)),
        ],
        compiler_params=pltpu.CompilerParams(collective_id=0, has_side_effects=True, vmem_limit_bytes=24 * 2**20),
        name="cancel",
    )(loading, reference, surveillance)


def doppler_tables(shards, segments):
    short = DOPP // segments
    order = np.arange(shards).reshape(-1, 2).T.reshape(-1)
    angle = 2.0 * np.pi / short * (np.outer(order, np.arange(short)) % short)
    table = np.concatenate([np.cos(angle), np.sin(angle)], axis=1)
    turn = 2.0 * np.pi / DOPP * np.outer(np.arange(segments), np.arange(DOPP))
    turns = np.stack([np.cos(turn), np.sin(turn)])
    return table.astype(np.float32), turns.astype(np.float32)


def doppler_kernel(samples, weights, cells, energies, table, turns, out, kept):
    near, _, lanes = cells.shape
    groups = near // 2
    segments = turns.shape[1]
    width = lanes // segments // 2
    basis = halves(table[...])
    short = DOPP // segments
    def group(g, carry):
        power = (energies[g] + energies[groups + g]) / samples
        scale = lax.rsqrt(samples * (power + EPSILON))
        by = jnp.broadcast_to(scale[0:1], (128, 128)).T[:width, 0:1]
        rows = jnp.concatenate([cells[g], cells[groups + g]], axis=0)
        wave = dot3(halves(rows.T), basis)
        total_r = total_i = None
        for s in range(segments):
            base = 2 * width * s
            a_r, a_i = wave[base : base + width, :short], wave[base : base + width, short:]
            b_r, b_i = (
                wave[base + width : base + 2 * width, :short],
                wave[base + width : base + 2 * width, short:],
            )
            y_r = (a_r + b_i) * by
            y_i = (b_r - a_i) * by
            y_r = jnp.concatenate([y_r] * segments, axis=1)
            y_i = jnp.concatenate([y_i] * segments, axis=1)
            if s == 0:
                total_r, total_i = y_r, y_i
                continue
            c, d = turns[0, s : s + 1, :], turns[1, s : s + 1, :]
            total_r = total_r + (y_r * c + y_i * d)
            total_i = total_i + (y_i * c - y_r * d)
        at = pl.ds(width * g, width)
        out[0, 0, at, :] = total_r
        out[0, 1, at, :] = total_i
        return carry

    for g in range(groups):
        group(g, 0)
    kept[...] = weights[...]


def doppler(weights, cells, energies, segments, samples):
    vmem = pl.BlockSpec(memory_space=pltpu.VMEM)
    shards = 2 * cells.shape[1]
    table, turns = doppler_tables(shards, segments)
    width = cells.shape[2] // segments // 2
    groups = cells.shape[0] // 2
    return pl.pallas_call(
        functools.partial(doppler_kernel, samples),
        out_shape=[
            jax.ShapeDtypeStruct((1, 2, width * groups, DOPP), jnp.float32),
            jax.ShapeDtypeStruct(weights.shape, jnp.float32),
        ],
        in_specs=[vmem] * 5,
        out_specs=[vmem, vmem],
        compiler_params=pltpu.CompilerParams(vmem_limit_bytes=24 * 2**20),
        name="doppler",
    )(weights, cells, energies, jnp.asarray(table), jnp.asarray(turns))


def per_device(reference_signal, surveillance, loading):
    length = reference_signal.shape[1]
    samples = float(length * lax.axis_size(TM))
    weights, cells, energies = cancel(loading, reference_signal, surveillance)
    full, weights = doppler(weights, cells, energies, length // SEG_LEN, samples)
    return full, jnp.swapaxes(weights.reshape(2, -1, LAGS), 1, 2)


def solution(mesh):
    split = Mesh(
        mesh.devices.reshape(4, 8, 2, mesh.shape["chan"]), ("tm_0", "tm_1", "tm_2", "chan")
    )
    in_specs = (P(None, TM), P(None, "chan", TM), P())
    out_specs = (P(TM_CHAN, None, None, None), P(None, None, "chan"))
    return jax.shard_map(
        per_device, mesh=split, in_specs=in_specs, out_specs=out_specs, check_vma=False
    )
```

```python
import functools

import jax
import jax.numpy as jnp
import numpy as np
from jax import lax
from jax.experimental import pallas as pl
from jax.experimental.pallas import tpu as pltpu
from jax.sharding import Mesh
from jax.sharding import PartitionSpec as P

LAGS = 256
DOPP = 1024
SEG_LEN = 512
TM = ("tm_0", "tm_1", "tm_2")
TM_CHAN = ("tm_0", "tm_1", "tm_2", "chan")
EPSILON = 1e-06
PANEL = 32
UNROLL = 2
PIVOTS = 4
ROWS = 40
MESH = pl.DeviceIdType.MESH

highest = lax.Precision.HIGHEST
NN = (((1,), (0,)), ((), ()))
NT = (((1,), (1,)), ((), ()))


def dot(a, b, dims=NN):
    return lax.dot_general(a, b, dims, precision=highest, preferred_element_type=jnp.float32)


def halves(x):
    high = x.astype(jnp.bfloat16)
    return high, (x - high.astype(jnp.float32)).astype(jnp.bfloat16)


def dot3(a, b, dims=NN):
    def one(x, y):
        return lax.dot_general(x, y, dims, preferred_element_type=jnp.float32)

    return one(a[0], b[0]) + (one(a[0], b[1]) + one(a[1], b[0]))


def dot_beside(a, b):
    both = lax.dot_general(a[0], jnp.concatenate(b, axis=0), NT, preferred_element_type=jnp.float32)
    rest = lax.dot_general(a[1], b[0], NT, preferred_element_type=jnp.float32)
    return both[:, :128] + (both[:, 128:] + rest)


def dot_stacked(a, b):
    rows = a[0].shape[0]
    both = lax.dot_general(jnp.concatenate(a, axis=0), b[0], NN, preferred_element_type=jnp.float32)
    rest = lax.dot_general(a[0], b[1], NN, preferred_element_type=jnp.float32)
    return both[:rows] + (both[rows:] + rest)


def toeplitz(row, rows):
    wide = jnp.broadcast_to(row, (rows, row.shape[1]))
    return pltpu.roll(wide, 0, 1, stride=1, stride_axis=0)


def each(count, act):
    if count == 2:
        act(1)
    else:
        lax.fori_loop(1, count, lambda d, carry: (act(d), carry)[1], 0)


class Exchange:
    def __init__(self, axes, src, dst, send, recv):
        self.axes, self.src, self.dst, self.send, self.recv = axes, src, dst, send, recv
        self.count = int(np.prod([lax.axis_size(a) for a in axes]))

    def copy(self, d):
        here = place(self.axes)
        there = lax.rem(here + d, self.count)
        return pltpu.make_async_remote_copy(
            src_ref=self.src(there),
            dst_ref=self.dst(here),
            send_sem=self.send.at[d - 1],
            recv_sem=self.recv.at[d - 1],
            device_id=device(self.axes, there),
            device_id_type=MESH,
        )

    def start(self):
        each(self.count, lambda d: self.copy(d).start())
        return self

    def wait(self):
        each(self.count, lambda d: self.copy(d).wait())


def place(axes):
    index = lax.axis_index(axes[0])
    for a in axes[1:]:
        index = index * lax.axis_size(a) + lax.axis_index(a)
    return index


def device(axes, index):
    coordinates = {}
    for a in reversed(axes):
        coordinates[a] = lax.rem(index, lax.axis_size(a))
        index = lax.div(index, lax.axis_size(a))
    return coordinates


def greet(barrier, axes, skip=0):
    count = int(np.prod([lax.axis_size(a) for a in axes]))
    here = place(axes)

    def one(d):
        pl.semaphore_signal(
            barrier, inc=1, device_id=device(axes, lax.rem(here + d, count)), device_id_type=MESH
        )

    if skip:
        for d in range(1, count):
            if d != skip:
                one(d)
        return count - 2
    each(count, one)
    return count - 1


def times(a, b):
    if a[1] is None and b[1] is None:
        return (a[0] * b[0], None)
    if a[1] is None:
        return (a[0] * b[0], a[0] * b[1])
    if b[1] is None:
        return (a[0] * b[0], a[1] * b[0])
    return (a[0] * b[0] - a[1] * b[1], a[0] * b[1] + a[1] * b[0])


def plus(a, b):
    if a[1] is None:
        return (a[0] + b[0], b[1])
    if b[1] is None:
        return (a[0] + b[0], a[1])
    return (a[0] + b[0], a[1] + b[1])


def minus(a, b):
    return (a[0] - b[0], None if b[1] is None else a[1] - b[1])


def negative(a):
    return (-a[0], None if a[1] is None else -a[1])


def conjugate(a):
    return (a[0], None if a[1] is None else -a[1])


def product(left, right):
    out = []
    for row in left:
        line = []
        for j in range(len(right[0])):
            total = times(row[0], right[0][j])
            for k in range(1, len(row)):
                total = plus(total, times(row[k], right[k][j]))
            line.append(total)
        out.append(line)
    return out


def adjoint(block):
    return [[conjugate(block[j][i]) for j in range(len(block))] for i in range(len(block[0]))]


def hermitian_inverse(block):
    size = len(block)
    if size == 1:
        return [[(1.0 / block[0][0][0], None)]]
    if size == 2:
        a, c, d = block[0][0][0], block[0][1], block[1][1][0]
        scale = 1.0 / (a * d - (c[0] * c[0] + c[1] * c[1]))
        off = (-c[0] * scale, -c[1] * scale)
        return [[(d * scale, None), off], [conjugate(off), (a * scale, None)]]
    half = size // 2
    head = [row[:half] for row in block[:half]]
    side = [row[half:] for row in block[:half]]
    tail = [row[half:] for row in block[half:]]
    head_inverse = hermitian_inverse(head)
    lifted = product(head_inverse, side)
    drop = product(adjoint(side), lifted)
    rest = [[minus(tail[i][j], drop[i][j]) for j in range(half)] for i in range(half)]
    rest_inverse = hermitian_inverse(rest)
    corner = product(lifted, rest_inverse)
    extra = product(corner, adjoint(lifted))
    first = [[plus(head_inverse[i][j], extra[i][j]) for j in range(half)] for i in range(half)]
    right = [[negative(corner[i][j]) for j in range(half)] for i in range(half)]
    below = adjoint(right)
    return [first[i] + right[i] for i in range(half)] + [below[i] + rest_inverse[i] for i in range(half)]


def added(terms):
    while len(terms) > 1:
        terms = [sum(terms[i : i + 2][1:], terms[i]) for i in range(0, len(terms), 2)]
    return terms[0]


def eliminate(real, imag):
    height, n = real.shape
    m = PIVOTS
    lane = lax.broadcasted_iota(jnp.int32, (1, n), 1)
    lanes = lax.broadcasted_iota(jnp.int32, (height, 128), 1)
    rows = lax.broadcasted_iota(jnp.int32, (height, 128), 0)

    def wide(value):
        return None if value is None else jnp.concatenate([value] * (n // 128), axis=1)

    for k in range(0, height, m):
        col_r = [jnp.broadcast_to(real[:, k + j : k + j + 1], (height, 128)) for j in range(m)]
        col_i = [jnp.broadcast_to(imag[:, k + j : k + j + 1], (height, 128)) for j in range(m)]
        block = [
            [(col_r[j][k + i : k + i + 1], col_i[j][k + i : k + i + 1]) for j in range(m)]
            for i in range(m)
        ]
        inverse = [[(wide(q[0]), wide(q[1])) for q in row] for row in hermitian_inverse(block)]
        hit = (lane >= k) & (lane < k + m)
        old = [
            (
                jnp.where(hit, jnp.where(lane == k + i, 1.0, 0.0), real[k + i : k + i + 1]),
                jnp.where(hit, 0.0, imag[k + i : k + i + 1]),
            )
            for i in range(m)
        ]
        new = product(inverse, [[value] for value in old])
        new = [line[0] for line in new]
        inside = (rows >= k) & (rows < k + m)
        col_r = [jnp.where(inside, jnp.where(rows == k + j, -1.0, 0.0), col_r[j]) for j in range(m)]
        col_i = [jnp.where(inside, 0.0, col_i[j]) for j in range(m)]
        gone = inside | ((lanes >= k) & (lanes < k + m))
        out_r, out_i = [], []
        for t in range(n // 128):
            cut = slice(128 * t, 128 * t + 128)
            mask = gone if t == 0 else inside
            next_r = jnp.where(mask, 0.0, real[:, cut])
            next_i = jnp.where(mask, 0.0, imag[:, cut])
            terms_r, terms_i = [], []
            for j in range(m):
                row_r, row_i = new[j][0][:, cut], new[j][1][:, cut]
                terms_r.append(col_r[j] * row_r - col_i[j] * row_i)
                terms_i.append(col_r[j] * row_i + col_i[j] * row_r)
            out_r.append(next_r - added(terms_r))
            out_i.append(next_i - added(terms_i))
        real = jnp.concatenate(out_r, axis=1)
        imag = jnp.concatenate(out_i, axis=1)
    return real, imag


def thirds(x):
    high = x.astype(jnp.bfloat16)
    rest = x - high.astype(jnp.float32)
    middle = rest.astype(jnp.bfloat16)
    return high, middle, (rest - middle.astype(jnp.float32)).astype(jnp.bfloat16)


def packed(factor, top_r, top_i):
    width = 2 * PANEL
    right = jnp.concatenate(
        [jnp.concatenate([top_r, top_i], axis=1), jnp.concatenate([-top_i, top_r], axis=1)], axis=0
    )
    high, middle, low = thirds(right)
    right = jnp.concatenate([high, middle, low, high, middle, high], axis=0)
    high = factor.astype(jnp.bfloat16).astype(jnp.float32)
    rest = factor - high
    middle = rest.astype(jnp.bfloat16).astype(jnp.float32)
    low = rest - middle
    if width < 128:
        parts = [high + pltpu.roll(high, width, 1), high + pltpu.roll(middle, width, 1), middle + pltpu.roll(low, width, 1)]
    else:
        parts = [high, high, high, middle, middle, low]
    left = jnp.concatenate(parts, axis=1).astype(jnp.bfloat16)
    return lax.dot_general(left, right, NN, preferred_element_type=jnp.float32)


def beside(first, second):
    lane = lax.broadcasted_iota(jnp.int32, first.shape, 1)
    both = jnp.where(lane < PANEL, first, pltpu.roll(second, PANEL, 1))
    return jnp.where(lane < 2 * PANEL, both, 0.0)


def invert(real, imag, top, done, between):
    b = PANEL
    panels = LAGS // b

    def turn(x):
        return pltpu.roll(x, LAGS - b, 1)

    def apply(last, live):
        all_r, all_i = real[...], imag[...]
        row = lax.broadcasted_iota(jnp.int32, (LAGS, 128), 0)
        outside = (row < last * b) | (row >= last * b + b)
        if live is not None:
            outside = outside & live
        factor = jnp.where(outside, beside(all_r[:, :128], all_i[:, :128]), 0.0)
        update = packed(factor, done[0], done[1])
        column = lax.broadcasted_iota(jnp.int32, (LAGS, LAGS), 1)
        drop = column < b
        if live is not None:
            drop = drop & live
        real[...] = turn(jnp.where(drop, 0.0, all_r) - update[:, :LAGS])
        imag[...] = turn(jnp.where(drop, 0.0, all_i) - update[:, LAGS:])
        held = pl.ds(pl.multiple_of(last * b, b), b)
        real[held, :] = turn(done[0])
        imag[held, :] = turn(done[1])

    top[0] = real[:b, :]
    top[1] = imag[:b, :]
    real[...] = pltpu.roll(real[...], b, 1)
    imag[...] = pltpu.roll(imag[...], b, 1)
    done[0] = real[LAGS - b :, :]
    done[1] = imag[LAGS - b :, :]

    def panel(index, carry):
        between(index)
        apply(lax.rem(index + panels - 1, panels), index > 0)
        new_r, new_i = eliminate(top[0], top[1])
        held = pl.ds(pl.multiple_of(lax.rem(index + 1, panels) * b, b), b)
        row_r, row_i = real[held, :], imag[held, :]
        update = packed(beside(row_r[:, :128], row_i[:, :128]), new_r, new_i)
        drop = lax.broadcasted_iota(jnp.int32, (b, LAGS), 1) < b
        top[0] = turn(jnp.where(drop, 0.0, row_r) - update[:, :LAGS])
        top[1] = turn(jnp.where(drop, 0.0, row_i) - update[:, LAGS:])
        done[0] = new_r
        done[1] = new_i
        return carry

    lax.fori_loop(0, panels, panel, 0)
    apply(panels - 1, None)


def edge_matrix(tail):
    blank = jnp.zeros((1, LAGS), jnp.float32)
    edge_r = toeplitz(jnp.concatenate([blank, tail[0:1]], axis=1), LAGS)[:, :LAGS]
    edge_i = toeplitz(jnp.concatenate([blank, tail[1:2]], axis=1), LAGS)[:, :LAGS]
    one = jnp.concatenate([edge_r, edge_i], axis=1)
    two = jnp.concatenate([edge_i, -edge_r], axis=1)
    return dot(one, one, NT), dot(one, two, NT)


def normal_matrix(column, edge_r, edge_i, loading):
    i0 = lax.broadcasted_iota(jnp.int32, (LAGS, LAGS), 0)
    i1 = lax.broadcasted_iota(jnp.int32, (LAGS, LAGS), 1)
    flip = jnp.where(i0 + i1 == LAGS - 1, 1.0, 0.0)
    behind = pltpu.roll(dot(column, flip), 1, 1)
    lane = lax.broadcasted_iota(jnp.int32, behind.shape, 1)
    behind = jnp.where(lane == 0, 0.0, behind)
    base_r = toeplitz(jnp.concatenate([column[0:1], behind[0:1]], axis=1), LAGS)[:, :LAGS]
    base_i = toeplitz(jnp.concatenate([-column[1:2], behind[1:2]], axis=1), LAGS)[:, :LAGS]
    diagonal = i0 == i1
    off = jnp.sum(jnp.sum(jnp.where(diagonal, edge_r, 0.0), axis=0, keepdims=True), axis=1, keepdims=True)
    lam = loading * (column[0:1, 0:1] - off / LAGS)
    real = base_r - edge_r
    return jnp.where(diagonal, real + lam, real), base_i - edge_i


PAIR, FAR, NEAR = TM[2:], TM[:2], (TM[2], "chan")
ALONG_Y, ALONG_Z = TM[:1], TM[1:2]


def cancel_kernel(
    loading, reference, surveillance, weights, cells, energies,
    table, halo, tail, mine, gram_pair, gram_all, real, imag, top, done,
    pair, ring_y, ring_z, cross, residual, corr, power, power_far,
    edge_sem, tail_send, tail_recv, gram_sem, gram_send, gram_recv,
    pair_sem, y_send, y_recv, z_send, z_recv, out_sem,
    all_send, all_recv, pf_send, pf_recv, pn_send, pn_recv,
):
    length = reference.shape[1]
    width = surveillance.shape[1]
    count = lax.axis_size(TM)
    here = place(TM)
    core, y, z, far, near = place(PAIR), place(ALONG_Y), place(ALONG_Z), place(FAR), place(NEAR)
    barrier = pltpu.get_barrier_semaphore()
    total = greet(barrier, TM)
    total += greet(barrier, NEAR, 4)

    def fill(tile, windows):
        delayed = [toeplitz(x, 128)[:, 128:] for x in windows]
        at = pl.ds(pl.multiple_of(128 * tile, 128), 128)
        for part in range(2):
            high, low = halves(delayed[part])
            table[part, 0, :, at] = high
            table[part, 1, :, at] = low
        return delayed

    def lagged(delayed, start):
        now = reference[:, pl.ds(pl.multiple_of(start, 128), 128)]
        now_r, now_i = now[0:1], now[1:2]
        return (delayed[0] * now_r + delayed[1] * now_i, delayed[0] * now_i - delayed[1] * now_r)

    def plus_all(sums, terms):
        return tuple(x + y for x, y in zip(sums, terms))

    tiles = (LAGS + length) // 128

    def fill_inner(tile, sums):
        start = pl.multiple_of(128 * tile - 384, 128)
        window = reference[:, pl.ds(start, LAGS)]
        delayed = fill(tile, [window[0:1], window[1:2]])
        return (
            plus_all(sums[0], lagged(delayed, 128 * tile - 256)),
            plus_all(sums[1], lagged(delayed, 128 * tile - 128)),
        )

    blank = (jnp.zeros((128, 128), jnp.float32),) * 2
    sums = lax.fori_loop(3, tiles - 1, fill_inner, (blank, blank))
    window = reference[:, length - LAGS :]
    delayed = fill(tiles - 1, [window[0:1], window[1:2]])
    sums = [plus_all(sums[0], lagged(delayed, length - 128)), sums[1]]

    pl.semaphore_wait(barrier, total)
    forward = pltpu.make_async_remote_copy(
        src_ref=reference.at[:, pl.ds(length - LAGS, LAGS)],
        dst_ref=halo,
        send_sem=edge_sem.at[0],
        recv_sem=edge_sem.at[1],
        device_id=device(TM, lax.rem(here + 1, count)),
        device_id_type=MESH,
    )
    forward.start()

    def tail_copy(d):
        return pltpu.make_async_remote_copy(
            src_ref=reference.at[:, pl.ds(length - LAGS, LAGS)],
            dst_ref=tail,
            send_sem=tail_send.at[d - 1],
            recv_sem=tail_recv.at[0],
            device_id=device(TM, lax.rem(here + d, count)),
            device_id_type=MESH,
        )

    @pl.when(here == count - 1)
    def _():
        tail[...] = reference[:, length - LAGS :]
        each(count, lambda d: tail_copy(d).start())

    forward.wait()
    before = jnp.where(here > 0, halo[...], 0.0)
    delayed = fill(1, [before[0:1], before[1:2]])
    sums[1] = plus_all(sums[1], lagged(delayed, 0))
    joint = jnp.concatenate([before[:, 128:], reference[:, :128]], axis=1)
    delayed = fill(2, [joint[0:1], joint[1:2]])
    sums[0] = plus_all(sums[0], lagged(delayed, 0))
    sums[1] = plus_all(sums[1], lagged(delayed, 128))
    for half in range(2):
        for part in range(2):
            line = jnp.sum(sums[half][part].T, axis=0, keepdims=True)
            gram_pair[0, 2 * part + half : 2 * part + half + 1, :] = line
    Exchange(PAIR, lambda p: gram_pair.at[0], lambda p: gram_pair.at[1], gram_sem.at[0:1], gram_sem.at[1:2]).start().wait()
    gram_all[far] = gram_pair[0] + gram_pair[1]
    to_gram = Exchange(FAR, lambda p: gram_all.at[far], lambda p: gram_all.at[p], gram_send, gram_recv).start()

    segments = length // SEG_LEN

    def taps_of(segment):
        taps = []
        for half in range(2):
            at = pl.ds(pl.multiple_of(segment * SEG_LEN + 256 - 128 * half, 128), SEG_LEN)
            taps.append([[table[part, piece, :, at] for piece in range(2)] for part in range(2)])
        return taps

    def signal_of(segment):
        at = pl.ds(pl.multiple_of(segment * SEG_LEN, 128), SEG_LEN)
        return surveillance[0, :, at], surveillance[1, :, at]

    def cross_terms(segment, total):
        s_re, s_im = signal_of(segment)
        zero = jnp.zeros((128 - 2 * width, SEG_LEN), jnp.float32)
        with_re = halves(jnp.concatenate([s_re, s_im, zero], axis=0))
        with_im = halves(jnp.concatenate([s_im, -s_re, zero], axis=0))
        return tuple(
            x + (dot_beside(taps[0], with_re) + dot_beside(taps[1], with_im))
            for x, taps in zip(total, taps_of(segment))
        )

    product = lax.fori_loop(0, segments, cross_terms, blank, unroll=UNROLL)
    for half in range(2):
        mine[half] = product[half].T[: 2 * width]
    to_pair = Exchange(PAIR, lambda p: mine.at[p], lambda p: pair, pair_sem.at[0:1], pair_sem.at[1:2]).start()

    @pl.when(here == count - 1)
    def _():
        each(count, lambda d: tail_copy(d).wait_send())

    @pl.when(here != count - 1)
    def _():
        tail_copy(1).wait_recv()

    edge_r, edge_i = edge_matrix(tail[...])
    real[...] = edge_r
    imag[...] = edge_i
    to_gram.wait()
    gram = jnp.sum(gram_all[...], axis=0)
    column = jnp.concatenate([gram[0:1], gram[1:2]], axis=1)
    column = jnp.concatenate([column, jnp.concatenate([gram[2:3], gram[3:4]], axis=1)], axis=0)
    column = jnp.concatenate([column, jnp.zeros((6, LAGS), jnp.float32)], axis=0)
    start_r, start_i = normal_matrix(column, real[...], imag[...], loading[0])
    real[...] = start_r
    imag[...] = start_i

    along_y = Exchange(ALONG_Y, lambda p: ring_y.at[y], lambda p: ring_y.at[p], y_send, y_recv)
    along_z = Exchange(ALONG_Z, lambda p: ring_z.at[z], lambda p: ring_z.at[p], z_send, z_recv)
    out = Exchange(PAIR, lambda p: cross.at[core], lambda p: cross.at[p], out_sem.at[0:1], out_sem.at[1:2])

    def between(index):
        @pl.when(index == 1)
        def _():
            to_pair.wait()
            ring_y[y] = mine[core] + pair[...]
            along_y.start()

        @pl.when(index == 3)
        def _():
            along_y.wait()
            ring_z[z] = (ring_y[0] + ring_y[1]) + (ring_y[2] + ring_y[3])
            along_z.start()

        @pl.when(index == 6)
        def _():
            along_z.wait()
            cross[core] = ((ring_z[0] + ring_z[1]) + (ring_z[2] + ring_z[3])) + (
                (ring_z[4] + ring_z[5]) + (ring_z[6] + ring_z[7])
            )
            out.start()

    invert(real, imag, top, done, between)
    out.wait()
    right = jnp.concatenate([cross[0], cross[1]], axis=1)
    spun = jnp.concatenate([-right[width:], right[:width]], axis=0)
    w = dot(right, real[...], NT) + dot(spun, imag[...], NT)
    weights[...] = w

    w_re, w_im = w[:width], w[width:]
    on_re = halves(w)
    on_im = halves(jnp.concatenate([-w_im, w_re], axis=0))
    own_row = lax.broadcasted_iota(jnp.int32, (128, SEG_LEN), 0) // (2 * width)

    def cancelled(segment, energy):
        taps = taps_of(segment)
        joined = [
            [jnp.concatenate([taps[0][part][piece], taps[1][part][piece]], axis=0) for piece in range(2)]
            for part in range(2)
        ]
        clutter = dot_stacked(on_re, joined[0]) + dot_stacked(on_im, joined[1])
        rest = jnp.concatenate(signal_of(segment), axis=0) - clutter
        residual[segment] = rest
        square = rest * rest
        for tile in range(SEG_LEN // 128):
            energy = energy + square[:, 128 * tile : 128 * tile + 128]
        return energy

    energy = lax.fori_loop(0, segments, cancelled, jnp.zeros((2 * width, 128), jnp.float32), unroll=UNROLL)
    energy = jnp.sum(energy, axis=1, keepdims=True)
    energy = jnp.broadcast_to(energy[:width] + energy[width:], (width, 128))
    energy = jnp.concatenate([energy, jnp.zeros((128 - width, 128), jnp.float32)], axis=0)
    power_far[far] = energy.T[:1]
    to_power = Exchange(FAR, lambda p: power_far.at[far], lambda p: power_far.at[p], pf_send, pf_recv).start()

    me = place(TM_CHAN)
    slot = lax.axis_index("chan") * count + here
    to_all = Exchange(TM_CHAN, lambda p: corr.at[p], lambda p: cells.at[slot], all_send, all_recv)
    for half in range(2):

        def correlate(segment, total):
            at = pl.ds(pl.multiple_of(segment * SEG_LEN + 256 - 128 * half, 128), SEG_LEN)
            rest = residual[segment]
            swapped = jnp.concatenate([rest[width:], -rest[:width]], axis=0)
            own = own_row == segment
            with_re = halves(jnp.where(own, jnp.concatenate([rest] * segments, axis=0), 0.0))
            with_im = halves(jnp.where(own, jnp.concatenate([swapped] * segments, axis=0), 0.0))
            real_taps = [table[0, piece, :, at] for piece in range(2)]
            imag_taps = [table[1, piece, :, at] for piece in range(2)]
            return total + (dot_beside(real_taps, with_re) + dot_beside(imag_taps, with_im))

        total = lax.fori_loop(0, segments, correlate, blank[0], unroll=UNROLL)
        corr[128 * half : 128 * half + 128] = total.reshape(128, 1, 128)

        def send(i, carry):
            p = 128 * half + lax.rem(me + i, 128)

            @pl.when(p != me)
            def _():
                to_all.copy(lax.rem(p - me + LAGS, LAGS)).start()

            return carry

        lax.fori_loop(0, 128, send, 0)
    cells[slot] = corr[me]
    to_power.wait()
    power[...] = jnp.sum(power_far[...], axis=0)
    energies[near] = power[...]
    to_near = Exchange(NEAR, lambda p: power, lambda p: energies.at[p], pn_send, pn_recv).start()
    to_all.wait()
    to_near.wait()


def cancel(loading, reference, surveillance):
    vmem = pl.BlockSpec(memory_space=pltpu.VMEM)
    length = reference.shape[1]
    width = surveillance.shape[1]
    dma = pltpu.SemaphoreType.DMA

    def block(*shape):
        return pltpu.VMEM(shape, jnp.float32)

    half = (2 * width, 128)
    return pl.pallas_call(
        cancel_kernel,
        out_shape=[
            jax.ShapeDtypeStruct((2 * width, LAGS), jnp.float32),
            jax.ShapeDtypeStruct((LAGS, 1, 128), jnp.float32),
            jax.ShapeDtypeStruct((8, 1, 128), jnp.float32),
        ],
        in_specs=[pl.BlockSpec(memory_space=pltpu.SMEM), vmem, vmem],
        out_specs=[vmem] * 3,
        scratch_shapes=[
            pltpu.VMEM((2, 2, 128, LAGS + length), jnp.bfloat16),
            block(2, LAGS), block(2, LAGS), block(2, *half), block(2, 4, 128), block(32, 4, 128),
            block(LAGS, LAGS), block(LAGS, LAGS), block(2, PANEL, LAGS), block(2, PANEL, LAGS),
            block(*half), block(4, *half), block(8, *half), block(2, *half), block(4, 2 * width, SEG_LEN),
            block(LAGS, 1, 128), block(1, 128), block(32, 1, 128),
            dma((2,)), dma((63,)), dma((1,)), dma((2,)), dma((31,)), dma((31,)),
            dma((2,)), dma((3,)), dma((3,)), dma((7,)), dma((7,)), dma((2,)),
            dma((255,)), dma((255,)), dma((31,)), dma((31,)), dma((7,)), dma((7,)),
        ],
        compiler_params=pltpu.CompilerParams(collective_id=0, has_side_effects=True, vmem_limit_bytes=24 * 2**20),
        name="cancel",
    )(loading, reference, surveillance)


def doppler_tables(shards, segments):
    short = DOPP // segments
    angle = 2.0 * np.pi / short * (np.outer(np.arange(shards), np.arange(short)) % short)
    table = np.concatenate([np.cos(angle), np.sin(angle)], axis=1)
    turn = 2.0 * np.pi / DOPP * np.outer(np.arange(segments), np.arange(DOPP))
    turns = np.stack([np.cos(turn), np.sin(turn)])
    return table.astype(np.float32), turns.astype(np.float32)


def doppler_kernel(samples, weights, cells, energies, table, turns, out, kept):
    lanes = cells.shape[2]
    groups = energies.shape[0] // 2
    shards = cells.shape[0] // groups
    segments = turns.shape[1]
    width = lanes // segments // 2
    basis = halves(table[...])
    short = DOPP // segments
    def group(g, carry):
        power = (energies[g] + energies[groups + g]) / samples
        scale = lax.rsqrt(samples * (power + EPSILON))
        by = jnp.broadcast_to(scale[0:1], (128, 128)).T[:width, 0:1]
        rows = cells[shards * g : shards * g + shards, 0, :]
        wave = dot3(halves(rows.T), basis)
        total_r = total_i = None
        for s in range(segments):
            base = 2 * width * s
            a_r, a_i = wave[base : base + width, :short], wave[base : base + width, short:]
            b_r, b_i = (
                wave[base + width : base + 2 * width, :short],
                wave[base + width : base + 2 * width, short:],
            )
            y_r = (a_r + b_i) * by
            y_i = (b_r - a_i) * by
            y_r = jnp.concatenate([y_r] * segments, axis=1)
            y_i = jnp.concatenate([y_i] * segments, axis=1)
            if s == 0:
                total_r, total_i = y_r, y_i
                continue
            c, d = turns[0, s : s + 1, :], turns[1, s : s + 1, :]
            total_r = total_r + (y_r * c + y_i * d)
            total_i = total_i + (y_i * c - y_r * d)
        at = pl.ds(width * g, width)
        out[0, 0, at, :] = total_r
        out[0, 1, at, :] = total_i
        return carry

    for g in range(groups):
        group(g, 0)
    kept[...] = weights[...]


def doppler(weights, cells, energies, segments, samples):
    vmem = pl.BlockSpec(memory_space=pltpu.VMEM)
    groups = energies.shape[0] // 2
    shards = cells.shape[0] // groups
    table, turns = doppler_tables(shards, segments)
    width = cells.shape[2] // segments // 2
    return pl.pallas_call(
        functools.partial(doppler_kernel, samples),
        out_shape=[
            jax.ShapeDtypeStruct((1, 2, width * groups, DOPP), jnp.float32),
            jax.ShapeDtypeStruct(weights.shape, jnp.float32),
        ],
        in_specs=[vmem] * 5,
        out_specs=[vmem, vmem],
        compiler_params=pltpu.CompilerParams(vmem_limit_bytes=24 * 2**20),
        name="doppler",
    )(weights, cells, energies, jnp.asarray(table), jnp.asarray(turns))


def per_device(reference_signal, surveillance, loading):
    length = reference_signal.shape[1]
    samples = float(length * lax.axis_size(TM))
    weights, cells, energies = cancel(loading, reference_signal, surveillance)
    full, weights = doppler(weights, cells, energies, length // SEG_LEN, samples)
    return full, jnp.swapaxes(weights.reshape(2, -1, LAGS), 1, 2)


def solution(mesh):
    split = Mesh(
        mesh.devices.reshape(4, 8, 2, mesh.shape["chan"]), ("tm_0", "tm_1", "tm_2", "chan")
    )
    in_specs = (P(None, TM), P(None, "chan", TM), P())
    out_specs = (P(TM_CHAN, None, None, None), P(None, None, "chan"))
    return jax.shard_map(
        per_device, mesh=split, in_specs=in_specs, out_specs=out_specs, check_vma=False
    )
```

```python
import functools

import jax
import jax.numpy as jnp
import numpy as np
from jax import lax
from jax.experimental import pallas as pl
from jax.experimental.pallas import tpu as pltpu
from jax.sharding import Mesh
from jax.sharding import PartitionSpec as P

LAGS = 256
DOPP = 1024
SEG_LEN = 512
TM = ("tm_0", "tm_1", "tm_2")
TM_CHAN = ("tm_0", "tm_1", "tm_2", "chan")
EPSILON = 1e-06
PANEL = 32
UNROLL = 2
PIVOTS = 4
ROWS = 40
MESH = pl.DeviceIdType.MESH

highest = lax.Precision.HIGHEST
NN = (((1,), (0,)), ((), ()))
NT = (((1,), (1,)), ((), ()))


def dot(a, b, dims=NN):
    return lax.dot_general(a, b, dims, precision=highest, preferred_element_type=jnp.float32)


def halves(x):
    high = x.astype(jnp.bfloat16)
    return high, (x - high.astype(jnp.float32)).astype(jnp.bfloat16)


def dot3(a, b, dims=NN):
    def one(x, y):
        return lax.dot_general(x, y, dims, preferred_element_type=jnp.float32)

    return one(a[0], b[0]) + (one(a[0], b[1]) + one(a[1], b[0]))


def dot_beside(a, b):
    both = lax.dot_general(a[0], jnp.concatenate(b, axis=0), NT, preferred_element_type=jnp.float32)
    rest = lax.dot_general(a[1], b[0], NT, preferred_element_type=jnp.float32)
    return both[:, :128] + (both[:, 128:] + rest)


def dot_stacked(a, b):
    rows = a[0].shape[0]
    both = lax.dot_general(jnp.concatenate(a, axis=0), b[0], NN, preferred_element_type=jnp.float32)
    rest = lax.dot_general(a[0], b[1], NN, preferred_element_type=jnp.float32)
    return both[:rows] + (both[rows:] + rest)


def toeplitz(row, rows):
    wide = jnp.broadcast_to(row, (rows, row.shape[1]))
    return pltpu.roll(wide, 0, 1, stride=1, stride_axis=0)


def each(count, act):
    if count == 2:
        act(1)
    else:
        lax.fori_loop(1, count, lambda d, carry: (act(d), carry)[1], 0)


class Exchange:
    def __init__(self, axes, src, dst, send, recv):
        self.axes, self.src, self.dst, self.send, self.recv = axes, src, dst, send, recv
        self.count = int(np.prod([lax.axis_size(a) for a in axes]))

    def copy(self, d):
        here = place(self.axes)
        there = lax.rem(here + d, self.count)
        return pltpu.make_async_remote_copy(
            src_ref=self.src(there),
            dst_ref=self.dst(here),
            send_sem=self.send.at[d - 1],
            recv_sem=self.recv.at[d - 1],
            device_id=device(self.axes, there),
            device_id_type=MESH,
        )

    def start(self):
        each(self.count, lambda d: self.copy(d).start())
        return self

    def wait(self):
        each(self.count, lambda d: self.copy(d).wait())


def place(axes):
    index = lax.axis_index(axes[0])
    for a in axes[1:]:
        index = index * lax.axis_size(a) + lax.axis_index(a)
    return index


def device(axes, index):
    coordinates = {}
    for a in reversed(axes):
        coordinates[a] = lax.rem(index, lax.axis_size(a))
        index = lax.div(index, lax.axis_size(a))
    return coordinates


def greet(barrier, axes, skip=0):
    count = int(np.prod([lax.axis_size(a) for a in axes]))
    here = place(axes)

    def one(d):
        pl.semaphore_signal(
            barrier, inc=1, device_id=device(axes, lax.rem(here + d, count)), device_id_type=MESH
        )

    if skip:
        for d in range(1, count):
            if d != skip:
                one(d)
        return count - 2
    each(count, one)
    return count - 1


def times(a, b):
    if a[1] is None and b[1] is None:
        return (a[0] * b[0], None)
    if a[1] is None:
        return (a[0] * b[0], a[0] * b[1])
    if b[1] is None:
        return (a[0] * b[0], a[1] * b[0])
    return (a[0] * b[0] - a[1] * b[1], a[0] * b[1] + a[1] * b[0])


def plus(a, b):
    if a[1] is None:
        return (a[0] + b[0], b[1])
    if b[1] is None:
        return (a[0] + b[0], a[1])
    return (a[0] + b[0], a[1] + b[1])


def minus(a, b):
    return (a[0] - b[0], None if b[1] is None else a[1] - b[1])


def negative(a):
    return (-a[0], None if a[1] is None else -a[1])


def conjugate(a):
    return (a[0], None if a[1] is None else -a[1])


def product(left, right):
    out = []
    for row in left:
        line = []
        for j in range(len(right[0])):
            total = times(row[0], right[0][j])
            for k in range(1, len(row)):
                total = plus(total, times(row[k], right[k][j]))
            line.append(total)
        out.append(line)
    return out


def adjoint(block):
    return [[conjugate(block[j][i]) for j in range(len(block))] for i in range(len(block[0]))]


def hermitian_inverse(block):
    size = len(block)
    if size == 1:
        return [[(1.0 / block[0][0][0], None)]]
    if size == 2:
        a, c, d = block[0][0][0], block[0][1], block[1][1][0]
        scale = 1.0 / (a * d - (c[0] * c[0] + c[1] * c[1]))
        off = (-c[0] * scale, -c[1] * scale)
        return [[(d * scale, None), off], [conjugate(off), (a * scale, None)]]
    half = size // 2
    head = [row[:half] for row in block[:half]]
    side = [row[half:] for row in block[:half]]
    tail = [row[half:] for row in block[half:]]
    head_inverse = hermitian_inverse(head)
    lifted = product(head_inverse, side)
    drop = product(adjoint(side), lifted)
    rest = [[minus(tail[i][j], drop[i][j]) for j in range(half)] for i in range(half)]
    rest_inverse = hermitian_inverse(rest)
    corner = product(lifted, rest_inverse)
    extra = product(corner, adjoint(lifted))
    first = [[plus(head_inverse[i][j], extra[i][j]) for j in range(half)] for i in range(half)]
    right = [[negative(corner[i][j]) for j in range(half)] for i in range(half)]
    below = adjoint(right)
    return [first[i] + right[i] for i in range(half)] + [below[i] + rest_inverse[i] for i in range(half)]


def added(terms):
    while len(terms) > 1:
        terms = [sum(terms[i : i + 2][1:], terms[i]) for i in range(0, len(terms), 2)]
    return terms[0]


def eliminate(real, imag):
    height, n = real.shape
    m = PIVOTS
    lane = lax.broadcasted_iota(jnp.int32, (1, n), 1)
    lanes = lax.broadcasted_iota(jnp.int32, (height, 128), 1)
    rows = lax.broadcasted_iota(jnp.int32, (height, 128), 0)

    def wide(value):
        return None if value is None else jnp.concatenate([value] * (n // 128), axis=1)

    for k in range(0, height, m):
        col_r = [jnp.broadcast_to(real[:, k + j : k + j + 1], (height, 128)) for j in range(m)]
        col_i = [jnp.broadcast_to(imag[:, k + j : k + j + 1], (height, 128)) for j in range(m)]
        block = [
            [(col_r[j][k + i : k + i + 1], col_i[j][k + i : k + i + 1]) for j in range(m)]
            for i in range(m)
        ]
        inverse = [[(wide(q[0]), wide(q[1])) for q in row] for row in hermitian_inverse(block)]
        hit = (lane >= k) & (lane < k + m)
        old = [
            (
                jnp.where(hit, jnp.where(lane == k + i, 1.0, 0.0), real[k + i : k + i + 1]),
                jnp.where(hit, 0.0, imag[k + i : k + i + 1]),
            )
            for i in range(m)
        ]
        new = product(inverse, [[value] for value in old])
        new = [line[0] for line in new]
        inside = (rows >= k) & (rows < k + m)
        col_r = [jnp.where(inside, jnp.where(rows == k + j, -1.0, 0.0), col_r[j]) for j in range(m)]
        col_i = [jnp.where(inside, 0.0, col_i[j]) for j in range(m)]
        gone = inside | ((lanes >= k) & (lanes < k + m))
        out_r, out_i = [], []
        for t in range(n // 128):
            cut = slice(128 * t, 128 * t + 128)
            mask = gone if t == 0 else inside
            next_r = jnp.where(mask, 0.0, real[:, cut])
            next_i = jnp.where(mask, 0.0, imag[:, cut])
            terms_r, terms_i = [], []
            for j in range(m):
                row_r, row_i = new[j][0][:, cut], new[j][1][:, cut]
                terms_r.append(col_r[j] * row_r - col_i[j] * row_i)
                terms_i.append(col_r[j] * row_i + col_i[j] * row_r)
            out_r.append(next_r - added(terms_r))
            out_i.append(next_i - added(terms_i))
        real = jnp.concatenate(out_r, axis=1)
        imag = jnp.concatenate(out_i, axis=1)
    return real, imag


def thirds(x):
    high = x.astype(jnp.bfloat16)
    rest = x - high.astype(jnp.float32)
    middle = rest.astype(jnp.bfloat16)
    return high, middle, (rest - middle.astype(jnp.float32)).astype(jnp.bfloat16)


def packed(factor, top_r, top_i):
    width = 2 * PANEL
    right = jnp.concatenate(
        [jnp.concatenate([top_r, top_i], axis=1), jnp.concatenate([-top_i, top_r], axis=1)], axis=0
    )
    high, middle, low = thirds(right)
    right = jnp.concatenate([high, middle, low, high, middle, high], axis=0)
    high = factor.astype(jnp.bfloat16).astype(jnp.float32)
    rest = factor - high
    middle = rest.astype(jnp.bfloat16).astype(jnp.float32)
    low = rest - middle
    if width < 128:
        parts = [high + pltpu.roll(high, width, 1), high + pltpu.roll(middle, width, 1), middle + pltpu.roll(low, width, 1)]
    else:
        parts = [high, high, high, middle, middle, low]
    left = jnp.concatenate(parts, axis=1).astype(jnp.bfloat16)
    return lax.dot_general(left, right, NN, preferred_element_type=jnp.float32)


def beside(first, second):
    lane = lax.broadcasted_iota(jnp.int32, first.shape, 1)
    both = jnp.where(lane < PANEL, first, pltpu.roll(second, PANEL, 1))
    return jnp.where(lane < 2 * PANEL, both, 0.0)


def invert(real, imag, top, done, between):
    b = PANEL
    panels = LAGS // b

    def turn(x):
        return pltpu.roll(x, LAGS - b, 1)

    def apply(last, live):
        all_r, all_i = real[...], imag[...]
        row = lax.broadcasted_iota(jnp.int32, (LAGS, 128), 0)
        outside = (row < last * b) | (row >= last * b + b)
        if live is not None:
            outside = outside & live
        factor = jnp.where(outside, beside(all_r[:, :128], all_i[:, :128]), 0.0)
        update = packed(factor, done[0], done[1])
        column = lax.broadcasted_iota(jnp.int32, (LAGS, LAGS), 1)
        drop = column < b
        if live is not None:
            drop = drop & live
        real[...] = turn(jnp.where(drop, 0.0, all_r) - update[:, :LAGS])
        imag[...] = turn(jnp.where(drop, 0.0, all_i) - update[:, LAGS:])
        held = pl.ds(pl.multiple_of(last * b, b), b)
        real[held, :] = turn(done[0])
        imag[held, :] = turn(done[1])

    top[0] = real[:b, :]
    top[1] = imag[:b, :]
    real[...] = pltpu.roll(real[...], b, 1)
    imag[...] = pltpu.roll(imag[...], b, 1)
    done[0] = real[LAGS - b :, :]
    done[1] = imag[LAGS - b :, :]

    def panel(index, carry):
        between(index)
        apply(lax.rem(index + panels - 1, panels), index > 0)
        new_r, new_i = eliminate(top[0], top[1])
        held = pl.ds(pl.multiple_of(lax.rem(index + 1, panels) * b, b), b)
        row_r, row_i = real[held, :], imag[held, :]
        update = packed(beside(row_r[:, :128], row_i[:, :128]), new_r, new_i)
        drop = lax.broadcasted_iota(jnp.int32, (b, LAGS), 1) < b
        top[0] = turn(jnp.where(drop, 0.0, row_r) - update[:, :LAGS])
        top[1] = turn(jnp.where(drop, 0.0, row_i) - update[:, LAGS:])
        done[0] = new_r
        done[1] = new_i
        return carry

    lax.fori_loop(0, panels, panel, 0)
    apply(panels - 1, None)


def edge_matrix(tail):
    blank = jnp.zeros((1, LAGS), jnp.float32)
    edge_r = toeplitz(jnp.concatenate([blank, tail[0:1]], axis=1), LAGS)[:, :LAGS]
    edge_i = toeplitz(jnp.concatenate([blank, tail[1:2]], axis=1), LAGS)[:, :LAGS]
    one = jnp.concatenate([edge_r, edge_i], axis=1)
    two = jnp.concatenate([edge_i, -edge_r], axis=1)
    return dot(one, one, NT), dot(one, two, NT)


def normal_matrix(column, edge_r, edge_i, loading):
    i0 = lax.broadcasted_iota(jnp.int32, (LAGS, LAGS), 0)
    i1 = lax.broadcasted_iota(jnp.int32, (LAGS, LAGS), 1)
    flip = jnp.where(i0 + i1 == LAGS - 1, 1.0, 0.0)
    behind = pltpu.roll(dot(column, flip), 1, 1)
    lane = lax.broadcasted_iota(jnp.int32, behind.shape, 1)
    behind = jnp.where(lane == 0, 0.0, behind)
    base_r = toeplitz(jnp.concatenate([column[0:1], behind[0:1]], axis=1), LAGS)[:, :LAGS]
    base_i = toeplitz(jnp.concatenate([-column[1:2], behind[1:2]], axis=1), LAGS)[:, :LAGS]
    diagonal = i0 == i1
    off = jnp.sum(jnp.sum(jnp.where(diagonal, edge_r, 0.0), axis=0, keepdims=True), axis=1, keepdims=True)
    lam = loading * (column[0:1, 0:1] - off / LAGS)
    real = base_r - edge_r
    return jnp.where(diagonal, real + lam, real), base_i - edge_i


PAIR, FAR, NEAR = TM[2:], TM[:2], (TM[2], "chan")
ALONG_Y, ALONG_Z = TM[:1], TM[1:2]


def cancel_kernel(
    loading, reference, surveillance_hbm, weights, cells, energies,
    surveillance, fetch_sem, table, halo, tail, mine, gram_pair, gram_all, real, imag, top, done,
    pair, ring_y, ring_z, cross, residual, corr, landed, turned, power, power_z, power_y,
    edge_sem, tail_send, tail_recv, gram_sem, gram_send, gram_recv,
    pair_sem, y_send, y_recv, z_send, z_recv, out_sem,
    far_send, far_recv, near_send, near_recv, pz_send, pz_recv, py_send, py_recv, pa_send, pa_recv,
):
    length = reference.shape[1]
    width = surveillance.shape[1]
    count = lax.axis_size(TM)
    here = place(TM)
    core, y, z, far, near = place(PAIR), place(ALONG_Y), place(ALONG_Z), place(FAR), place(NEAR)
    fetch = pltpu.make_async_copy(surveillance_hbm, surveillance, fetch_sem.at[0])
    fetch.start()
    barrier = pltpu.get_barrier_semaphore()
    total = greet(barrier, TM)
    total += greet(barrier, NEAR, 4)

    def fill(tile, windows):
        delayed = [toeplitz(x, 128)[:, 128:] for x in windows]
        at = pl.ds(pl.multiple_of(128 * tile, 128), 128)
        for part in range(2):
            high, low = halves(delayed[part])
            table[part, 0, :, at] = high
            table[part, 1, :, at] = low
        return delayed

    def lagged(delayed, start):
        now = reference[:, pl.ds(pl.multiple_of(start, 128), 128)]
        now_r, now_i = now[0:1], now[1:2]
        return (delayed[0] * now_r + delayed[1] * now_i, delayed[0] * now_i - delayed[1] * now_r)

    def plus_all(sums, terms):
        return tuple(x + y for x, y in zip(sums, terms))

    tiles = (LAGS + length) // 128

    def fill_inner(tile, sums):
        start = pl.multiple_of(128 * tile - 384, 128)
        window = reference[:, pl.ds(start, LAGS)]
        delayed = fill(tile, [window[0:1], window[1:2]])
        return (
            plus_all(sums[0], lagged(delayed, 128 * tile - 256)),
            plus_all(sums[1], lagged(delayed, 128 * tile - 128)),
        )

    blank = (jnp.zeros((128, 128), jnp.float32),) * 2
    sums = lax.fori_loop(3, tiles - 1, fill_inner, (blank, blank))
    window = reference[:, length - LAGS :]
    delayed = fill(tiles - 1, [window[0:1], window[1:2]])
    sums = [plus_all(sums[0], lagged(delayed, length - 128)), sums[1]]

    pl.semaphore_wait(barrier, total)
    forward = pltpu.make_async_remote_copy(
        src_ref=reference.at[:, pl.ds(length - LAGS, LAGS)],
        dst_ref=halo,
        send_sem=edge_sem.at[0],
        recv_sem=edge_sem.at[1],
        device_id=device(TM, lax.rem(here + 1, count)),
        device_id_type=MESH,
    )
    forward.start()

    def tail_copy(d):
        return pltpu.make_async_remote_copy(
            src_ref=reference.at[:, pl.ds(length - LAGS, LAGS)],
            dst_ref=tail,
            send_sem=tail_send.at[d - 1],
            recv_sem=tail_recv.at[0],
            device_id=device(TM, lax.rem(here + d, count)),
            device_id_type=MESH,
        )

    @pl.when(here == count - 1)
    def _():
        tail[...] = reference[:, length - LAGS :]
        each(count, lambda d: tail_copy(d).start())

    forward.wait()
    before = jnp.where(here > 0, halo[...], 0.0)
    delayed = fill(1, [before[0:1], before[1:2]])
    sums[1] = plus_all(sums[1], lagged(delayed, 0))
    joint = jnp.concatenate([before[:, 128:], reference[:, :128]], axis=1)
    delayed = fill(2, [joint[0:1], joint[1:2]])
    sums[0] = plus_all(sums[0], lagged(delayed, 0))
    sums[1] = plus_all(sums[1], lagged(delayed, 128))
    for half in range(2):
        for part in range(2):
            line = jnp.sum(sums[half][part].T, axis=0, keepdims=True)
            gram_pair[0, 2 * part + half : 2 * part + half + 1, :] = line
    Exchange(PAIR, lambda p: gram_pair.at[0], lambda p: gram_pair.at[1], gram_sem.at[0:1], gram_sem.at[1:2]).start().wait()
    gram_all[far] = gram_pair[0] + gram_pair[1]
    to_gram = Exchange(FAR, lambda p: gram_all.at[far], lambda p: gram_all.at[p], gram_send, gram_recv).start()

    fetch.wait()
    segments = length // SEG_LEN

    def taps_of(segment):
        taps = []
        for half in range(2):
            at = pl.ds(pl.multiple_of(segment * SEG_LEN + 256 - 128 * half, 128), SEG_LEN)
            taps.append([[table[part, piece, :, at] for piece in range(2)] for part in range(2)])
        return taps

    def signal_of(segment):
        at = pl.ds(pl.multiple_of(segment * SEG_LEN, 128), SEG_LEN)
        return surveillance[0, :, at], surveillance[1, :, at]

    def cross_terms(segment, total):
        s_re, s_im = signal_of(segment)
        zero = jnp.zeros((128 - 2 * width, SEG_LEN), jnp.float32)
        with_re = halves(jnp.concatenate([s_re, s_im, zero], axis=0))
        with_im = halves(jnp.concatenate([s_im, -s_re, zero], axis=0))
        return tuple(
            x + (dot_beside(taps[0], with_re) + dot_beside(taps[1], with_im))
            for x, taps in zip(total, taps_of(segment))
        )

    product = lax.fori_loop(0, segments, cross_terms, blank, unroll=UNROLL)
    for half in range(2):
        mine[half] = product[half].T[: 2 * width]
    to_pair = Exchange(PAIR, lambda p: mine.at[p], lambda p: pair, pair_sem.at[0:1], pair_sem.at[1:2]).start()

    @pl.when(here == count - 1)
    def _():
        each(count, lambda d: tail_copy(d).wait_send())

    @pl.when(here != count - 1)
    def _():
        tail_copy(1).wait_recv()

    edge_r, edge_i = edge_matrix(tail[...])
    real[...] = edge_r
    imag[...] = edge_i
    along_y = Exchange(ALONG_Y, lambda p: ring_y.at[y], lambda p: ring_y.at[p], y_send, y_recv)
    to_pair.wait()
    ring_y[y] = mine[core] + pair[...]
    along_y.start()
    to_gram.wait()
    gram = jnp.sum(gram_all[...], axis=0)
    column = jnp.concatenate([gram[0:1], gram[1:2]], axis=1)
    column = jnp.concatenate([column, jnp.concatenate([gram[2:3], gram[3:4]], axis=1)], axis=0)
    column = jnp.concatenate([column, jnp.zeros((6, LAGS), jnp.float32)], axis=0)
    start_r, start_i = normal_matrix(column, real[...], imag[...], loading[0])
    real[...] = start_r
    imag[...] = start_i

    along_z = Exchange(ALONG_Z, lambda p: ring_z.at[z], lambda p: ring_z.at[p], z_send, z_recv)
    out = Exchange(PAIR, lambda p: cross.at[core], lambda p: cross.at[p], out_sem.at[0:1], out_sem.at[1:2])

    def between(index):
        @pl.when(index == 2)
        def _():
            along_y.wait()
            ring_z[z] = (ring_y[0] + ring_y[1]) + (ring_y[2] + ring_y[3])
            along_z.start()

        @pl.when(index == 6)
        def _():
            along_z.wait()
            cross[core] = ((ring_z[0] + ring_z[1]) + (ring_z[2] + ring_z[3])) + (
                (ring_z[4] + ring_z[5]) + (ring_z[6] + ring_z[7])
            )
            out.start()

    invert(real, imag, top, done, between)
    out.wait()
    right = jnp.concatenate([cross[0], cross[1]], axis=1)
    spun = jnp.concatenate([-right[width:], right[:width]], axis=0)
    w = dot(right, real[...], NT) + dot(spun, imag[...], NT)
    weights[...] = w

    w_re, w_im = w[:width], w[width:]
    on_re = halves(w)
    on_im = halves(jnp.concatenate([-w_im, w_re], axis=0))
    own_row = lax.broadcasted_iota(jnp.int32, (128, SEG_LEN), 0) // (2 * width)

    def cancelled(segment, energy):
        taps = taps_of(segment)
        joined = [
            [jnp.concatenate([taps[0][part][piece], taps[1][part][piece]], axis=0) for piece in range(2)]
            for part in range(2)
        ]
        clutter = dot_stacked(on_re, joined[0]) + dot_stacked(on_im, joined[1])
        rest = jnp.concatenate(signal_of(segment), axis=0) - clutter
        residual[segment] = rest
        square = rest * rest
        for tile in range(SEG_LEN // 128):
            energy = energy + square[:, 128 * tile : 128 * tile + 128]
        return energy

    energy = lax.fori_loop(0, segments, cancelled, jnp.zeros((2 * width, 128), jnp.float32), unroll=UNROLL)
    energy = jnp.sum(energy, axis=1, keepdims=True)
    energy = jnp.broadcast_to(energy[:width] + energy[width:], (width, 128))
    energy = jnp.concatenate([energy, jnp.zeros((128 - width, 128), jnp.float32)], axis=0)
    power_z[z] = energy.T[:8]
    to_z = Exchange(ALONG_Z, lambda p: power_z.at[z], lambda p: power_z.at[p], pz_send, pz_recv).start()

    to_far = Exchange(FAR, lambda p: corr.at[p], lambda p: landed.at[p], far_send, far_recv)
    for half in range(2):

        def correlate(segment, total):
            at = pl.ds(pl.multiple_of(segment * SEG_LEN + 256 - 128 * half, 128), SEG_LEN)
            rest = residual[segment]
            swapped = jnp.concatenate([rest[width:], -rest[:width]], axis=0)
            own = own_row == segment
            with_re = halves(jnp.where(own, jnp.concatenate([rest] * segments, axis=0), 0.0))
            with_im = halves(jnp.where(own, jnp.concatenate([swapped] * segments, axis=0), 0.0))
            real_taps = [table[0, piece, :, at] for piece in range(2)]
            imag_taps = [table[1, piece, :, at] for piece in range(2)]
            return total + (dot_beside(real_taps, with_re) + dot_beside(imag_taps, with_im))

        total = lax.fori_loop(0, segments, correlate, blank[0], unroll=UNROLL)
        corr[16 * half : 16 * half + 16] = total.reshape(16, 8, 128)

        def send(p, carry):
            @pl.when(p != far)
            def _():
                to_far.copy(lax.rem(p - far + 32, 32)).start()

            return carry

        lax.fori_loop(16 * half, 16 * half + 16, send, 0)
    landed[far] = corr[far]
    to_z.wait()
    parts = [power_z[i] for i in range(8)]
    power_y[y] = ((parts[0] + parts[1]) + (parts[2] + parts[3])) + ((parts[4] + parts[5]) + (parts[6] + parts[7]))
    to_y = Exchange(ALONG_Y, lambda p: power_y.at[y], lambda p: power_y.at[p], py_send, py_recv).start()
    to_far.wait()
    everything = landed[...]
    for lag in range(8):
        turned[lag] = everything[:, lag, :]
    to_near = Exchange(NEAR, lambda p: turned.at[p], lambda p: cells.at[p], near_send, near_recv).start()
    cells[near] = turned[near]
    to_y.wait()
    power[...] = (power_y[0] + power_y[1]) + (power_y[2] + power_y[3])
    energies[near] = power[...]
    Exchange(NEAR, lambda p: power, lambda p: energies.at[p], pa_send, pa_recv).start().wait()
    to_near.wait()


def cancel(loading, reference, surveillance):
    vmem = pl.BlockSpec(memory_space=pltpu.VMEM)
    length = reference.shape[1]
    width = surveillance.shape[1]
    dma = pltpu.SemaphoreType.DMA

    def block(*shape):
        return pltpu.VMEM(shape, jnp.float32)

    half = (2 * width, 128)
    return pl.pallas_call(
        cancel_kernel,
        out_shape=[
            jax.ShapeDtypeStruct((2 * width, LAGS), jnp.float32),
            jax.ShapeDtypeStruct((8, 32, 128), jnp.float32),
            jax.ShapeDtypeStruct((8, 8, 128), jnp.float32),
        ],
        in_specs=[pl.BlockSpec(memory_space=pltpu.SMEM), vmem, pl.BlockSpec(memory_space=pltpu.HBM)],
        out_specs=[vmem] * 3,
        scratch_shapes=[
            block(*surveillance.shape), dma((1,)),
            pltpu.VMEM((2, 2, 128, LAGS + length), jnp.bfloat16),
            block(2, LAGS), block(2, LAGS), block(2, *half), block(2, 4, 128), block(32, 4, 128),
            block(LAGS, LAGS), block(LAGS, LAGS), block(2, PANEL, LAGS), block(2, PANEL, LAGS),
            block(*half), block(4, *half), block(8, *half), block(2, *half), block(4, 2 * width, SEG_LEN),
            block(32, 8, 128), block(32, 8, 128), block(8, 32, 128), block(8, 128), block(8, 8, 128), block(4, 8, 128),
            dma((2,)), dma((63,)), dma((1,)), dma((2,)), dma((31,)), dma((31,)),
            dma((2,)), dma((3,)), dma((3,)), dma((7,)), dma((7,)), dma((2,)),
            dma((31,)), dma((31,)), dma((7,)), dma((7,)), dma((7,)), dma((7,)), dma((3,)), dma((3,)), dma((7,)), dma((7,)),
        ],
        compiler_params=pltpu.CompilerParams(collective_id=0, has_side_effects=True, vmem_limit_bytes=56200000),
        name="cancel",
    )(loading, reference, surveillance)


def doppler_tables(shards, segments):
    short = DOPP // segments
    order = np.arange(shards).reshape(-1, 2).T.reshape(-1)
    angle = 2.0 * np.pi / short * (np.outer(order, np.arange(short)) % short)
    table = np.concatenate([np.cos(angle), np.sin(angle)], axis=1)
    turn = 2.0 * np.pi / DOPP * np.outer(np.arange(segments), np.arange(DOPP))
    turns = np.stack([np.cos(turn), np.sin(turn)])
    return table.astype(np.float32), turns.astype(np.float32)


def doppler_kernel(samples, weights, cells, energies, table, turns, out, kept):
    near, _, lanes = cells.shape
    groups = near // 2
    segments = turns.shape[1]
    width = lanes // segments // 2
    basis = halves(table[...])
    short = DOPP // segments
    def group(g, carry):
        power = (energies[g] + energies[groups + g]) / samples
        scale = lax.rsqrt(samples * (power + EPSILON))
        by = jnp.broadcast_to(scale[0:1], (128, 128)).T[:width, 0:1]
        rows = jnp.concatenate([cells[g], cells[groups + g]], axis=0)
        wave = dot3(halves(rows.T), basis)
        total_r = total_i = None
        for s in range(segments):
            base = 2 * width * s
            a_r, a_i = wave[base : base + width, :short], wave[base : base + width, short:]
            b_r, b_i = (
                wave[base + width : base + 2 * width, :short],
                wave[base + width : base + 2 * width, short:],
            )
            y_r = (a_r + b_i) * by
            y_i = (b_r - a_i) * by
            y_r = jnp.concatenate([y_r] * segments, axis=1)
            y_i = jnp.concatenate([y_i] * segments, axis=1)
            if s == 0:
                total_r, total_i = y_r, y_i
                continue
            c, d = turns[0, s : s + 1, :], turns[1, s : s + 1, :]
            total_r = total_r + (y_r * c + y_i * d)
            total_i = total_i + (y_i * c - y_r * d)
        at = pl.ds(width * g, width)
        out[0, 0, at, :] = total_r
        out[0, 1, at, :] = total_i
        return carry

    for g in range(groups):
        group(g, 0)
    kept[...] = weights[...]


def doppler(weights, cells, energies, segments, samples):
    vmem = pl.BlockSpec(memory_space=pltpu.VMEM)
    shards = 2 * cells.shape[1]
    table, turns = doppler_tables(shards, segments)
    width = cells.shape[2] // segments // 2
    groups = cells.shape[0] // 2
    return pl.pallas_call(
        functools.partial(doppler_kernel, samples),
        out_shape=[
            jax.ShapeDtypeStruct((1, 2, width * groups, DOPP), jnp.float32),
            jax.ShapeDtypeStruct(weights.shape, jnp.float32),
        ],
        in_specs=[vmem] * 5,
        out_specs=[vmem, vmem],
        compiler_params=pltpu.CompilerParams(vmem_limit_bytes=24 * 2**20),
        name="doppler",
    )(weights, cells, energies, jnp.asarray(table), jnp.asarray(turns))


def per_device(reference_signal, surveillance, loading):
    length = reference_signal.shape[1]
    samples = float(length * lax.axis_size(TM))
    weights, cells, energies = cancel(loading, reference_signal, surveillance)
    full, weights = doppler(weights, cells, energies, length // SEG_LEN, samples)
    return full, jnp.swapaxes(weights.reshape(2, -1, LAGS), 1, 2)


def solution(mesh):
    split = Mesh(
        mesh.devices.reshape(4, 8, 2, mesh.shape["chan"]), ("tm_0", "tm_1", "tm_2", "chan")
    )
    in_specs = (P(None, TM), P(None, "chan", TM), P())
    out_specs = (P(TM_CHAN, None, None, None), P(None, None, "chan"))
    return jax.shard_map(
        per_device, mesh=split, in_specs=in_specs, out_specs=out_specs, check_vma=False
    )
```

```python
import functools

import jax
import jax.numpy as jnp
import numpy as np
from jax import lax
from jax.experimental import pallas as pl
from jax.experimental.pallas import tpu as pltpu
from jax.sharding import Mesh
from jax.sharding import PartitionSpec as P

LAGS = 256
DOPP = 1024
SEG_LEN = 512
TM = ("tm_0", "tm_1", "tm_2")
TM_CHAN = ("tm_0", "tm_1", "tm_2", "chan")
EPSILON = 1e-06
PANEL = 32
UNROLL = 2
PIVOTS = 4
ROWS = 40
MESH = pl.DeviceIdType.MESH

highest = lax.Precision.HIGHEST
NN = (((1,), (0,)), ((), ()))
NT = (((1,), (1,)), ((), ()))


def dot(a, b, dims=NN):
    return lax.dot_general(a, b, dims, precision=highest, preferred_element_type=jnp.float32)


def halves(x):
    high = x.astype(jnp.bfloat16)
    return high, (x - high.astype(jnp.float32)).astype(jnp.bfloat16)


def dot3(a, b, dims=NN):
    def one(x, y):
        return lax.dot_general(x, y, dims, preferred_element_type=jnp.float32)

    return one(a[0], b[0]) + (one(a[0], b[1]) + one(a[1], b[0]))


def dot_beside(a, b):
    both = lax.dot_general(a[0], jnp.concatenate(b, axis=0), NT, preferred_element_type=jnp.float32)
    rest = lax.dot_general(a[1], b[0], NT, preferred_element_type=jnp.float32)
    return both[:, :128] + (both[:, 128:] + rest)


def dot_stacked(a, b):
    rows = a[0].shape[0]
    both = lax.dot_general(jnp.concatenate(a, axis=0), b[0], NN, preferred_element_type=jnp.float32)
    rest = lax.dot_general(a[0], b[1], NN, preferred_element_type=jnp.float32)
    return both[:rows] + (both[rows:] + rest)


def toeplitz(row, rows):
    wide = jnp.broadcast_to(row, (rows, row.shape[1]))
    return pltpu.roll(wide, 0, 1, stride=1, stride_axis=0)


def each(count, act):
    if count == 2:
        act(1)
    else:
        lax.fori_loop(1, count, lambda d, carry: (act(d), carry)[1], 0)


def wrapped(index, count):
    return jnp.where(index >= count, index - count, index)


class Exchange:
    def __init__(self, axes, src, dst, send, recv):
        self.axes, self.src, self.dst, self.send, self.recv = axes, src, dst, send, recv
        self.count = int(np.prod([lax.axis_size(a) for a in axes]))

    def copy(self, d, there=None):
        here = place(self.axes)
        if there is None:
            there = wrapped(here + d, self.count)
        return pltpu.make_async_remote_copy(
            src_ref=self.src(there),
            dst_ref=self.dst(here),
            send_sem=self.send.at[d - 1],
            recv_sem=self.recv.at[d - 1],
            device_id=device(self.axes, there),
            device_id_type=MESH,
        )

    def start(self):
        each(self.count, lambda d: self.copy(d).start())
        return self

    def wait(self):
        partner = wrapped(place(self.axes) + 1, self.count)
        each(self.count, lambda d: self.copy(d, partner).wait())


def place(axes):
    index = lax.axis_index(axes[0])
    for a in axes[1:]:
        index = index * lax.axis_size(a) + lax.axis_index(a)
    return index


def device(axes, index):
    coordinates = {}
    for a in reversed(axes):
        coordinates[a] = lax.rem(index, lax.axis_size(a))
        index = lax.div(index, lax.axis_size(a))
    return coordinates


def greet(barrier, axes, skip=0):
    count = int(np.prod([lax.axis_size(a) for a in axes]))
    here = place(axes)

    def one(d):
        pl.semaphore_signal(
            barrier, inc=1, device_id=device(axes, wrapped(here + d, count)), device_id_type=MESH
        )

    if skip:
        for d in range(1, count):
            if d != skip:
                one(d)
        return count - 2
    each(count, one)
    return count - 1


def times(a, b):
    if a[1] is None and b[1] is None:
        return (a[0] * b[0], None)
    if a[1] is None:
        return (a[0] * b[0], a[0] * b[1])
    if b[1] is None:
        return (a[0] * b[0], a[1] * b[0])
    return (a[0] * b[0] - a[1] * b[1], a[0] * b[1] + a[1] * b[0])


def plus(a, b):
    if a[1] is None:
        return (a[0] + b[0], b[1])
    if b[1] is None:
        return (a[0] + b[0], a[1])
    return (a[0] + b[0], a[1] + b[1])


def minus(a, b):
    return (a[0] - b[0], None if b[1] is None else a[1] - b[1])


def negative(a):
    return (-a[0], None if a[1] is None else -a[1])


def conjugate(a):
    return (a[0], None if a[1] is None else -a[1])


def product(left, right):
    out = []
    for row in left:
        line = []
        for j in range(len(right[0])):
            total = times(row[0], right[0][j])
            for k in range(1, len(row)):
                total = plus(total, times(row[k], right[k][j]))
            line.append(total)
        out.append(line)
    return out


def adjoint(block):
    return [[conjugate(block[j][i]) for j in range(len(block))] for i in range(len(block[0]))]


def hermitian_inverse(block):
    size = len(block)
    if size == 1:
        return [[(1.0 / block[0][0][0], None)]]
    if size == 2:
        a, c, d = block[0][0][0], block[0][1], block[1][1][0]
        scale = 1.0 / (a * d - (c[0] * c[0] + c[1] * c[1]))
        off = (-c[0] * scale, -c[1] * scale)
        return [[(d * scale, None), off], [conjugate(off), (a * scale, None)]]
    half = size // 2
    head = [row[:half] for row in block[:half]]
    side = [row[half:] for row in block[:half]]
    tail = [row[half:] for row in block[half:]]
    head_inverse = hermitian_inverse(head)
    lifted = product(head_inverse, side)
    drop = product(adjoint(side), lifted)
    rest = [[minus(tail[i][j], drop[i][j]) for j in range(half)] for i in range(half)]
    rest_inverse = hermitian_inverse(rest)
    corner = product(lifted, rest_inverse)
    extra = product(corner, adjoint(lifted))
    first = [[plus(head_inverse[i][j], extra[i][j]) for j in range(half)] for i in range(half)]
    right = [[negative(corner[i][j]) for j in range(half)] for i in range(half)]
    below = adjoint(right)
    return [first[i] + right[i] for i in range(half)] + [below[i] + rest_inverse[i] for i in range(half)]


def added(terms):
    while len(terms) > 1:
        terms = [sum(terms[i : i + 2][1:], terms[i]) for i in range(0, len(terms), 2)]
    return terms[0]


def eliminate(real, imag):
    height, n = real.shape
    m = PIVOTS
    lane = lax.broadcasted_iota(jnp.int32, (1, n), 1)
    lanes = lax.broadcasted_iota(jnp.int32, (height, 128), 1)
    rows = lax.broadcasted_iota(jnp.int32, (height, 128), 0)

    def wide(value):
        return None if value is None else jnp.concatenate([value] * (n // 128), axis=1)

    for k in range(0, height, m):
        col_r = [jnp.broadcast_to(real[:, k + j : k + j + 1], (height, 128)) for j in range(m)]
        col_i = [jnp.broadcast_to(imag[:, k + j : k + j + 1], (height, 128)) for j in range(m)]
        block = [
            [(col_r[j][k + i : k + i + 1], col_i[j][k + i : k + i + 1]) for j in range(m)]
            for i in range(m)
        ]
        inverse = [[(wide(q[0]), wide(q[1])) for q in row] for row in hermitian_inverse(block)]
        hit = (lane >= k) & (lane < k + m)
        old = [
            (
                jnp.where(hit, jnp.where(lane == k + i, 1.0, 0.0), real[k + i : k + i + 1]),
                jnp.where(hit, 0.0, imag[k + i : k + i + 1]),
            )
            for i in range(m)
        ]
        new = product(inverse, [[value] for value in old])
        new = [line[0] for line in new]
        inside = (rows >= k) & (rows < k + m)
        col_r = [jnp.where(inside, jnp.where(rows == k + j, -1.0, 0.0), col_r[j]) for j in range(m)]
        col_i = [jnp.where(inside, 0.0, col_i[j]) for j in range(m)]
        gone = inside | ((lanes >= k) & (lanes < k + m))
        out_r, out_i = [], []
        for t in range(n // 128):
            cut = slice(128 * t, 128 * t + 128)
            mask = gone if t == 0 else inside
            next_r = jnp.where(mask, 0.0, real[:, cut])
            next_i = jnp.where(mask, 0.0, imag[:, cut])
            terms_r, terms_i = [], []
            for j in range(m):
                row_r, row_i = new[j][0][:, cut], new[j][1][:, cut]
                terms_r.append(col_r[j] * row_r - col_i[j] * row_i)
                terms_i.append(col_r[j] * row_i + col_i[j] * row_r)
            out_r.append(next_r - added(terms_r))
            out_i.append(next_i - added(terms_i))
        real = jnp.concatenate(out_r, axis=1)
        imag = jnp.concatenate(out_i, axis=1)
    return real, imag


def thirds(x):
    high = x.astype(jnp.bfloat16)
    rest = x - high.astype(jnp.float32)
    middle = rest.astype(jnp.bfloat16)
    return high, middle, (rest - middle.astype(jnp.float32)).astype(jnp.bfloat16)


def packed(factor, top_r, top_i):
    width = 2 * PANEL
    right = jnp.concatenate(
        [jnp.concatenate([top_r, top_i], axis=1), jnp.concatenate([-top_i, top_r], axis=1)], axis=0
    )
    high, middle, low = thirds(right)
    right = jnp.concatenate([high, middle, low, high, middle, high], axis=0)
    high = factor.astype(jnp.bfloat16).astype(jnp.float32)
    rest = factor - high
    middle = rest.astype(jnp.bfloat16).astype(jnp.float32)
    low = rest - middle
    if width < 128:
        parts = [high + pltpu.roll(high, width, 1), high + pltpu.roll(middle, width, 1), middle + pltpu.roll(low, width, 1)]
    else:
        parts = [high, high, high, middle, middle, low]
    left = jnp.concatenate(parts, axis=1).astype(jnp.bfloat16)
    return lax.dot_general(left, right, NN, preferred_element_type=jnp.float32)


def beside(first, second):
    lane = lax.broadcasted_iota(jnp.int32, first.shape, 1)
    both = jnp.where(lane < PANEL, first, pltpu.roll(second, PANEL, 1))
    return jnp.where(lane < 2 * PANEL, both, 0.0)


def invert(real, imag, top, done, between):
    b = PANEL
    panels = LAGS // b

    def turn(x):
        return pltpu.roll(x, LAGS - b, 1)

    def apply(last, live):
        all_r, all_i = real[...], imag[...]
        row = lax.broadcasted_iota(jnp.int32, (LAGS, 128), 0)
        outside = (row < last * b) | (row >= last * b + b)
        if live is not None:
            outside = outside & live
        factor = jnp.where(outside, beside(all_r[:, :128], all_i[:, :128]), 0.0)
        update = packed(factor, done[0], done[1])
        column = lax.broadcasted_iota(jnp.int32, (LAGS, LAGS), 1)
        drop = column < b
        if live is not None:
            drop = drop & live
        real[...] = turn(jnp.where(drop, 0.0, all_r) - update[:, :LAGS])
        imag[...] = turn(jnp.where(drop, 0.0, all_i) - update[:, LAGS:])
        held = pl.ds(pl.multiple_of(last * b, b), b)
        real[held, :] = turn(done[0])
        imag[held, :] = turn(done[1])

    top[0] = real[:b, :]
    top[1] = imag[:b, :]
    real[...] = pltpu.roll(real[...], b, 1)
    imag[...] = pltpu.roll(imag[...], b, 1)
    done[0] = real[LAGS - b :, :]
    done[1] = imag[LAGS - b :, :]

    def panel(index, carry):
        between(index)
        apply(lax.rem(index + panels - 1, panels), index > 0)
        new_r, new_i = eliminate(top[0], top[1])
        held = pl.ds(pl.multiple_of(lax.rem(index + 1, panels) * b, b), b)
        row_r, row_i = real[held, :], imag[held, :]
        update = packed(beside(row_r[:, :128], row_i[:, :128]), new_r, new_i)
        drop = lax.broadcasted_iota(jnp.int32, (b, LAGS), 1) < b
        top[0] = turn(jnp.where(drop, 0.0, row_r) - update[:, :LAGS])
        top[1] = turn(jnp.where(drop, 0.0, row_i) - update[:, LAGS:])
        done[0] = new_r
        done[1] = new_i
        return carry

    lax.fori_loop(0, panels, panel, 0)
    apply(panels - 1, None)


def edge_matrix(tail):
    blank = jnp.zeros((1, LAGS), jnp.float32)
    edge_r = toeplitz(jnp.concatenate([blank, tail[0:1]], axis=1), LAGS)[:, :LAGS]
    edge_i = toeplitz(jnp.concatenate([blank, tail[1:2]], axis=1), LAGS)[:, :LAGS]
    one = jnp.concatenate([edge_r, edge_i], axis=1)
    two = jnp.concatenate([edge_i, -edge_r], axis=1)
    return dot(one, one, NT), dot(one, two, NT)


def normal_matrix(column, edge_r, edge_i, loading):
    i0 = lax.broadcasted_iota(jnp.int32, (LAGS, LAGS), 0)
    i1 = lax.broadcasted_iota(jnp.int32, (LAGS, LAGS), 1)
    flip = jnp.where(i0 + i1 == LAGS - 1, 1.0, 0.0)
    behind = pltpu.roll(dot(column, flip), 1, 1)
    lane = lax.broadcasted_iota(jnp.int32, behind.shape, 1)
    behind = jnp.where(lane == 0, 0.0, behind)
    base_r = toeplitz(jnp.concatenate([column[0:1], behind[0:1]], axis=1), LAGS)[:, :LAGS]
    base_i = toeplitz(jnp.concatenate([-column[1:2], behind[1:2]], axis=1), LAGS)[:, :LAGS]
    diagonal = i0 == i1
    off = jnp.sum(jnp.sum(jnp.where(diagonal, edge_r, 0.0), axis=0, keepdims=True), axis=1, keepdims=True)
    lam = loading * (column[0:1, 0:1] - off / LAGS)
    real = base_r - edge_r
    return jnp.where(diagonal, real + lam, real), base_i - edge_i


PAIR, FAR, NEAR = TM[2:], TM[:2], (TM[2], "chan")
ALONG_Y, ALONG_Z = TM[:1], TM[1:2]


def cancel_kernel(
    loading, reference, surveillance_hbm, weights, cells, energies,
    surveillance, fetch_sem, table, halo, tail, mine, gram_pair, gram_all, real, imag, top, done,
    pair, ring_y, ring_z, cross, residual, corr, landed, turned, power, power_z, power_y,
    edge_sem, tail_send, tail_recv, gram_sem, gram_send, gram_recv,
    pair_sem, y_send, y_recv, z_send, z_recv, out_sem,
    far_send, far_recv, near_send, near_recv, pz_send, pz_recv, py_send, py_recv, pa_send, pa_recv,
):
    length = reference.shape[1]
    width = surveillance.shape[1]
    count = lax.axis_size(TM)
    here = place(TM)
    core, y, z, far, near = place(PAIR), place(ALONG_Y), place(ALONG_Z), place(FAR), place(NEAR)
    fetch = pltpu.make_async_copy(surveillance_hbm, surveillance, fetch_sem.at[0])
    fetch.start()
    barrier = pltpu.get_barrier_semaphore()
    total = greet(barrier, TM)
    total += greet(barrier, NEAR, 4)

    def fill(tile, windows):
        delayed = [toeplitz(x, 128)[:, 128:] for x in windows]
        at = pl.ds(pl.multiple_of(128 * tile, 128), 128)
        for part in range(2):
            high, low = halves(delayed[part])
            table[part, 0, :, at] = high
            table[part, 1, :, at] = low
        return delayed

    def lagged(delayed, start):
        now = reference[:, pl.ds(pl.multiple_of(start, 128), 128)]
        now_r, now_i = now[0:1], now[1:2]
        return (delayed[0] * now_r + delayed[1] * now_i, delayed[0] * now_i - delayed[1] * now_r)

    def plus_all(sums, terms):
        return tuple(x + y for x, y in zip(sums, terms))

    tiles = (LAGS + length) // 128

    def fill_inner(tile, sums):
        start = pl.multiple_of(128 * tile - 384, 128)
        window = reference[:, pl.ds(start, LAGS)]
        delayed = fill(tile, [window[0:1], window[1:2]])
        return (
            plus_all(sums[0], lagged(delayed, 128 * tile - 256)),
            plus_all(sums[1], lagged(delayed, 128 * tile - 128)),
        )

    blank = (jnp.zeros((128, 128), jnp.float32),) * 2
    sums = lax.fori_loop(3, tiles - 1, fill_inner, (blank, blank))
    window = reference[:, length - LAGS :]
    delayed = fill(tiles - 1, [window[0:1], window[1:2]])
    sums = [plus_all(sums[0], lagged(delayed, length - 128)), sums[1]]

    pl.semaphore_wait(barrier, total)
    forward = pltpu.make_async_remote_copy(
        src_ref=reference.at[:, pl.ds(length - LAGS, LAGS)],
        dst_ref=halo,
        send_sem=edge_sem.at[0],
        recv_sem=edge_sem.at[1],
        device_id=device(TM, lax.rem(here + 1, count)),
        device_id_type=MESH,
    )
    forward.start()

    def tail_copy(d):
        return pltpu.make_async_remote_copy(
            src_ref=reference.at[:, pl.ds(length - LAGS, LAGS)],
            dst_ref=tail,
            send_sem=tail_send.at[d - 1],
            recv_sem=tail_recv.at[0],
            device_id=device(TM, lax.rem(here + d, count)),
            device_id_type=MESH,
        )

    @pl.when(here == count - 1)
    def _():
        tail[...] = reference[:, length - LAGS :]
        each(count, lambda d: tail_copy(d).start())

    forward.wait()
    before = jnp.where(here > 0, halo[...], 0.0)
    delayed = fill(1, [before[0:1], before[1:2]])
    sums[1] = plus_all(sums[1], lagged(delayed, 0))
    joint = jnp.concatenate([before[:, 128:], reference[:, :128]], axis=1)
    delayed = fill(2, [joint[0:1], joint[1:2]])
    sums[0] = plus_all(sums[0], lagged(delayed, 0))
    sums[1] = plus_all(sums[1], lagged(delayed, 128))
    for half in range(2):
        for part in range(2):
            line = jnp.sum(sums[half][part].T, axis=0, keepdims=True)
            gram_pair[0, 2 * part + half : 2 * part + half + 1, :] = line
    Exchange(PAIR, lambda p: gram_pair.at[0], lambda p: gram_pair.at[1], gram_sem.at[0:1], gram_sem.at[1:2]).start().wait()
    gram_all[far] = gram_pair[0] + gram_pair[1]
    to_gram = Exchange(FAR, lambda p: gram_all.at[far], lambda p: gram_all.at[p], gram_send, gram_recv).start()

    fetch.wait()
    segments = length // SEG_LEN

    def taps_of(segment):
        taps = []
        for half in range(2):
            at = pl.ds(pl.multiple_of(segment * SEG_LEN + 256 - 128 * half, 128), SEG_LEN)
            taps.append([[table[part, piece, :, at] for piece in range(2)] for part in range(2)])
        return taps

    def signal_of(segment):
        at = pl.ds(pl.multiple_of(segment * SEG_LEN, 128), SEG_LEN)
        return surveillance[0, :, at], surveillance[1, :, at]

    def cross_terms(segment, total):
        s_re, s_im = signal_of(segment)
        zero = jnp.zeros((128 - 2 * width, SEG_LEN), jnp.float32)
        with_re = halves(jnp.concatenate([s_re, s_im, zero], axis=0))
        with_im = halves(jnp.concatenate([s_im, -s_re, zero], axis=0))
        return tuple(
            x + (dot_beside(taps[0], with_re) + dot_beside(taps[1], with_im))
            for x, taps in zip(total, taps_of(segment))
        )

    product = lax.fori_loop(0, segments, cross_terms, blank, unroll=UNROLL)
    for half in range(2):
        mine[half] = product[half].T[: 2 * width]
    to_pair = Exchange(PAIR, lambda p: mine.at[p], lambda p: pair, pair_sem.at[0:1], pair_sem.at[1:2]).start()

    @pl.when(here == count - 1)
    def _():
        each(count, lambda d: tail_copy(d).wait_send())

    @pl.when(here != count - 1)
    def _():
        tail_copy(1).wait_recv()

    edge_r, edge_i = edge_matrix(tail[...])
    real[...] = edge_r
    imag[...] = edge_i
    along_y = Exchange(ALONG_Y, lambda p: ring_y.at[y], lambda p: ring_y.at[p], y_send, y_recv)
    to_pair.wait()
    ring_y[y] = mine[core] + pair[...]
    along_y.start()
    to_gram.wait()
    gram = jnp.sum(gram_all[...], axis=0)
    column = jnp.concatenate([gram[0:1], gram[1:2]], axis=1)
    column = jnp.concatenate([column, jnp.concatenate([gram[2:3], gram[3:4]], axis=1)], axis=0)
    column = jnp.concatenate([column, jnp.zeros((6, LAGS), jnp.float32)], axis=0)
    start_r, start_i = normal_matrix(column, real[...], imag[...], loading[0])
    real[...] = start_r
    imag[...] = start_i

    along_z = Exchange(ALONG_Z, lambda p: ring_z.at[z], lambda p: ring_z.at[p], z_send, z_recv)
    out = Exchange(PAIR, lambda p: cross.at[core], lambda p: cross.at[p], out_sem.at[0:1], out_sem.at[1:2])

    def between(index):
        @pl.when(index == 2)
        def _():
            along_y.wait()
            ring_z[z] = (ring_y[0] + ring_y[1]) + (ring_y[2] + ring_y[3])
            along_z.start()

        @pl.when(index == 6)
        def _():
            along_z.wait()
            cross[core] = ((ring_z[0] + ring_z[1]) + (ring_z[2] + ring_z[3])) + (
                (ring_z[4] + ring_z[5]) + (ring_z[6] + ring_z[7])
            )
            out.start()

    invert(real, imag, top, done, between)
    out.wait()
    right = jnp.concatenate([cross[0], cross[1]], axis=1)
    spun = jnp.concatenate([-right[width:], right[:width]], axis=0)
    w = dot(right, real[...], NT) + dot(spun, imag[...], NT)
    weights[...] = w

    w_re, w_im = w[:width], w[width:]
    on_re = halves(w)
    on_im = halves(jnp.concatenate([-w_im, w_re], axis=0))
    own_row = lax.broadcasted_iota(jnp.int32, (128, SEG_LEN), 0) // (2 * width)

    def cancelled(segment, energy):
        taps = taps_of(segment)
        joined = [
            [jnp.concatenate([taps[0][part][piece], taps[1][part][piece]], axis=0) for piece in range(2)]
            for part in range(2)
        ]
        clutter = dot_stacked(on_re, joined[0]) + dot_stacked(on_im, joined[1])
        rest = jnp.concatenate(signal_of(segment), axis=0) - clutter
        residual[segment] = rest
        square = rest * rest
        for tile in range(SEG_LEN // 128):
            energy = energy + square[:, 128 * tile : 128 * tile + 128]
        return energy

    energy = lax.fori_loop(0, segments, cancelled, jnp.zeros((2 * width, 128), jnp.float32), unroll=UNROLL)
    energy = jnp.sum(energy, axis=1, keepdims=True)
    energy = jnp.broadcast_to(energy[:width] + energy[width:], (width, 128))
    energy = jnp.concatenate([energy, jnp.zeros((128 - width, 128), jnp.float32)], axis=0)
    power_z[z] = energy.T[:8]
    to_z = Exchange(ALONG_Z, lambda p: power_z.at[z], lambda p: power_z.at[p], pz_send, pz_recv).start()

    to_far = Exchange(FAR, lambda p: corr.at[p], lambda p: landed.at[p], far_send, far_recv)
    for half in range(2):

        def correlate(segment, total):
            at = pl.ds(pl.multiple_of(segment * SEG_LEN + 256 - 128 * half, 128), SEG_LEN)
            rest = residual[segment]
            swapped = jnp.concatenate([rest[width:], -rest[:width]], axis=0)
            own = own_row == segment
            with_re = halves(jnp.where(own, jnp.concatenate([rest] * segments, axis=0), 0.0))
            with_im = halves(jnp.where(own, jnp.concatenate([swapped] * segments, axis=0), 0.0))
            real_taps = [table[0, piece, :, at] for piece in range(2)]
            imag_taps = [table[1, piece, :, at] for piece in range(2)]
            return total + (dot_beside(real_taps, with_re) + dot_beside(imag_taps, with_im))

        total = lax.fori_loop(0, segments, correlate, blank[0], unroll=UNROLL)
        corr[16 * half : 16 * half + 16] = total.reshape(16, 8, 128)

        def send(p, carry):
            @pl.when(p != far)
            def _():
                to_far.copy(lax.rem(p - far + 32, 32)).start()

            return carry

        lax.fori_loop(16 * half, 16 * half + 16, send, 0)
    landed[far] = corr[far]
    to_z.wait()
    parts = [power_z[i] for i in range(8)]
    power_y[y] = ((parts[0] + parts[1]) + (parts[2] + parts[3])) + ((parts[4] + parts[5]) + (parts[6] + parts[7]))
    to_y = Exchange(ALONG_Y, lambda p: power_y.at[y], lambda p: power_y.at[p], py_send, py_recv).start()
    to_far.wait()
    everything = landed[...]
    for lag in range(8):
        turned[lag] = everything[:, lag, :]
    to_near = Exchange(NEAR, lambda p: turned.at[p], lambda p: cells.at[p], near_send, near_recv).start()
    cells[near] = turned[near]
    to_y.wait()
    power[...] = (power_y[0] + power_y[1]) + (power_y[2] + power_y[3])
    energies[near] = power[...]
    Exchange(NEAR, lambda p: power, lambda p: energies.at[p], pa_send, pa_recv).start().wait()
    to_near.wait()


def cancel(loading, reference, surveillance):
    vmem = pl.BlockSpec(memory_space=pltpu.VMEM)
    length = reference.shape[1]
    width = surveillance.shape[1]
    dma = pltpu.SemaphoreType.DMA

    def block(*shape):
        return pltpu.VMEM(shape, jnp.float32)

    half = (2 * width, 128)
    return pl.pallas_call(
        cancel_kernel,
        out_shape=[
            jax.ShapeDtypeStruct((2 * width, LAGS), jnp.float32),
            jax.ShapeDtypeStruct((8, 32, 128), jnp.float32),
            jax.ShapeDtypeStruct((8, 8, 128), jnp.float32),
        ],
        in_specs=[pl.BlockSpec(memory_space=pltpu.SMEM), vmem, pl.BlockSpec(memory_space=pltpu.HBM)],
        out_specs=[vmem] * 3,
        scratch_shapes=[
            block(*surveillance.shape), dma((1,)),
            pltpu.VMEM((2, 2, 128, LAGS + length), jnp.bfloat16),
            block(2, LAGS), block(2, LAGS), block(2, *half), block(2, 4, 128), block(32, 4, 128),
            block(LAGS, LAGS), block(LAGS, LAGS), block(2, PANEL, LAGS), block(2, PANEL, LAGS),
            block(*half), block(4, *half), block(8, *half), block(2, *half), block(4, 2 * width, SEG_LEN),
            block(32, 8, 128), block(32, 8, 128), block(8, 32, 128), block(8, 128), block(8, 8, 128), block(4, 8, 128),
            dma((2,)), dma((63,)), dma((1,)), dma((2,)), dma((31,)), dma((31,)),
            dma((2,)), dma((3,)), dma((3,)), dma((7,)), dma((7,)), dma((2,)),
            dma((31,)), dma((31,)), dma((7,)), dma((7,)), dma((7,)), dma((7,)), dma((3,)), dma((3,)), dma((7,)), dma((7,)),
        ],
        compiler_params=pltpu.CompilerParams(collective_id=0, has_side_effects=True, vmem_limit_bytes=56200000),
        name="cancel",
    )(loading, reference, surveillance)


def doppler_tables(shards, segments):
    short = DOPP // segments
    order = np.arange(shards).reshape(-1, 2).T.reshape(-1)
    angle = 2.0 * np.pi / short * (np.outer(order, np.arange(short)) % short)
    table = np.concatenate([np.cos(angle), np.sin(angle)], axis=1)
    turn = 2.0 * np.pi / DOPP * np.outer(np.arange(segments), np.arange(DOPP))
    turns = np.stack([np.cos(turn), np.sin(turn)])
    return table.astype(np.float32), turns.astype(np.float32)


def doppler_kernel(samples, weights, cells, energies, table, turns, out, kept):
    near, _, lanes = cells.shape
    groups = near // 2
    segments = turns.shape[1]
    width = lanes // segments // 2
    basis = halves(table[...])
    short = DOPP // segments
    def group(g, carry):
        power = (energies[g] + energies[groups + g]) / samples
        scale = lax.rsqrt(samples * (power + EPSILON))
        by = jnp.broadcast_to(scale[0:1], (128, 128)).T[:width, 0:1]
        rows = jnp.concatenate([cells[g], cells[groups + g]], axis=0)
        wave = dot3(halves(rows.T), basis)
        total_r = total_i = None
        for s in range(segments):
            base = 2 * width * s
            a_r, a_i = wave[base : base + width, :short], wave[base : base + width, short:]
            b_r, b_i = (
                wave[base + width : base + 2 * width, :short],
                wave[base + width : base + 2 * width, short:],
            )
            y_r = (a_r + b_i) * by
            y_i = (b_r - a_i) * by
            y_r = jnp.concatenate([y_r] * segments, axis=1)
            y_i = jnp.concatenate([y_i] * segments, axis=1)
            if s == 0:
                total_r, total_i = y_r, y_i
                continue
            c, d = turns[0, s : s + 1, :], turns[1, s : s + 1, :]
            total_r = total_r + (y_r * c + y_i * d)
            total_i = total_i + (y_i * c - y_r * d)
        at = pl.ds(width * g, width)
        out[0, 0, at, :] = total_r
        out[0, 1, at, :] = total_i
        return carry

    for g in range(groups):
        group(g, 0)
    kept[...] = weights[...]


def doppler(weights, cells, energies, segments, samples):
    vmem = pl.BlockSpec(memory_space=pltpu.VMEM)
    shards = 2 * cells.shape[1]
    table, turns = doppler_tables(shards, segments)
    width = cells.shape[2] // segments // 2
    groups = cells.shape[0] // 2
    return pl.pallas_call(
        functools.partial(doppler_kernel, samples),
        out_shape=[
            jax.ShapeDtypeStruct((1, 2, width * groups, DOPP), jnp.float32),
            jax.ShapeDtypeStruct(weights.shape, jnp.float32),
        ],
        in_specs=[vmem] * 5,
        out_specs=[vmem, vmem],
        compiler_params=pltpu.CompilerParams(vmem_limit_bytes=24 * 2**20),
        name="doppler",
    )(weights, cells, energies, jnp.asarray(table), jnp.asarray(turns))


def per_device(reference_signal, surveillance, loading):
    length = reference_signal.shape[1]
    samples = float(length * lax.axis_size(TM))
    weights, cells, energies = cancel(loading, reference_signal, surveillance)
    full, weights = doppler(weights, cells, energies, length // SEG_LEN, samples)
    return full, jnp.swapaxes(weights.reshape(2, -1, LAGS), 1, 2)


def solution(mesh):
    split = Mesh(
        mesh.devices.reshape(4, 8, 2, mesh.shape["chan"]), ("tm_0", "tm_1", "tm_2", "chan")
    )
    in_specs = (P(None, TM), P(None, "chan", TM), P())
    out_specs = (P(TM_CHAN, None, None, None), P(None, None, "chan"))
    return jax.shard_map(
        per_device, mesh=split, in_specs=in_specs, out_specs=out_specs, check_vma=False
    )
```

```python
import functools

import jax
import jax.numpy as jnp
import numpy as np
from jax import lax
from jax.experimental import pallas as pl
from jax.experimental.pallas import tpu as pltpu
from jax.sharding import Mesh
from jax.sharding import PartitionSpec as P

LAGS = 256
DOPP = 1024
SEG_LEN = 512
TM = ("tm_0", "tm_1", "tm_2")
TM_CHAN = ("tm_0", "tm_1", "tm_2", "chan")
EPSILON = 1e-06
PANEL = 32
UNROLL = 2
PIVOTS = 4
ROWS = 40
MESH = pl.DeviceIdType.MESH

highest = lax.Precision.HIGHEST
NN = (((1,), (0,)), ((), ()))
NT = (((1,), (1,)), ((), ()))


def dot(a, b, dims=NN):
    return lax.dot_general(a, b, dims, precision=highest, preferred_element_type=jnp.float32)


def halves(x):
    high = x.astype(jnp.bfloat16)
    return high, (x - high.astype(jnp.float32)).astype(jnp.bfloat16)


def dot3(a, b, dims=NN):
    def one(x, y):
        return lax.dot_general(x, y, dims, preferred_element_type=jnp.float32)

    return one(a[0], b[0]) + (one(a[0], b[1]) + one(a[1], b[0]))


def dot_beside(a, b):
    both = lax.dot_general(a[0], jnp.concatenate(b, axis=0), NT, preferred_element_type=jnp.float32)
    rest = lax.dot_general(a[1], b[0], NT, preferred_element_type=jnp.float32)
    return both[:, :128] + (both[:, 128:] + rest)


def dot_stacked(a, b):
    rows = a[0].shape[0]
    both = lax.dot_general(jnp.concatenate(a, axis=0), b[0], NN, preferred_element_type=jnp.float32)
    rest = lax.dot_general(a[0], b[1], NN, preferred_element_type=jnp.float32)
    return both[:rows] + (both[rows:] + rest)


def toeplitz(row, rows):
    wide = jnp.broadcast_to(row, (rows, row.shape[1]))
    return pltpu.roll(wide, 0, 1, stride=1, stride_axis=0)


def each(count, act):
    if count == 2:
        act(1)
    else:
        lax.fori_loop(1, count, lambda d, carry: (act(d), carry)[1], 0)


class Exchange:
    def __init__(self, axes, src, dst, send, recv):
        self.axes, self.src, self.dst, self.send, self.recv = axes, src, dst, send, recv
        self.count = int(np.prod([lax.axis_size(a) for a in axes]))

    def copy(self, d):
        here = place(self.axes)
        there = lax.rem(here + d, self.count)
        return pltpu.make_async_remote_copy(
            src_ref=self.src(there),
            dst_ref=self.dst(here),
            send_sem=self.send.at[d - 1],
            recv_sem=self.recv.at[d - 1],
            device_id=device(self.axes, there),
            device_id_type=MESH,
        )

    def start(self):
        each(self.count, lambda d: self.copy(d).start())
        return self

    def wait(self):
        each(self.count, lambda d: self.copy(d).wait())


def place(axes):
    index = lax.axis_index(axes[0])
    for a in axes[1:]:
        index = index * lax.axis_size(a) + lax.axis_index(a)
    return index


def device(axes, index):
    coordinates = {}
    for a in reversed(axes):
        coordinates[a] = lax.rem(index, lax.axis_size(a))
        index = lax.div(index, lax.axis_size(a))
    return coordinates


def greet(barrier, axes, skip=0):
    count = int(np.prod([lax.axis_size(a) for a in axes]))
    here = place(axes)

    def one(d):
        pl.semaphore_signal(
            barrier, inc=1, device_id=device(axes, lax.rem(here + d, count)), device_id_type=MESH
        )

    if skip:
        for d in range(1, count):
            if d != skip:
                one(d)
        return count - 2
    each(count, one)
    return count - 1


def times(a, b):
    if a[1] is None and b[1] is None:
        return (a[0] * b[0], None)
    if a[1] is None:
        return (a[0] * b[0], a[0] * b[1])
    if b[1] is None:
        return (a[0] * b[0], a[1] * b[0])
    return (a[0] * b[0] - a[1] * b[1], a[0] * b[1] + a[1] * b[0])


def plus(a, b):
    if a[1] is None:
        return (a[0] + b[0], b[1])
    if b[1] is None:
        return (a[0] + b[0], a[1])
    return (a[0] + b[0], a[1] + b[1])


def minus(a, b):
    return (a[0] - b[0], None if b[1] is None else a[1] - b[1])


def negative(a):
    return (-a[0], None if a[1] is None else -a[1])


def conjugate(a):
    return (a[0], None if a[1] is None else -a[1])


def product(left, right):
    out = []
    for row in left:
        line = []
        for j in range(len(right[0])):
            total = times(row[0], right[0][j])
            for k in range(1, len(row)):
                total = plus(total, times(row[k], right[k][j]))
            line.append(total)
        out.append(line)
    return out


def adjoint(block):
    return [[conjugate(block[j][i]) for j in range(len(block))] for i in range(len(block[0]))]


def hermitian_inverse(block):
    size = len(block)
    if size == 1:
        return [[(1.0 / block[0][0][0], None)]]
    if size == 2:
        a, c, d = block[0][0][0], block[0][1], block[1][1][0]
        scale = 1.0 / (a * d - (c[0] * c[0] + c[1] * c[1]))
        off = (-c[0] * scale, -c[1] * scale)
        return [[(d * scale, None), off], [conjugate(off), (a * scale, None)]]
    half = size // 2
    head = [row[:half] for row in block[:half]]
    side = [row[half:] for row in block[:half]]
    tail = [row[half:] for row in block[half:]]
    head_inverse = hermitian_inverse(head)
    lifted = product(head_inverse, side)
    drop = product(adjoint(side), lifted)
    rest = [[minus(tail[i][j], drop[i][j]) for j in range(half)] for i in range(half)]
    rest_inverse = hermitian_inverse(rest)
    corner = product(lifted, rest_inverse)
    extra = product(corner, adjoint(lifted))
    first = [[plus(head_inverse[i][j], extra[i][j]) for j in range(half)] for i in range(half)]
    right = [[negative(corner[i][j]) for j in range(half)] for i in range(half)]
    below = adjoint(right)
    return [first[i] + right[i] for i in range(half)] + [below[i] + rest_inverse[i] for i in range(half)]


def added(terms):
    while len(terms) > 1:
        terms = [sum(terms[i : i + 2][1:], terms[i]) for i in range(0, len(terms), 2)]
    return terms[0]


def eliminate(real, imag):
    height, n = real.shape
    m = PIVOTS
    lane = lax.broadcasted_iota(jnp.int32, (1, n), 1)
    lanes = lax.broadcasted_iota(jnp.int32, (height, 128), 1)
    rows = lax.broadcasted_iota(jnp.int32, (height, 128), 0)

    def wide(value):
        return None if value is None else jnp.concatenate([value] * (n // 128), axis=1)

    for k in range(0, height, m):
        col_r = [jnp.broadcast_to(real[:, k + j : k + j + 1], (height, 128)) for j in range(m)]
        col_i = [jnp.broadcast_to(imag[:, k + j : k + j + 1], (height, 128)) for j in range(m)]
        block = [
            [(col_r[j][k + i : k + i + 1], col_i[j][k + i : k + i + 1]) for j in range(m)]
            for i in range(m)
        ]
        inverse = [[(wide(q[0]), wide(q[1])) for q in row] for row in hermitian_inverse(block)]
        hit = (lane >= k) & (lane < k + m)
        old = [
            (
                jnp.where(hit, jnp.where(lane == k + i, 1.0, 0.0), real[k + i : k + i + 1]),
                jnp.where(hit, 0.0, imag[k + i : k + i + 1]),
            )
            for i in range(m)
        ]
        new = product(inverse, [[value] for value in old])
        new = [line[0] for line in new]
        inside = (rows >= k) & (rows < k + m)
        col_r = [jnp.where(inside, jnp.where(rows == k + j, -1.0, 0.0), col_r[j]) for j in range(m)]
        col_i = [jnp.where(inside, 0.0, col_i[j]) for j in range(m)]
        gone = inside | ((lanes >= k) & (lanes < k + m))
        out_r, out_i = [], []
        for t in range(n // 128):
            cut = slice(128 * t, 128 * t + 128)
            mask = gone if t == 0 else inside
            next_r = jnp.where(mask, 0.0, real[:, cut])
            next_i = jnp.where(mask, 0.0, imag[:, cut])
            terms_r, terms_i = [], []
            for j in range(m):
                row_r, row_i = new[j][0][:, cut], new[j][1][:, cut]
                terms_r.append(col_r[j] * row_r - col_i[j] * row_i)
                terms_i.append(col_r[j] * row_i + col_i[j] * row_r)
            out_r.append(next_r - added(terms_r))
            out_i.append(next_i - added(terms_i))
        real = jnp.concatenate(out_r, axis=1)
        imag = jnp.concatenate(out_i, axis=1)
    return real, imag


def thirds(x):
    high = x.astype(jnp.bfloat16)
    rest = x - high.astype(jnp.float32)
    middle = rest.astype(jnp.bfloat16)
    return high, middle, (rest - middle.astype(jnp.float32)).astype(jnp.bfloat16)


def packed(factor, top_r, top_i):
    width = 2 * PANEL
    right = jnp.concatenate(
        [jnp.concatenate([top_r, top_i], axis=1), jnp.concatenate([-top_i, top_r], axis=1)], axis=0
    )
    high, middle, low = thirds(right)
    right = jnp.concatenate([high, middle, low, high, middle, high], axis=0)
    high = factor.astype(jnp.bfloat16).astype(jnp.float32)
    rest = factor - high
    middle = rest.astype(jnp.bfloat16).astype(jnp.float32)
    low = rest - middle
    if width < 128:
        parts = [high + pltpu.roll(high, width, 1), high + pltpu.roll(middle, width, 1), middle + pltpu.roll(low, width, 1)]
    else:
        parts = [high, high, high, middle, middle, low]
    left = jnp.concatenate(parts, axis=1).astype(jnp.bfloat16)
    return lax.dot_general(left, right, NN, preferred_element_type=jnp.float32)


def beside(first, second):
    lane = lax.broadcasted_iota(jnp.int32, first.shape, 1)
    both = jnp.where(lane < PANEL, first, pltpu.roll(second, PANEL, 1))
    return jnp.where(lane < 2 * PANEL, both, 0.0)


def invert(real, imag, top, done, between):
    b = PANEL
    panels = LAGS // b

    def turn(x):
        return pltpu.roll(x, LAGS - b, 1)

    def apply(last, live):
        all_r, all_i = real[...], imag[...]
        row = lax.broadcasted_iota(jnp.int32, (LAGS, 128), 0)
        outside = (row < last * b) | (row >= last * b + b)
        if live is not None:
            outside = outside & live
        factor = jnp.where(outside, beside(all_r[:, :128], all_i[:, :128]), 0.0)
        update = packed(factor, done[0], done[1])
        column = lax.broadcasted_iota(jnp.int32, (LAGS, LAGS), 1)
        drop = column < b
        if live is not None:
            drop = drop & live
        real[...] = turn(jnp.where(drop, 0.0, all_r) - update[:, :LAGS])
        imag[...] = turn(jnp.where(drop, 0.0, all_i) - update[:, LAGS:])
        held = pl.ds(pl.multiple_of(last * b, b), b)
        real[held, :] = turn(done[0])
        imag[held, :] = turn(done[1])

    top[0] = real[:b, :]
    top[1] = imag[:b, :]
    real[...] = pltpu.roll(real[...], b, 1)
    imag[...] = pltpu.roll(imag[...], b, 1)
    done[0] = real[LAGS - b :, :]
    done[1] = imag[LAGS - b :, :]

    def panel(index, carry):
        between(index)
        apply(lax.rem(index + panels - 1, panels), index > 0)
        new_r, new_i = eliminate(top[0], top[1])
        held = pl.ds(pl.multiple_of(lax.rem(index + 1, panels) * b, b), b)
        row_r, row_i = real[held, :], imag[held, :]
        update = packed(beside(row_r[:, :128], row_i[:, :128]), new_r, new_i)
        drop = lax.broadcasted_iota(jnp.int32, (b, LAGS), 1) < b
        top[0] = turn(jnp.where(drop, 0.0, row_r) - update[:, :LAGS])
        top[1] = turn(jnp.where(drop, 0.0, row_i) - update[:, LAGS:])
        done[0] = new_r
        done[1] = new_i
        return carry

    lax.fori_loop(0, panels, panel, 0)
    apply(panels - 1, None)


def edge_matrix(tail):
    blank = jnp.zeros((1, LAGS), jnp.float32)
    edge_r = toeplitz(jnp.concatenate([blank, tail[0:1]], axis=1), LAGS)[:, :LAGS]
    edge_i = toeplitz(jnp.concatenate([blank, tail[1:2]], axis=1), LAGS)[:, :LAGS]
    one = jnp.concatenate([edge_r, edge_i], axis=1)
    two = jnp.concatenate([edge_i, -edge_r], axis=1)
    return dot(one, one, NT), dot(one, two, NT)


def normal_matrix(column, edge_r, edge_i, loading):
    i0 = lax.broadcasted_iota(jnp.int32, (LAGS, LAGS), 0)
    i1 = lax.broadcasted_iota(jnp.int32, (LAGS, LAGS), 1)
    flip = jnp.where(i0 + i1 == LAGS - 1, 1.0, 0.0)
    flip = flip.astype(jnp.bfloat16)
    turned = [lax.dot_general(x, flip, NN, preferred_element_type=jnp.float32) for x in thirds(column)]
    behind = pltpu.roll(turned[0] + (turned[1] + turned[2]), 1, 1)
    lane = lax.broadcasted_iota(jnp.int32, behind.shape, 1)
    behind = jnp.where(lane == 0, 0.0, behind)
    base_r = toeplitz(jnp.concatenate([column[0:1], behind[0:1]], axis=1), LAGS)[:, :LAGS]
    base_i = toeplitz(jnp.concatenate([-column[1:2], behind[1:2]], axis=1), LAGS)[:, :LAGS]
    diagonal = i0 == i1
    off = jnp.sum(jnp.sum(jnp.where(diagonal, edge_r, 0.0), axis=0, keepdims=True), axis=1, keepdims=True)
    lam = loading * (column[0:1, 0:1] - off / LAGS)
    real = base_r - edge_r
    return jnp.where(diagonal, real + lam, real), base_i - edge_i


PAIR, FAR, NEAR = TM[2:], TM[:2], (TM[2], "chan")
ALONG_Y, ALONG_Z = TM[:1], TM[1:2]


def cancel_kernel(
    loading, reference, surveillance_hbm, weights, cells, energies,
    surveillance, fetch_sem, table, halo, tail, mine, gram_pair, gram_all, real, imag, top, done,
    pair, ring_y, ring_z, cross, residual, corr, landed, turned, power, power_z, power_y,
    edge_sem, tail_send, tail_recv, gram_sem, gram_send, gram_recv,
    pair_sem, y_send, y_recv, z_send, z_recv, out_sem,
    far_send, far_recv, near_send, near_recv, pz_send, pz_recv, py_send, py_recv, pa_send, pa_recv,
):
    length = reference.shape[1]
    width = surveillance.shape[1]
    count = lax.axis_size(TM)
    here = place(TM)
    core, y, z, far, near = place(PAIR), place(ALONG_Y), place(ALONG_Z), place(FAR), place(NEAR)
    fetch = pltpu.make_async_copy(surveillance_hbm, surveillance, fetch_sem.at[0])
    fetch.start()
    barrier = pltpu.get_barrier_semaphore()
    total = greet(barrier, TM)
    total += greet(barrier, NEAR, 4)

    def fill(tile, windows):
        delayed = [toeplitz(x, 128)[:, 128:] for x in windows]
        at = pl.ds(pl.multiple_of(128 * tile, 128), 128)
        for part in range(2):
            high, low = halves(delayed[part])
            table[part, 0, :, at] = high
            table[part, 1, :, at] = low
        return delayed

    def lagged(delayed, start):
        now = reference[:, pl.ds(pl.multiple_of(start, 128), 128)]
        now_r, now_i = now[0:1], now[1:2]
        return (delayed[0] * now_r + delayed[1] * now_i, delayed[0] * now_i - delayed[1] * now_r)

    def plus_all(sums, terms):
        return tuple(x + y for x, y in zip(sums, terms))

    tiles = (LAGS + length) // 128

    def fill_inner(tile, sums):
        start = pl.multiple_of(128 * tile - 384, 128)
        window = reference[:, pl.ds(start, LAGS)]
        delayed = fill(tile, [window[0:1], window[1:2]])
        return (
            plus_all(sums[0], lagged(delayed, 128 * tile - 256)),
            plus_all(sums[1], lagged(delayed, 128 * tile - 128)),
        )

    blank = (jnp.zeros((128, 128), jnp.float32),) * 2
    sums = lax.fori_loop(3, tiles - 1, fill_inner, (blank, blank))
    window = reference[:, length - LAGS :]
    delayed = fill(tiles - 1, [window[0:1], window[1:2]])
    sums = [plus_all(sums[0], lagged(delayed, length - 128)), sums[1]]

    pl.semaphore_wait(barrier, total)
    forward = pltpu.make_async_remote_copy(
        src_ref=reference.at[:, pl.ds(length - LAGS, LAGS)],
        dst_ref=halo,
        send_sem=edge_sem.at[0],
        recv_sem=edge_sem.at[1],
        device_id=device(TM, lax.rem(here + 1, count)),
        device_id_type=MESH,
    )
    forward.start()

    def tail_copy(d):
        return pltpu.make_async_remote_copy(
            src_ref=reference.at[:, pl.ds(length - LAGS, LAGS)],
            dst_ref=tail,
            send_sem=tail_send.at[d - 1],
            recv_sem=tail_recv.at[0],
            device_id=device(TM, lax.rem(here + d, count)),
            device_id_type=MESH,
        )

    @pl.when(here == count - 1)
    def _():
        tail[...] = reference[:, length - LAGS :]
        each(count, lambda d: tail_copy(d).start())

    forward.wait()
    before = jnp.where(here > 0, halo[...], 0.0)
    delayed = fill(1, [before[0:1], before[1:2]])
    sums[1] = plus_all(sums[1], lagged(delayed, 0))
    joint = jnp.concatenate([before[:, 128:], reference[:, :128]], axis=1)
    delayed = fill(2, [joint[0:1], joint[1:2]])
    sums[0] = plus_all(sums[0], lagged(delayed, 0))
    sums[1] = plus_all(sums[1], lagged(delayed, 128))
    for half in range(2):
        for part in range(2):
            line = jnp.sum(sums[half][part].T, axis=0, keepdims=True)
            gram_pair[0, 2 * part + half : 2 * part + half + 1, :] = line
    Exchange(PAIR, lambda p: gram_pair.at[0], lambda p: gram_pair.at[1], gram_sem.at[0:1], gram_sem.at[1:2]).start().wait()
    gram_all[far] = gram_pair[0] + gram_pair[1]
    to_gram = Exchange(FAR, lambda p: gram_all.at[far], lambda p: gram_all.at[p], gram_send, gram_recv).start()

    fetch.wait()
    segments = length // SEG_LEN

    def taps_of(segment):
        taps = []
        for half in range(2):
            at = pl.ds(pl.multiple_of(segment * SEG_LEN + 256 - 128 * half, 128), SEG_LEN)
            taps.append([[table[part, piece, :, at] for piece in range(2)] for part in range(2)])
        return taps

    def signal_of(segment):
        at = pl.ds(pl.multiple_of(segment * SEG_LEN, 128), SEG_LEN)
        return surveillance[0, :, at], surveillance[1, :, at]

    def cross_terms(segment, total):
        s_re, s_im = signal_of(segment)
        zero = jnp.zeros((128 - 2 * width, SEG_LEN), jnp.float32)
        with_re = halves(jnp.concatenate([s_re, s_im, zero], axis=0))
        with_im = halves(jnp.concatenate([s_im, -s_re, zero], axis=0))
        return tuple(
            x + (dot_beside(taps[0], with_re) + dot_beside(taps[1], with_im))
            for x, taps in zip(total, taps_of(segment))
        )

    product = lax.fori_loop(0, segments, cross_terms, blank, unroll=UNROLL)
    for half in range(2):
        mine[half] = product[half].T[: 2 * width]
    to_pair = Exchange(PAIR, lambda p: mine.at[p], lambda p: pair, pair_sem.at[0:1], pair_sem.at[1:2]).start()

    @pl.when(here == count - 1)
    def _():
        each(count, lambda d: tail_copy(d).wait_send())

    @pl.when(here != count - 1)
    def _():
        tail_copy(1).wait_recv()

    edge_r, edge_i = edge_matrix(tail[...])
    real[...] = edge_r
    imag[...] = edge_i
    along_y = Exchange(ALONG_Y, lambda p: ring_y.at[y], lambda p: ring_y.at[p], y_send, y_recv)
    to_pair.wait()
    ring_y[y] = mine[core] + pair[...]
    along_y.start()
    to_gram.wait()
    gram = jnp.sum(gram_all[...], axis=0)
    column = jnp.concatenate([gram[0:1], gram[1:2]], axis=1)
    column = jnp.concatenate([column, jnp.concatenate([gram[2:3], gram[3:4]], axis=1)], axis=0)
    column = jnp.concatenate([column, jnp.zeros((6, LAGS), jnp.float32)], axis=0)
    start_r, start_i = normal_matrix(column, real[...], imag[...], loading[0])
    real[...] = start_r
    imag[...] = start_i

    along_z = Exchange(ALONG_Z, lambda p: ring_z.at[z], lambda p: ring_z.at[p], z_send, z_recv)
    out = Exchange(PAIR, lambda p: cross.at[core], lambda p: cross.at[p], out_sem.at[0:1], out_sem.at[1:2])

    def between(index):
        @pl.when(index == 2)
        def _():
            along_y.wait()
            ring_z[z] = (ring_y[0] + ring_y[1]) + (ring_y[2] + ring_y[3])
            along_z.start()

        @pl.when(index == 6)
        def _():
            along_z.wait()
            cross[core] = ((ring_z[0] + ring_z[1]) + (ring_z[2] + ring_z[3])) + (
                (ring_z[4] + ring_z[5]) + (ring_z[6] + ring_z[7])
            )
            out.start()

    invert(real, imag, top, done, between)
    out.wait()
    right = jnp.concatenate([cross[0], cross[1]], axis=1)
    spun = jnp.concatenate([-right[width:], right[:width]], axis=0)
    w = dot(right, real[...], NT) + dot(spun, imag[...], NT)
    weights[...] = w

    w_re, w_im = w[:width], w[width:]
    on_re = halves(w)
    on_im = halves(jnp.concatenate([-w_im, w_re], axis=0))
    own_row = lax.broadcasted_iota(jnp.int32, (128, SEG_LEN), 0) // (2 * width)

    def cancelled(segment, energy):
        taps = taps_of(segment)
        joined = [
            [jnp.concatenate([taps[0][part][piece], taps[1][part][piece]], axis=0) for piece in range(2)]
            for part in range(2)
        ]
        clutter = dot_stacked(on_re, joined[0]) + dot_stacked(on_im, joined[1])
        rest = jnp.concatenate(signal_of(segment), axis=0) - clutter
        residual[segment] = rest
        square = rest * rest
        for tile in range(SEG_LEN // 128):
            energy = energy + square[:, 128 * tile : 128 * tile + 128]
        return energy

    energy = lax.fori_loop(0, segments, cancelled, jnp.zeros((2 * width, 128), jnp.float32), unroll=UNROLL)
    energy = jnp.sum(energy, axis=1, keepdims=True)
    energy = jnp.broadcast_to(energy[:width] + energy[width:], (width, 128))
    energy = jnp.concatenate([energy, jnp.zeros((128 - width, 128), jnp.float32)], axis=0)
    power_z[z] = energy.T[:8]
    to_z = Exchange(ALONG_Z, lambda p: power_z.at[z], lambda p: power_z.at[p], pz_send, pz_recv).start()

    to_far = Exchange(FAR, lambda p: corr.at[p], lambda p: landed.at[p], far_send, far_recv)
    for half in range(2):

        def correlate(segment, total):
            at = pl.ds(pl.multiple_of(segment * SEG_LEN + 256 - 128 * half, 128), SEG_LEN)
            rest = residual[segment]
            swapped = jnp.concatenate([rest[width:], -rest[:width]], axis=0)
            own = own_row == segment
            with_re = halves(jnp.where(own, jnp.concatenate([rest] * segments, axis=0), 0.0))
            with_im = halves(jnp.where(own, jnp.concatenate([swapped] * segments, axis=0), 0.0))
            real_taps = [table[0, piece, :, at] for piece in range(2)]
            imag_taps = [table[1, piece, :, at] for piece in range(2)]
            return total + (dot_beside(real_taps, with_re) + dot_beside(imag_taps, with_im))

        total = lax.fori_loop(0, segments, correlate, blank[0], unroll=UNROLL)
        corr[16 * half : 16 * half + 16] = total.reshape(16, 8, 128)

        def send(p, carry):
            @pl.when(p != far)
            def _():
                to_far.copy(lax.rem(p - far + 32, 32)).start()

            return carry

        lax.fori_loop(16 * half, 16 * half + 16, send, 0)
    landed[far] = corr[far]
    to_z.wait()
    parts = [power_z[i] for i in range(8)]
    power_y[y] = ((parts[0] + parts[1]) + (parts[2] + parts[3])) + ((parts[4] + parts[5]) + (parts[6] + parts[7]))
    to_y = Exchange(ALONG_Y, lambda p: power_y.at[y], lambda p: power_y.at[p], py_send, py_recv).start()
    to_far.wait()
    everything = landed[...]
    for lag in range(8):
        turned[lag] = everything[:, lag, :]
    to_near = Exchange(NEAR, lambda p: turned.at[p], lambda p: cells.at[p], near_send, near_recv).start()
    cells[near] = turned[near]
    to_y.wait()
    power[...] = (power_y[0] + power_y[1]) + (power_y[2] + power_y[3])
    energies[near] = power[...]
    Exchange(NEAR, lambda p: power, lambda p: energies.at[p], pa_send, pa_recv).start().wait()
    to_near.wait()


def cancel(loading, reference, surveillance):
    vmem = pl.BlockSpec(memory_space=pltpu.VMEM)
    length = reference.shape[1]
    width = surveillance.shape[1]
    dma = pltpu.SemaphoreType.DMA

    def block(*shape):
        return pltpu.VMEM(shape, jnp.float32)

    half = (2 * width, 128)
    return pl.pallas_call(
        cancel_kernel,
        out_shape=[
            jax.ShapeDtypeStruct((2 * width, LAGS), jnp.float32),
            jax.ShapeDtypeStruct((8, 32, 128), jnp.float32),
            jax.ShapeDtypeStruct((8, 8, 128), jnp.float32),
        ],
        in_specs=[pl.BlockSpec(memory_space=pltpu.SMEM), vmem, pl.BlockSpec(memory_space=pltpu.HBM)],
        out_specs=[vmem] * 3,
        scratch_shapes=[
            block(*surveillance.shape), dma((1,)),
            pltpu.VMEM((2, 2, 128, LAGS + length), jnp.bfloat16),
            block(2, LAGS), block(2, LAGS), block(2, *half), block(2, 4, 128), block(32, 4, 128),
            block(LAGS, LAGS), block(LAGS, LAGS), block(2, PANEL, LAGS), block(2, PANEL, LAGS),
            block(*half), block(4, *half), block(8, *half), block(2, *half), block(4, 2 * width, SEG_LEN),
            block(32, 8, 128), block(32, 8, 128), block(8, 32, 128), block(8, 128), block(8, 8, 128), block(4, 8, 128),
            dma((2,)), dma((63,)), dma((1,)), dma((2,)), dma((31,)), dma((31,)),
            dma((2,)), dma((3,)), dma((3,)), dma((7,)), dma((7,)), dma((2,)),
            dma((31,)), dma((31,)), dma((7,)), dma((7,)), dma((7,)), dma((7,)), dma((3,)), dma((3,)), dma((7,)), dma((7,)),
        ],
        compiler_params=pltpu.CompilerParams(collective_id=0, has_side_effects=True, vmem_limit_bytes=56200000),
        name="cancel",
    )(loading, reference, surveillance)


def doppler_tables(shards, segments):
    short = DOPP // segments
    order = np.arange(shards).reshape(-1, 2).T.reshape(-1)
    angle = 2.0 * np.pi / short * (np.outer(order, np.arange(short)) % short)
    table = np.concatenate([np.cos(angle), np.sin(angle)], axis=1)
    turn = 2.0 * np.pi / DOPP * np.outer(np.arange(segments), np.arange(DOPP))
    turns = np.stack([np.cos(turn), np.sin(turn)])
    return table.astype(np.float32), turns.astype(np.float32)


def doppler_kernel(samples, weights, cells, energies, table, turns, out, kept):
    near, _, lanes = cells.shape
    groups = near // 2
    segments = turns.shape[1]
    width = lanes // segments // 2
    basis = halves(table[...])
    short = DOPP // segments
    def group(g, carry):
        power = (energies[g] + energies[groups + g]) / samples
        scale = lax.rsqrt(samples * (power + EPSILON))
        by = jnp.broadcast_to(scale[0:1], (128, 128)).T[:width, 0:1]
        rows = jnp.concatenate([cells[g], cells[groups + g]], axis=0)
        wave = dot3(halves(rows.T), basis)
        total_r = total_i = None
        for s in range(segments):
            base = 2 * width * s
            a_r, a_i = wave[base : base + width, :short], wave[base : base + width, short:]
            b_r, b_i = (
                wave[base + width : base + 2 * width, :short],
                wave[base + width : base + 2 * width, short:],
            )
            y_r = (a_r + b_i) * by
            y_i = (b_r - a_i) * by
            y_r = jnp.concatenate([y_r] * segments, axis=1)
            y_i = jnp.concatenate([y_i] * segments, axis=1)
            if s == 0:
                total_r, total_i = y_r, y_i
                continue
            c, d = turns[0, s : s + 1, :], turns[1, s : s + 1, :]
            total_r = total_r + (y_r * c + y_i * d)
            total_i = total_i + (y_i * c - y_r * d)
        at = pl.ds(width * g, width)
        out[0, 0, at, :] = total_r
        out[0, 1, at, :] = total_i
        return carry

    for g in range(groups):
        group(g, 0)
    kept[...] = weights[...]


def doppler(weights, cells, energies, segments, samples):
    vmem = pl.BlockSpec(memory_space=pltpu.VMEM)
    shards = 2 * cells.shape[1]
    table, turns = doppler_tables(shards, segments)
    width = cells.shape[2] // segments // 2
    groups = cells.shape[0] // 2
    return pl.pallas_call(
        functools.partial(doppler_kernel, samples),
        out_shape=[
            jax.ShapeDtypeStruct((1, 2, width * groups, DOPP), jnp.float32),
            jax.ShapeDtypeStruct(weights.shape, jnp.float32),
        ],
        in_specs=[vmem] * 5,
        out_specs=[vmem, vmem],
        compiler_params=pltpu.CompilerParams(vmem_limit_bytes=24 * 2**20),
        name="doppler",
    )(weights, cells, energies, jnp.asarray(table), jnp.asarray(turns))


def per_device(reference_signal, surveillance, loading):
    length = reference_signal.shape[1]
    samples = float(length * lax.axis_size(TM))
    weights, cells, energies = cancel(loading, reference_signal, surveillance)
    full, weights = doppler(weights, cells, energies, length // SEG_LEN, samples)
    return full, jnp.swapaxes(weights.reshape(2, -1, LAGS), 1, 2)


def solution(mesh):
    split = Mesh(
        mesh.devices.reshape(4, 8, 2, mesh.shape["chan"]), ("tm_0", "tm_1", "tm_2", "chan")
    )
    in_specs = (P(None, TM), P(None, "chan", TM), P())
    out_specs = (P(TM_CHAN, None, None, None), P(None, None, "chan"))
    return jax.shard_map(
        per_device, mesh=split, in_specs=in_specs, out_specs=out_specs, check_vma=False
    )
```
